32 devices in a mesh: frames: 8 (over z, y), chan: 4 (over x, core).
Axes of the slice: x: 2, y: 2, z: 4, core: 2. Of those that a mesh axis runs over, the one named last changes fastest.
Arguments:
- signal: float32 [512, 32768], P('chan', 'frames'), may hold values from -6 to 6
- dilated_dirs: bfloat16 [3, 7, 512, 512], P(None, None, 'chan'), may hold values from -0.09375 to 0.09375
- dilated_gains: float32 [3, 512], P(None, 'chan'), may hold values from 0.3 to 0.9
- dilated_bias: float32 [3, 512], P(None, 'chan'), may hold values from -1 to 1
- snake_first: float32 [3, 512], P(None, 'chan'), may hold values from 0.3 to 1.2
- snake_second: float32 [3, 512], P(None, 'chan'), may hold values from 0.3 to 1.2
- pointwise_dirs: bfloat16 [3, 512, 512], P(None, 'chan'), may hold values from -0.25 to 0.25
- pointwise_gains: float32 [3, 512], P(None, 'chan'), may hold values from 0.3 to 0.9
- pointwise_bias: float32 [3, 512], P(None, 'chan'), may hold values from -1 to 1
- snake_last: float32 [512], P('chan'), may hold values from 0.3 to 1.2
- strided_dirs: bfloat16 [16, 1024, 512], P(None, 'chan'), may hold values from -0.0625 to 0.0625
- strided_gains: float32 [1024], P('chan'), may hold values from 0.3 to 0.9
- strided_bias: float32 [1024], P('chan'), may hold values from -1 to 1
- latent_proj: bfloat16 [8, 1024], P(None, 'chan'), may hold values from -0.1875 to 0.1875
- latent_bias: float32 [8], replicated, may hold values from -3 to 3
- codebook: float32 [8, 8192], replicated, may hold values from -6 to 6
- output_proj: bfloat16 [1024, 8], P('chan'), may hold values from -2 to 2
- output_bias: float32 [1024], P('chan'), may hold values from -3 to 3
- utterances: int32 [10], replicated, may hold values from 1 to 800, 4096 in all
- code_index: int32 [4096], P('frames'), may hold values from 0 to 8191
- refill_index: int32 [8192], replicated, may hold values from 0 to 4095
- cotangent: bfloat16 [1024, 4096], P('chan', 'frames'), may hold values from -6 to 6
Outputs:
- output: float32 [1024, 4096], P('chan', 'frames')
- grad_signal: float32 [512, 32768], P('chan', 'frames')
- grad_dilated_dirs: float32 [3, 7, 512, 512], P(None, None, 'chan')
- grad_dilated_gains: float32 [3, 512], P(None, 'chan')
- grad_dilated_bias: float32 [3, 512], P(None, 'chan')
- grad_snake_first: float32 [3, 512], P(None, 'chan')
- grad_snake_second: float32 [3, 512], P(None, 'chan')
- grad_pointwise_dirs: float32 [3, 512, 512], P(None, 'chan')
- grad_pointwise_gains: float32 [3, 512], P(None, 'chan')
- grad_pointwise_bias: float32 [3, 512], P(None, 'chan')
- grad_snake_last: float32 [512], P('chan')
- grad_strided_dirs: float32 [16, 1024, 512], P(None, 'chan')
- grad_strided_gains: float32 [1024], P('chan')
- grad_strided_bias: float32 [1024], P('chan')
- grad_latent_proj: float32 [8, 1024], P(None, 'chan')
- grad_latent_bias: float32 [8], replicated
- grad_codebook: float32 [8, 8192], replicated
- grad_output_proj: float32 [1024, 8], P('chan')
- grad_output_bias: float32 [1024], P('chan')
- refreshed: float32 [8, 8192], replicated
The draws below stay inside these ranges and needn't reach their ends.
All inputs are finite; a program needn't handle non-finite values.
Results may differ from the reference program's by a relative error of at most 0.019.
Values may be sent and summed in bfloat16 or wider, within the bound.
No kernel may reach another device: no remote copies, remote signals or barrier semaphores. Data moves between devices by JAX's collectives and lax.ppermute only.
A program may use at most 256 MiB of HBM per device.

```python
import math
import jax
import jax.numpy as jnp
import numpy as np
from jax import lax

C = 512
C2 = 1024
LATENT = 8
CODES = 8192
UNITS = 3
KERNEL = 7
STRIDE = 8
LEN_MOST = 800
FRAMES = 4096
SAMPLES = 32768
UTTS = 10


def plant(values, stream_key, low, top_value):
    longest = values.shape.index(max(values.shape))
    spots = []
    for shift in (0, 1):
        where = [jax.random.randint(jax.random.fold_in(stream_key, axis), (), 0, length) for axis, length in enumerate(values.shape)]
        where[longest] = (where[longest] + shift) % values.shape[longest]
        spots.append(tuple(where))
    return values.at[spots[0]].set(low).at[spots[1]].set(top_value)


def block_levels(rng, dims, split, low, top_value):
    loudness = 1.0
    for position, blocks in split:
        draws = jax.random.uniform(jax.random.fold_in(jax.random.fold_in(rng, 6), position), (blocks,), jnp.float32, low / len(split), top_value / len(split))
        loudness = loudness * jnp.repeat(jnp.exp(draws), dims[position] // blocks).reshape((-1,) + (1,) * (len(dims) - 1 - position))
    return loudness


def rank_bounds(amount, slope):
    portions = [(1 << 20) // math.isqrt(standing ** slope) + 1 for standing in range(1, amount + 1)]
    spread = 1 + sum(portions) // (1 << 30)
    return np.cumsum(np.array([max(1, weight // spread) for weight in portions]))


def ranked(rng, shape, count, lean):
    grid = rank_bounds(count, lean)
    lot = jax.random.randint(jax.random.fold_in(rng, 1), shape, 0, int(grid[count - 1]))
    rank = jnp.searchsorted(jnp.asarray(grid, jnp.int32), lot, side="right")
    return jax.random.permutation(jax.random.fold_in(rng, 2), count)[rank].astype(jnp.int32)


def split_up(amount, total, limit, skew):
    weights = [(1 << 20) // math.isqrt(grade ** skew) + 1 for grade in range(2, amount + 1)]
    spare, given = total - limit - (amount - 1), [1] * (amount - 1)
    while spare > 0:
        movable = [i for i in range(amount - 1) if given[i] < limit]
        pool, remaining = sum([weights[i] for i in movable]), spare
        for i in movable:
            extra = min(limit - given[i], max(1, remaining * weights[i] // pool), spare)
            given[i] = given[i] + extra
            spare = spare - extra
    return np.array([limit] + given)


def ragged_sizes(stream_key, amount, total, bound, lean):
    if amount == 2:
        one = jax.random.randint(stream_key, (), max(1, total - bound), min(bound, total - 1) + 1)
        return jnp.stack([one, total - one])
    lengths = jnp.asarray(split_up(amount, total, bound, lean), jnp.int32)
    pairs = (amount - 1) // 2
    donor, taker = lengths[1:1 + 2 * pairs:2], lengths[2:2 + 2 * pairs:2]
    room = jnp.minimum(donor - 1, bound - taker)
    shifted = jax.random.randint(jax.random.fold_in(stream_key, 1), (pairs,), 0, 1 << 20) % (room + 1)
    lengths = lengths.at[1:1 + 2 * pairs:2].set(donor - shifted).at[2:2 + 2 * pairs:2].set(taker + shifted)
    return lengths[jax.random.permutation(jax.random.fold_in(stream_key, 2), amount)]


def noise(key, shape, deviation, most, cuts=(), held_as=jnp.bfloat16):
    factor_of = block_levels(key, shape, cuts, -0.22, 0.18) if cuts else 1.0
    entries = jax.random.normal(key, shape, jnp.float32) * deviation * factor_of
    return jnp.minimum(jnp.maximum(entries, -most), most).astype(held_as)


def setup_inputs(seed: int = 0) -> dict:
    key_list = jax.random.split(jax.random.key(seed), 23)
    signal = noise(key_list[0], (C, SAMPLES), 1.0, 6.0, ((0, 4), (1, 8)), jnp.float32)
    dilated_dirs = noise(key_list[1], (UNITS, KERNEL, C, C), (KERNEL * C) ** -0.5, 0.09375, ((2, 4),))
    dilated_gains = jnp.clip(jnp.exp(math.log(0.9) - 1.0986122 * jax.random.uniform(key_list[2], (UNITS, C), jnp.float32) ** block_levels(key_list[2], (UNITS, C), ((1, 4),), -0.2, 0.2)), 0.3, 0.9)
    dilated_bias = noise(key_list[3], (UNITS, C), 0.2, 1.0, ((1, 4),), jnp.float32)
    snake_first = jnp.clip(jnp.exp(math.log(1.2) - 1.3862944 * jax.random.uniform(key_list[4], (UNITS, C), jnp.float32) ** block_levels(key_list[4], (UNITS, C), ((1, 4),), -0.2, 0.2)), 0.3, 1.2)
    snake_second = jnp.clip(jnp.exp(math.log(1.2) - 1.3862944 * jax.random.uniform(key_list[5], (UNITS, C), jnp.float32) ** block_levels(key_list[5], (UNITS, C), ((1, 4),), -0.2, 0.2)), 0.3, 1.2)
    pointwise_dirs = noise(key_list[6], (UNITS, C, C), C ** -0.5, 0.25, ((1, 4),))
    pointwise_gains = jnp.clip(jnp.exp(math.log(0.9) - 1.0986122 * jax.random.uniform(key_list[7], (UNITS, C), jnp.float32) ** block_levels(key_list[7], (UNITS, C), ((1, 4),), -0.2, 0.2)), 0.3, 0.9)
    pointwise_bias = noise(key_list[8], (UNITS, C), 0.2, 1.0, ((1, 4),), jnp.float32)
    snake_last = jnp.clip(jnp.exp(math.log(1.2) - 1.3862944 * jax.random.uniform(key_list[9], (C,), jnp.float32) ** block_levels(key_list[9], (C,), ((0, 4),), -0.2, 0.2)), 0.3, 1.2)
    strided_dirs = noise(key_list[10], (2 * STRIDE, C2, C), (2 * STRIDE * C) ** -0.5, 0.0625, ((1, 4),))
    strided_gains = jnp.clip(jnp.exp(math.log(0.9) - 1.0986122 * jax.random.uniform(key_list[11], (C2,), jnp.float32) ** block_levels(key_list[11], (C2,), ((0, 4),), -0.2, 0.2)), 0.3, 0.9)
    strided_bias = noise(key_list[12], (C2,), 0.2, 1.0, ((0, 4),), jnp.float32)
    latent_proj = noise(key_list[13], (LATENT, C2), C2 ** -0.5, 0.1875, ((1, 4),))
    latent_bias = noise(key_list[14], (LATENT,), 0.5, 3.0, (), jnp.float32)
    codebook = noise(key_list[15], (LATENT, CODES), 1.0, 6.0, (), jnp.float32)
    output_proj = noise(key_list[16], (C2, LATENT), LATENT ** -0.5, 2.0, ((0, 4),))
    output_bias = noise(key_list[17], (C2,), 0.5, 3.0, ((0, 4),), jnp.float32)
    utterances = ragged_sizes(key_list[18], UTTS, FRAMES, LEN_MOST, 1).astype(jnp.int32)
    code_index = plant(ranked(key_list[19], (FRAMES,), CODES, 1), jax.random.fold_in(key_list[19], 3), 0, CODES - 1).astype(jnp.int32)
    refill_index = plant(jax.random.randint(key_list[20], (CODES,), 0, FRAMES), jax.random.fold_in(key_list[20], 1), 0, FRAMES - 1).astype(jnp.int32)
    cotangent = noise(key_list[21], (C2, FRAMES), 1.0, 6.0, ((0, 4), (1, 8)))
    return {"signal": signal, "dilated_dirs": dilated_dirs, "dilated_gains": dilated_gains, "dilated_bias": dilated_bias, "snake_first": snake_first, "snake_second": snake_second, "pointwise_dirs": pointwise_dirs, "pointwise_gains": pointwise_gains, "pointwise_bias": pointwise_bias, "snake_last": snake_last, "strided_dirs": strided_dirs, "strided_gains": strided_gains, "strided_bias": strided_bias, "latent_proj": latent_proj, "latent_bias": latent_bias, "codebook": codebook, "output_proj": output_proj, "output_bias": output_bias, "utterances": utterances, "code_index": code_index, "refill_index": refill_index, "cotangent": cotangent}


norm_eps = 1e-06
commit_weight = 4.0

@jax.custom_vjp
def low(v):
    return lax.optimization_barrier(v.astype(jnp.bfloat16)).astype(jnp.float32)

@jax.custom_vjp
def low_back(v):
    return v

def low_keep(v):
    return (low(v), None)

def low_pass(kept, grad):
    return (grad,)

def back_keep(v):
    return (v, None)

def back_low(kept, grad):
    return (low(grad),)
low.defvjp(low_keep, low_pass)
low_back.defvjp(back_keep, back_low)

def snake_act(value, alpha):
    return value + jnp.sin(alpha[:, None] * value) ** 2 / alpha[:, None]

def taps_norm(direction, gain):
    return direction * (gain * lax.rsqrt(lax.optimization_barrier(jnp.sum(direction * direction, axis=(0, 2))) + norm_eps))[None, :, None]

def rows_norm(direction, gain):
    return direction * (gain * lax.rsqrt(lax.optimization_barrier(jnp.sum(direction * direction, axis=1)) + norm_eps))[:, None]

def unit_scale(value):
    return value * lax.rsqrt(lax.optimization_barrier(jnp.sum(value * value, axis=0)) + 1.0)[None, :]

def make_dilated(labels, spacing, taps):
    margin = taps // 2 * spacing
    extent = labels.shape[0]
    tags = jnp.pad(labels, (margin, margin), constant_values=-1)
    masks = [tags[k * spacing:k * spacing + extent] == labels for k in range(taps)]

    @jax.checkpoint
    def dilated_conv(active, weight):
        padded = jnp.pad(active, ((0, 0), (margin, margin)))
        result = jnp.zeros((weight.shape[1], extent), active.dtype)
        for kernel_tap in range(taps):
            start = kernel_tap * spacing
            same = masks[kernel_tap].astype(active.dtype)
            result = result + jnp.dot(weight[kernel_tap], padded[:, start:start + extent] * same[None, :], precision=lax.Precision.HIGHEST)
        return result
    return dilated_conv

def make_strided(labels, stride):
    half = stride // 2
    frames = labels.shape[0] // stride
    tags = jnp.pad(labels, (half, half), constant_values=-1)
    centre = labels[::stride]
    masks = [tags[k:k + stride * frames:stride] == centre for k in range(2 * stride)]

    @jax.checkpoint
    def strided_conv(active, weight):
        padded = jnp.pad(active, ((0, 0), (half, half)))
        result = jnp.zeros((weight.shape[1], frames), active.dtype)
        for kernel_tap in range(2 * stride):
            columns = padded[:, kernel_tap:kernel_tap + stride * frames:stride]
            same = masks[kernel_tap].astype(active.dtype)
            result = result + jnp.dot(weight[kernel_tap], columns * same[None, :], precision=lax.Precision.HIGHEST)
        return result
    return strided_conv

def reference(signal, dilated_dirs, dilated_gains, dilated_bias, snake_first, snake_second, pointwise_dirs, pointwise_gains, pointwise_bias, snake_last, strided_dirs, strided_gains, strided_bias, latent_proj, latent_bias, codebook, output_proj, output_bias, utterances, code_index, refill_index, cotangent):
    bounds = jnp.cumsum(utterances).astype(jnp.int32) * STRIDE
    spots = jnp.arange(SAMPLES, dtype=jnp.int32)
    labels = lax.optimization_barrier(jnp.sum((spots[:, None] >= bounds[None, :]).astype(jnp.int32), axis=1)).astype(jnp.int32)
    convs = [make_dilated(labels, 3 ** member, KERNEL) for member in range(UNITS)]
    strided_conv = make_strided(labels, STRIDE)

    def forward(signal, dilated_dirs, dilated_gains, dilated_bias, snake_first, snake_second, pointwise_dirs, pointwise_gains, pointwise_bias, snake_last, strided_dirs, strided_gains, strided_bias, latent_proj, latent_bias, codebook, output_proj, output_bias):
        stream = signal
        for member in range(UNITS):
            active = low(snake_act(stream, snake_first[member]))
            weight7 = low(taps_norm(dilated_dirs[member], dilated_gains[member]))
            middle = low_back(convs[member](active, weight7)) + dilated_bias[member][:, None]
            second = low(snake_act(middle, snake_second[member]))
            weight1 = low(rows_norm(pointwise_dirs[member], pointwise_gains[member]))
            stream = stream + low_back(jnp.dot(weight1, second, precision=lax.Precision.HIGHEST)) + pointwise_bias[member][:, None]
        active3 = low(snake_act(stream, snake_last))
        weights = low(taps_norm(strided_dirs, strided_gains))
        hidden = low_back(strided_conv(active3, weights)) + strided_bias[:, None]
        latent = jnp.dot(latent_proj, hidden, precision=lax.Precision.HIGHEST) + latent_bias[:, None]
        normed = unit_scale(latent)
        coded = unit_scale(codebook)
        chosen = jnp.take(coded, code_index, axis=1)
        output = jnp.dot(output_proj, low(chosen), precision=lax.Precision.HIGHEST) + output_bias[:, None]
        commit = commit_weight * jnp.sum((normed - chosen) ** 2)
        return ((output, commit), latent)
    floats = (signal, dilated_dirs, dilated_gains, dilated_bias, snake_first, snake_second, pointwise_dirs, pointwise_gains, pointwise_bias, snake_last, strided_dirs, strided_gains, strided_bias, latent_proj, latent_bias, codebook, output_proj, output_bias)
    floats = tuple((value.astype(jnp.float32) for value in floats))
    results, pull, latent = jax.vjp(forward, *floats, has_aux=True)
    grads = pull((cotangent.astype(jnp.float32), jnp.ones((), jnp.float32)))
    usage = jnp.zeros((CODES,), jnp.float32).at[code_index].add(1.0)
    picked = jnp.take(latent, refill_index, axis=1)
    refreshed = jnp.where(usage[None, :] > 0, floats[15], picked)
    return (results[0], grads[0], grads[1], grads[2], grads[3], grads[4], grads[5], grads[6], grads[7], grads[8], grads[9], grads[10], grads[11], grads[12], grads[13], grads[14], grads[15], grads[16], grads[17], refreshed)
```

```python
import jax
import jax.numpy as jnp
from jax import lax
from jax.experimental import pallas as pl
from jax.experimental.pallas import tpu as pltpu
from jax.sharding import PartitionSpec as P

CODES = 8192
STRIDE = 8
NORM_EPS = 1e-06
COMMIT = 4.0

BF = jnp.bfloat16
F32 = jnp.float32

SEG = 16
HALO = 128
LEAD = 28
CHUNK = 256
VMEM = 60 * 2**20

INV_PI = 0.3183098861837907
PI_HIGH = 3.140625
PI_LOW = 0.000967653589793116


def reduced(angle):
    turns = jnp.round(angle * INV_PI)
    return (angle - turns * PI_HIGH) - turns * PI_LOW


def sin_over(square):
    return 0.999999995 + square * (
        -0.166666573 + square * (8.33303355e-03 + square * (-1.98077678e-04 + square * 2.60223459e-06))
    )


def cos_of(square):
    return 0.999999948 + square * (
        -4.99998973e-01
        + square * (4.16633930e-02 + square * (-1.38522741e-03 + square * 2.31212358e-05))
    )


def snake(value, alpha, inverse):
    angle = reduced(alpha * value)
    square = angle * angle
    part = sin_over(square)
    return value + (square * part * part) * inverse


def snake_parts(value, alpha, inverse):
    angle = reduced(alpha * value)
    square = angle * angle
    part = sin_over(square)
    sine2 = (square * part * part) * inverse
    double = 2.0 * angle * part * cos_of(square)
    return value + sine2, 1.0 + double, (value * double - sine2) * inverse


def lanes4(mask):
    return jnp.concatenate([mask] * 4, axis=1)


def own_mask(start, count, span, own):
    row = lax.broadcasted_iota(jnp.int32, (count, 128), 0) + start
    place = (row & (SEG - 1)) * span + (row >> 4)
    return jnp.where((place >= HALO) & (place < HALO + own), 1.0, 0.0).astype(F32)


def fold(values):
    rows, cols = values.shape
    return values.reshape(rows // 8, 8, cols).sum(axis=0)


def load_weights(pieces, weights, sems):
    me = lax.axis_index("chan")
    copies = []
    for p, piece in enumerate(pieces):
        rows = piece.shape[1]
        slot = pl.multiple_of((me ^ p) * rows, rows)
        copy = pltpu.make_async_copy(piece, weights.at[:, pl.ds(slot, rows), :], sems.at[p])
        copy.start()
        copies.append(copy)
    return copies


def fill_masks(mask, labels, spacing, rows):
    base = LEAD * SEG
    here = labels[pl.ds(base, rows), :]
    for tap in range(7):
        there = labels[pl.ds(base + (tap - 3) * spacing * SEG, rows), :]
        mask[tap] = jnp.where(there == here, 1.0, 0.0).astype(BF)


def fill_ends(wide, full, margin, rows):
    edge = margin * SEG
    wide[pl.ds(0, edge), :] = full[pl.ds(8 + rows - edge - 1, edge), :].astype(BF)
    wide[pl.ds(edge + rows, edge), :] = full[pl.ds(8 + 1, edge), :].astype(BF)


def dot_nt(left, right):
    return lax.dot_general(left, right, (((1,), (1,)), ((), ())), preferred_element_type=F32)


def dot_nn(left, right):
    return lax.dot_general(left, right, (((1,), (0,)), ((), ())), preferred_element_type=F32)


def dot_tn(left, right):
    return lax.dot_general(left, right, (((0,), (0,)), ((), ())), preferred_element_type=F32)


A1, I1, A2, I2, S7, B7, S1, B1 = range(8)


def unit_forward(stream, pieces, vecs, labels, spacing):
    rows, chans = stream.shape
    margin = 3 * spacing

    def kernel(s_ref, p0, p1, p2, p3, v_ref, l_ref, out_ref, mid_ref, weights, wide, full, mask, sems):
        copies = load_weights((p0, p1, p2, p3), weights, sems)
        fill_masks(mask, l_ref, spacing, rows)

        @pl.loop(0, rows, step=CHUNK)
        def _(start):
            start = pl.multiple_of(start, CHUNK)
            act = snake(s_ref[pl.ds(start, CHUNK), :], v_ref[A1 : A1 + 1, :], v_ref[I1 : I1 + 1, :])
            full[pl.ds(8 + start, CHUNK), :] = act
            wide[pl.ds(margin * SEG + start, CHUNK), :] = act.astype(BF)

        fill_ends(wide, full, margin, rows)
        for copy in copies:
            copy.wait()

        @pl.loop(0, rows, step=CHUNK)
        def _(start):
            start = pl.multiple_of(start, CHUNK)
            total = None
            for tap in range(7):
                columns = wide[pl.ds(start + tap * spacing * SEG, CHUNK), :]
                if tap != 3:
                    columns = columns * lanes4(mask[tap, pl.ds(start, CHUNK), :])
                term = dot_nt(columns, weights[tap])
                total = term if total is None else total + term
            middle = total * v_ref[S7 : S7 + 1, :] + v_ref[B7 : B7 + 1, :]
            mid_ref[pl.ds(start, CHUNK), :] = middle
            second = snake(middle, v_ref[A2 : A2 + 1, :], v_ref[I2 : I2 + 1, :]).astype(BF)
            term = dot_nt(second, weights[7])
            out_ref[pl.ds(start, CHUNK), :] = (
                s_ref[pl.ds(start, CHUNK), :] + term * v_ref[S1 : S1 + 1, :] + v_ref[B1 : B1 + 1, :]
            )

    whole = pl.BlockSpec(memory_space=pltpu.VMEM)
    held = pl.BlockSpec(memory_space=pl.ANY)
    return pl.pallas_call(
        kernel,
        out_shape=[jax.ShapeDtypeStruct((rows, chans), F32)] * 2,
        in_specs=[whole] + [held] * 4 + [whole] * 2,
        out_specs=[whole] * 2,
        scratch_shapes=[
            pltpu.VMEM((8, chans, chans), BF),
            pltpu.VMEM((rows + 2 * margin * SEG, chans), BF),
            pltpu.VMEM((rows + 16, chans), F32),
            pltpu.VMEM((7, rows, 128), BF),
            pltpu.SemaphoreType.DMA((4,)),
        ],
        compiler_params=pltpu.CompilerParams(vmem_limit_bytes=VMEM),
        cost_estimate=pl.CostEstimate(
            flops=2 * rows * 8 * chans * chans, bytes_accessed=16 * 2**20, transcendentals=0
        ),
        name=f"unit_forward_{spacing}",
    )(stream, *pieces, vecs, labels)


def unit_weights_back(grad, stream, middle, piece1s, vecs, labels, spacing, own):
    rows, chans = stream.shape
    margin = 3 * spacing
    span = rows // SEG
    part = chans // 4

    def kernel(
        g_ref, s_ref, m_ref, p0, p1, p2, p3, v_ref, l_ref,
        d_ref, keep_ref, send_ref, sum_ref,
        w1, wide, full, mask, low_t, mid_t, second, results, sums, sems, out_sems,
    ):
        me = lax.axis_index("chan")
        copies = []
        for p, piece in enumerate((p0, p1, p2, p3)):
            slot = pl.multiple_of((me ^ p) * part, part)
            copy = pltpu.make_async_copy(piece.at[7], w1.at[pl.ds(slot, part), :], sems.at[p])
            copy.start()
            copies.append(copy)
        fill_masks(mask, l_ref, spacing, rows)
        sums[...] = jnp.zeros_like(sums)
        for copy in copies:
            copy.wait()

        @pl.loop(0, rows, step=CHUNK)
        def _(start):
            start = pl.multiple_of(start, CHUNK)
            here = pl.ds(start, CHUNK)
            mine = lanes4(own_mask(start, CHUNK, span, own))
            act = snake(s_ref[here, :], v_ref[A1 : A1 + 1, :], v_ref[I1 : I1 + 1, :])
            full[pl.ds(8 + start, CHUNK), :] = act
            wide[pl.ds(margin * SEG + start, CHUNK), :] = act.astype(BF)
            grad_here = g_ref[here, :]
            scaled = grad_here * v_ref[S1 : S1 + 1, :]
            low_t[:, here] = (scaled * mine).T.astype(BF)
            back = dot_nn(scaled.astype(BF), w1[...])
            value, slope, by_alpha = snake_parts(
                m_ref[here, :], v_ref[A2 : A2 + 1, :], v_ref[I2 : I2 + 1, :]
            )
            second[here, :] = value.astype(BF)
            dmiddle = back * slope
            mine_mid = dmiddle * mine
            sums[0] += fold(grad_here * mine)
            sums[1] += fold(mine_mid)
            sums[2] += fold(back * by_alpha * mine)
            d_ref[here, :] = (dmiddle * v_ref[S7 : S7 + 1, :]).astype(BF)
            mid_t[:, here] = (mine_mid * v_ref[S7 : S7 + 1, :]).T.astype(BF)

        fill_ends(wide, full, margin, rows)
        sum_ref[...] = jnp.concatenate(
            [sums[i].sum(axis=0, keepdims=True) for i in range(3)] + [jnp.zeros((5, chans), F32)], axis=0
        )
        results[7] = dot_nn(low_t[...], second[...]).astype(BF)

        @pl.loop(0, 7)
        def _(tap):
            columns = wide[pl.ds(pl.multiple_of(tap * (spacing * SEG), SEG), rows), :]
            columns = columns * lanes4(mask[tap])
            results[tap] = dot_nn(mid_t[...], columns).astype(BF)

        outs = []
        for p, target in enumerate((keep_ref.at[0], send_ref.at[0], keep_ref.at[1], send_ref.at[1])):
            slot = pl.multiple_of((me ^ p) * part, part)
            copy = pltpu.make_async_copy(results.at[:, pl.ds(slot, part), :], target, out_sems.at[p])
            copy.start()
            outs.append(copy)
        for copy in outs:
            copy.wait()

    whole = pl.BlockSpec(memory_space=pltpu.VMEM)
    held = pl.BlockSpec(memory_space=pl.ANY)
    return pl.pallas_call(
        kernel,
        out_shape=[
            jax.ShapeDtypeStruct((rows, chans), BF),
            jax.ShapeDtypeStruct((2, 8, part, chans), BF),
            jax.ShapeDtypeStruct((2, 8, part, chans), BF),
            jax.ShapeDtypeStruct((8, chans), F32),
        ],
        in_specs=[whole] * 3 + [held] * 4 + [whole] * 2,
        out_specs=[whole, held, held, whole],
        scratch_shapes=[
            pltpu.VMEM((chans, chans), BF),
            pltpu.VMEM((rows + 2 * margin * SEG, chans), BF),
            pltpu.VMEM((rows + 16, chans), F32),
            pltpu.VMEM((7, rows, 128), BF),
            pltpu.VMEM((chans, rows), BF),
            pltpu.VMEM((chans, rows), BF),
            pltpu.VMEM((rows, chans), BF),
            pltpu.VMEM((8, chans, chans), BF),
            pltpu.VMEM((3, 8, chans), F32),
            pltpu.SemaphoreType.DMA((4,)),
            pltpu.SemaphoreType.DMA((4,)),
        ],
        compiler_params=pltpu.CompilerParams(vmem_limit_bytes=VMEM),
        cost_estimate=pl.CostEstimate(
            flops=2 * rows * 9 * chans * chans, bytes_accessed=20 * 2**20, transcendentals=0
        ),
        name=f"unit_weights_back_{spacing}",
    )(grad, stream, middle, *piece1s, vecs, labels)


def unit_input_back(grad, stream, scaled, pieces, vecs, labels, spacing, own):
    rows, chans = stream.shape
    margin = 3 * spacing
    span = rows // SEG

    def kernel(g_ref, s_ref, d_ref, p0, p1, p2, p3, v_ref, l_ref, out_ref, sum_ref, weights, wide, full, mask, sums, sems):
        copies = load_weights((p0, p1, p2, p3), weights, sems)
        fill_masks(mask, l_ref, spacing, rows)
        sums[...] = jnp.zeros_like(sums)

        @pl.loop(0, rows, step=CHUNK)
        def _(start):
            start = pl.multiple_of(start, CHUNK)
            value = d_ref[pl.ds(start, CHUNK), :]
            full[pl.ds(8 + start, CHUNK), :] = value.astype(F32)
            wide[pl.ds(margin * SEG + start, CHUNK), :] = value

        fill_ends(wide, full, margin, rows)
        for copy in copies:
            copy.wait()

        @pl.loop(0, rows, step=CHUNK)
        def _(start):
            start = pl.multiple_of(start, CHUNK)
            here = pl.ds(start, CHUNK)
            total = None
            for tap in range(7):
                columns = wide[pl.ds(start + (6 - tap) * spacing * SEG, CHUNK), :]
                if tap != 3:
                    columns = columns * lanes4(mask[6 - tap, pl.ds(start, CHUNK), :])
                term = dot_nn(columns, weights[tap])
                total = term if total is None else total + term
            mine = lanes4(own_mask(start, CHUNK, span, own))
            value, slope, by_alpha = snake_parts(
                s_ref[here, :], v_ref[A1 : A1 + 1, :], v_ref[I1 : I1 + 1, :]
            )
            sums[...] += fold(total * by_alpha * mine)
            out_ref[here, :] = g_ref[here, :] + total * slope

        sum_ref[...] = jnp.concatenate(
            [sums[...].sum(axis=0, keepdims=True), jnp.zeros((7, chans), F32)], axis=0
        )

    whole = pl.BlockSpec(memory_space=pltpu.VMEM)
    held = pl.BlockSpec(memory_space=pl.ANY)
    return pl.pallas_call(
        kernel,
        out_shape=[jax.ShapeDtypeStruct((rows, chans), F32), jax.ShapeDtypeStruct((8, chans), F32)],
        in_specs=[whole] * 3 + [held] * 4 + [whole] * 2,
        out_specs=[whole] * 2,
        scratch_shapes=[
            pltpu.VMEM((8, chans, chans), BF),
            pltpu.VMEM((rows + 2 * margin * SEG, chans), BF),
            pltpu.VMEM((rows + 16, chans), F32),
            pltpu.VMEM((7, rows, 128), BF),
            pltpu.VMEM((8, chans), F32),
            pltpu.SemaphoreType.DMA((4,)),
        ],
        compiler_params=pltpu.CompilerParams(vmem_limit_bytes=VMEM),
        cost_estimate=pl.CostEstimate(
            flops=2 * rows * 7 * chans * chans, bytes_accessed=16 * 2**20, transcendentals=0
        ),
        name=f"unit_input_back_{spacing}",
    )(grad, stream, scaled, *pieces, vecs, labels)


def enter(pieces, own):
    part, count = pieces[0].shape
    span = count // SEG

    def kernel(p0, p1, p2, p3, out_ref, turned, placed):
        me = lax.axis_index("chan")
        for p, piece in enumerate((p0, p1, p2, p3)):
            turned[...] = piece[...].astype(F32).T
            for a in range(SEG):
                placed[pl.ds(a, span, stride=SEG), :] = turned[pl.ds(a * span, span), :]
            out_ref[:, pl.ds(pl.multiple_of((me ^ p) * part, part), part)] = placed[...]

    whole = pl.BlockSpec(memory_space=pltpu.VMEM)
    return pl.pallas_call(
        kernel,
        out_shape=jax.ShapeDtypeStruct((count, 4 * part), F32),
        in_specs=[whole] * 4,
        out_specs=whole,
        scratch_shapes=[pltpu.VMEM((count, part), F32)] * 2,
        compiler_params=pltpu.CompilerParams(vmem_limit_bytes=VMEM),
        name="enter",
    )(*pieces)


def leave(grad, own):
    rows, chans = grad.shape
    span = rows // SEG
    part = chans // 4

    def kernel(g_ref, o0, o1, o2, o3, ordered, placed):
        me = lax.axis_index("chan")
        for p, out in enumerate((o0, o1, o2, o3)):
            placed[...] = g_ref[:, pl.ds(pl.multiple_of((me ^ p) * part, part), part)]
            for a in range(SEG):
                ordered[pl.ds(a * span, span), :] = placed[pl.ds(a, span, stride=SEG), :]
            out[...] = ordered[pl.ds(HALO, own), :].T.astype(out.dtype)

    whole = pl.BlockSpec(memory_space=pltpu.VMEM)
    return pl.pallas_call(
        kernel,
        out_shape=[jax.ShapeDtypeStruct((part, own), F32)] + [jax.ShapeDtypeStruct((part, own), BF)] * 3,
        in_specs=[whole],
        out_specs=[whole] * 4,
        scratch_shapes=[pltpu.VMEM((rows, part), F32)] * 2,
        compiler_params=pltpu.CompilerParams(vmem_limit_bytes=VMEM),
        name="leave",
    )(grad)


def bottleneck(stream, joined, vecs, labels, chosen, picked_grad, own):
    rows, chans = stream.shape
    span = rows // SEG
    groups = span // STRIDE
    count = groups * SEG
    taps = joined.shape[0]
    edge = 16 * SEG

    def kernel(s_ref, q_ref, v_ref, l_ref, c_ref, o_ref, g_ref, lat_ref, dch_ref, m_ref, sum_ref, wide, full, codes, sums):
        @pl.loop(0, rows, step=CHUNK)
        def _(start):
            start = pl.multiple_of(start, CHUNK)
            act = snake(s_ref[pl.ds(start, CHUNK), :], v_ref[0:1, :], v_ref[1:2, :])
            full[pl.ds(8 + start, CHUNK), :] = act
            wide[pl.ds(edge + start, CHUNK), :] = act.astype(BF)

        wide[pl.ds(0, edge), :] = full[pl.ds(8 + rows - edge - 1, edge), :].astype(BF)
        wide[pl.ds(edge + rows, edge), :] = full[pl.ds(8 + 1, edge), :].astype(BF)

        def tap_mask(tap, first, amount):
            base = (LEAD + first * STRIDE) * SEG
            pieces = []
            for g in range(amount):
                start = base + g * STRIDE * SEG
                there = l_ref[pl.ds(start + (tap - 4) * SEG, SEG), :]
                pieces.append(jnp.where(there == l_ref[pl.ds(start, SEG), :], 1.0, 0.0).astype(F32))
            return jnp.concatenate(pieces, axis=0)

        def tap_columns(tap):
            base = edge + (tap - 4) * SEG
            picked = jnp.concatenate(
                [wide[pl.ds(base + g * STRIDE * SEG, SEG), :] for g in range(groups)], axis=0
            )
            return picked * lanes4(tap_mask(tap, 0, groups).astype(BF))

        total = jnp.zeros((count, 128), F32)
        for tap in range(taps):
            total = total + dot_nt(tap_columns(tap), q_ref[tap])
        lane = lax.broadcasted_iota(jnp.int32, (count, 128), 1)
        latent = jnp.where(lane < 8, total + pltpu.roll(total, 112, 1) + v_ref[2:3, :128], 0.0)
        lat_ref[...] = latent
        inverse = lax.rsqrt(jnp.sum(latent * latent, axis=1, keepdims=True) + 1.0)
        normed = latent * inverse
        spread = (2.0 * COMMIT) * (normed - c_ref[...])
        row = lax.broadcasted_iota(jnp.int32, (count, 128), 0)
        place = (row & (SEG - 1)) * groups + (row >> 4)
        mine = (place >= HALO // STRIDE) & (place < (HALO + own) // STRIDE)
        dch_ref[...] = jnp.where(mine, o_ref[...] - spread, 0.0)
        dlatent = (spread - normed * jnp.sum(normed * spread, axis=1, keepdims=True)) * inverse

        def split(values):
            high = values.astype(BF).astype(F32)
            return high + pltpu.roll(values - high, 8, 1), pltpu.roll(high, 16, 1)

        dmine = jnp.where(mine, dlatent, 0.0)
        sum_ref[1:2, :] = jnp.concatenate([jnp.sum(dmine, axis=0, keepdims=True)] * 4, axis=1)
        pair, _unused = split(dmine)
        pair = pair.astype(BF)
        for tap in range(taps):
            both = dot_tn(pair, tap_columns(tap))
            m_ref[tap] = both[0:8, :] + both[8:16, :]

        pair, again = split(dlatent)
        codes[pl.ds(8 + SEG, count), :] = pair + again
        codes[pl.ds(8, SEG), :] = codes[pl.ds(8 + count - 1, SEG), :]
        codes[pl.ds(8 + SEG + count, SEG), :] = codes[pl.ds(8 + SEG + 1, SEG), :]
        sums[...] = jnp.zeros_like(sums)
        for rest in range(STRIDE):
            total = None
            for tap in (rest - 4, rest + 4, rest + 12):
                if 0 <= tap < taps:
                    hop = (tap - 4 - rest) // STRIDE
                    left = codes[pl.ds(8 + SEG - hop * SEG, count), :] * tap_mask(tap, -hop, groups)
                    term = dot_nn(left.astype(BF), q_ref[tap])
                    total = term if total is None else total + term
            for g in range(groups):
                here = pl.ds((g * STRIDE + rest) * SEG, SEG)
                part = total[g * SEG : (g + 1) * SEG, :]
                value, slope, by_alpha = snake_parts(s_ref[here, :], v_ref[0:1, :], v_ref[1:2, :])
                g_ref[here, :] = part * slope
                mask = lanes4(own_mask((g * STRIDE + rest) * SEG, SEG, span, own))
                sums[...] += fold(part * by_alpha * mask)
        sum_ref[0:1, :] = sums[...].sum(axis=0, keepdims=True)
        sum_ref[2:8, :] = jnp.zeros((6, chans), F32)

    whole = pl.BlockSpec(memory_space=pltpu.VMEM)
    return pl.pallas_call(
        kernel,
        out_shape=[
            jax.ShapeDtypeStruct((rows, chans), F32),
            jax.ShapeDtypeStruct((count, 128), F32),
            jax.ShapeDtypeStruct((count, 128), F32),
            jax.ShapeDtypeStruct((taps, 8, chans), F32),
            jax.ShapeDtypeStruct((8, chans), F32),
        ],
        in_specs=[whole] * 6,
        out_specs=[whole] * 5,
        scratch_shapes=[
            pltpu.VMEM((rows + 2 * edge, chans), BF),
            pltpu.VMEM((rows + 16, chans), F32),
            pltpu.VMEM((count + 2 * SEG + 16, 128), F32),
            pltpu.VMEM((8, chans), F32),
        ],
        compiler_params=pltpu.CompilerParams(vmem_limit_bytes=VMEM),
        cost_estimate=pl.CostEstimate(
            flops=2 * rows * 4 * chans * chans, bytes_accessed=12 * 2**20, transcendentals=0
        ),
        name="bottleneck",
    )(stream, joined, vecs, labels, chosen, picked_grad)


def swap(value, axis, bit):
    count = lax.axis_size(axis)
    return lax.ppermute(value, axis, [(i, i ^ (1 << bit)) for i in range(count)])


def bits_of(axis):
    count = lax.axis_size(axis)
    return [(axis, bit) for bit in range(count.bit_length() - 1)]


def total_over(value, steps):
    for axis, bit in steps:
        value = value + swap(value, axis, bit)
    return value


def spread_sum(value, steps):
    value = value.astype(BF)
    for axis, bit in steps:
        half = value.shape[0] // 2
        low, high = value[:half], value[half:]
        upper = ((lax.axis_index(axis) >> bit) & 1) == 1
        got = swap(jnp.where(upper, low, high), axis, bit)
        value = (jnp.where(upper, high, low).astype(F32) + got.astype(F32)).astype(BF)
    for axis, bit in reversed(steps):
        upper = ((lax.axis_index(axis) >> bit) & 1) == 1
        got = swap(value, axis, bit)
        value = jnp.concatenate([jnp.where(upper, got, value), jnp.where(upper, value, got)], axis=0)
    return value


def from_owners(value):
    far = swap(value, "chan", 1)
    return [value, swap(value, "chan", 0), far, swap(far, "chan", 0)]


def to_peer(value, peer):
    return lax.ppermute(value, "chan", [(i, i ^ peer) for i in range(4)])


def terms(value, count):
    parts = []
    for _ in range(count):
        part = value.astype(BF)
        parts.append(part)
        value = value - part.astype(F32)
    return parts


def local(
    signal,
    dilated_dirs,
    dilated_gains,
    dilated_bias,
    snake_first,
    snake_second,
    pointwise_dirs,
    pointwise_gains,
    pointwise_bias,
    snake_last,
    strided_dirs,
    strided_gains,
    strided_bias,
    latent_proj,
    latent_bias,
    codebook,
    output_proj,
    output_bias,
    utterances,
    code_index,
    refill_index,
    cotangent,
):
    part, extent = signal.shape
    chans = 4 * part
    own = extent // 4
    frames = code_index.shape[0]
    own_frames = frames // 4
    whole = lax.axis_size("frames") * extent
    units = dilated_dirs.shape[0]
    span = (own + 2 * HALO) // SEG
    me = lax.axis_index("chan")
    block = lax.axis_index("frames")
    ring = lax.axis_size("frames")
    origin = block * extent + me * own

    low = signal.astype(BF)
    right = [(i, i + 1) for i in range(ring - 1)]
    left = [(i + 1, i) for i in range(ring - 1)]
    wide = jnp.concatenate(
        [
            lax.ppermute(low[:, extent - HALO :], "frames", right),
            low,
            lax.ppermute(low[:, :HALO], "frames", left),
        ],
        axis=1,
    )
    pieces = []
    for peer in range(4):
        piece = lax.dynamic_slice_in_dim(wide, (me ^ peer) * own, own + 2 * HALO, axis=1)
        pieces.append(piece if peer == 0 else to_peer(piece, peer))
    stream = enter(pieces, own)

    weights = []
    for member in range(units):
        joined = jnp.concatenate([dilated_dirs[member], pointwise_dirs[member][None]], axis=0)
        weights.append(from_owners(joined))

    square7 = jnp.sum(jnp.square(dilated_dirs.astype(F32)), axis=(1, 3)) + NORM_EPS
    square1 = jnp.sum(jnp.square(pointwise_dirs.astype(F32)), axis=2) + NORM_EPS
    scale7 = dilated_gains * lax.rsqrt(square7)
    scale1 = pointwise_gains * lax.rsqrt(square1)
    mine = [snake_first, 1.0 / snake_first, snake_second, 1.0 / snake_second, scale7, dilated_bias, scale1, pointwise_bias]
    packed = jnp.concatenate(
        [jnp.stack(mine, axis=1).reshape(8 * units, part), snake_last[None], (1.0 / snake_last)[None], jnp.zeros((6, part), F32)]
    )
    vecs = jnp.zeros((packed.shape[0], chans), F32)
    for peer in range(4):
        got = packed if peer == 0 else to_peer(packed, peer)
        vecs = lax.dynamic_update_slice(vecs, got, (0, (me ^ peer) * part))

    bounds = jnp.cumsum(utterances) * STRIDE
    b_place = jnp.arange(-LEAD, span + LEAD, dtype=jnp.int32)
    spots = (origin - HALO + b_place[:, None] + span * jnp.arange(SEG, dtype=jnp.int32)[None, :]).reshape(-1)
    found = jnp.sum((spots[:, None] >= bounds[None, :]).astype(F32), axis=1)
    found = jnp.where((spots >= 0) & (spots < whole), found, -1.0)
    labels = jnp.broadcast_to(found[:, None], (found.shape[0], 128))

    squares = jnp.sum(jnp.square(strided_dirs.astype(F32)), axis=(0, 2)) + NORM_EPS
    scales = strided_gains * lax.rsqrt(squares)
    project = latent_proj.astype(F32) * scales[None, :]
    split = jnp.concatenate(terms(project, 3), axis=0)
    taps = strided_dirs.shape[0]
    mixed = lax.dot_general(split, strided_dirs, (((1,), (1,)), ((), ())), preferred_element_type=F32)
    mixed = mixed[0:8] + mixed[8:16] + mixed[16:24]
    shift = jnp.sum(latent_proj.astype(F32) * strided_bias[None, :], axis=1)
    mixed = jnp.concatenate([mixed.reshape(8 * taps, chans), jnp.broadcast_to(jnp.pad(shift, (0, 0))[:, None], (8, chans))])
    mixed = total_over(mixed, bits_of("chan"))
    shift = mixed[8 * taps :, 0] + latent_bias
    mixed = mixed[: 8 * taps].reshape(8, taps, chans).transpose(1, 0, 2)
    high, rest = terms(mixed, 2)
    joined = jnp.concatenate([high, high, rest, jnp.zeros((taps, 104, chans), BF)], axis=1)

    coded_scale = lax.rsqrt(jnp.sum(codebook * codebook, axis=0) + 1.0)
    coded = codebook * coded_scale[None, :]
    table = jnp.concatenate(terms(coded, 3), axis=0)
    extra = HALO // STRIDE
    around = jnp.concatenate(
        [
            lax.ppermute(code_index[frames - extra :], "frames", right),
            code_index,
            lax.ppermute(code_index[:extra], "frames", left),
        ]
    )
    span_frames = span // STRIDE
    near = lax.dynamic_slice_in_dim(around, me * own_frames, own_frames + 2 * extra)
    near = near.reshape(SEG, span_frames).T.reshape(-1)
    wanted = jnp.concatenate([near, code_index])
    hot = (wanted[:, None] == jnp.arange(CODES, dtype=jnp.int32)[None, :]).astype(BF)
    found = lax.dot_general(hot, table, (((1,), (1,)), ((), ())), preferred_element_type=F32)
    found = found[:, 0:8] + found[:, 8:16] + found[:, 16:24]
    chosen = jnp.pad(found[: near.shape[0]], ((0, 0), (0, 120)))
    chosen_low = found[near.shape[0] :].astype(BF)
    output = (
        lax.dot_general(output_proj, chosen_low, (((1,), (1,)), ((), ())), preferred_element_type=F32)
        + output_bias[:, None]
    )
    dproj_out = lax.dot_general(cotangent, chosen_low, (((1,), (0,)), ((), ())), preferred_element_type=F32)
    dbias_out = jnp.sum(cotangent.astype(F32), axis=1)
    pulled = lax.dot_general(cotangent, output_proj, (((0,), (0,)), ((), ())), preferred_element_type=F32)
    mine_pulled = None
    for peer in range(4):
        piece = lax.dynamic_slice_in_dim(pulled, (me ^ peer) * own_frames, own_frames, axis=0)
        piece = piece if peer == 0 else to_peer(piece, peer)
        mine_pulled = piece if mine_pulled is None else mine_pulled + piece
    mine_pulled = jnp.pad(mine_pulled, ((extra, extra), (0, 120)))
    mine_pulled = mine_pulled.reshape(SEG, span_frames, 128).transpose(1, 0, 2).reshape(-1, 128)
    sums_out = jnp.concatenate([dproj_out, dbias_out[:, None]], axis=1)
    sums_out = total_over(sums_out, bits_of("frames"))

    saved = []
    for member in range(units):
        vec = vecs[8 * member : 8 * member + 8]
        result, middle = unit_forward(stream, weights[member], vec, labels, 3**member)
        saved.append((stream, middle, vec))
        stream = result

    tail_vecs = jnp.concatenate(
        [vecs[8 * units : 8 * units + 2], jnp.pad(shift, (0, chans - 8))[None], jnp.zeros((5, chans), F32)]
    )
    grad, latent, dchosen, mixed_grad, last_sums = bottleneck(
        stream, joined, tail_vecs, labels, chosen, mine_pulled, own
    )

    place = (
        jnp.arange(SEG, dtype=jnp.int32)[None, :] * span_frames + jnp.arange(span_frames, dtype=jnp.int32)[:, None]
    ).reshape(-1)
    owned = (place >= extra) & (place < extra + own_frames)
    place = jnp.where(owned, place - extra + block * frames + me * own_frames, -1)
    dchosen = dchosen[:, :8]
    rows_in = jnp.concatenate(terms(dchosen, 2) + [owned.astype(BF)[:, None]], axis=1)
    hot = (near[:, None] == jnp.arange(CODES, dtype=jnp.int32)[None, :]).astype(BF)
    into = lax.dot_general(rows_in, hot, (((0,), (0,)), ((), ())), preferred_element_type=F32)
    hot = (place[:, None] == refill_index[None, :]).astype(BF)
    picked = lax.dot_general(
        latent[:, :8].astype(BF), hot, (((0,), (0,)), ((), ())), preferred_element_type=F32
    )
    everything = bits_of("chan") + bits_of("frames")
    payload = jnp.concatenate(
        [
            (into[0:8] + into[8:16]).astype(BF).reshape(8 * CODES // 128, 128),
            picked.astype(BF).reshape(8 * CODES // 128, 128),
            into[16].astype(BF).reshape(CODES // 128, 128),
            mixed_grad.astype(BF).reshape(taps * 8 * chans // 128, 128),
        ],
        axis=0,
    )
    payload = jnp.pad(payload, ((0, -payload.shape[0] % 2048), (0, 0)))
    payload = spread_sum(payload, everything)

    pieces_sum, small = [None] * units, [None] * units
    for member in reversed(range(units)):
        stream_in, middle, vec = saved[member]
        spacing = 3**member
        scaled, keep, send, sums_a = unit_weights_back(
            grad, stream_in, middle, weights[member], vec, labels, spacing, own
        )
        got = swap(send, "chan", 0)
        near2 = (keep.astype(F32) + got.astype(F32)).astype(BF)
        got = swap(near2[1], "chan", 1)
        mine2 = (near2[0].astype(F32) + got.astype(F32)).astype(BF).reshape(8 * part, chans)
        pieces_sum[member] = spread_sum(mine2, bits_of("frames")).reshape(8, part, chans)
        grad, sums_b = unit_input_back(
            grad, stream_in, scaled, weights[member], vec, labels, spacing, own
        )
        small[member] = jnp.concatenate([sums_a[:3], sums_b[:1]], axis=0)

    outs = leave(grad, own)
    grad_signal = jnp.zeros((part, extent), F32)
    for peer in range(4):
        got = outs[0] if peer == 0 else to_peer(outs[peer], peer).astype(F32)
        grad_signal = lax.dynamic_update_slice(grad_signal, got, (0, (me ^ peer) * own))

    small = jnp.concatenate(small + [last_sums[0:2], jnp.zeros((2, chans), F32)], axis=0)
    small = total_over(small, everything)
    mine_small = lax.dynamic_slice_in_dim(small, me * part, part, axis=1)
    dbias1 = mine_small[0 : 4 * units : 4]
    dbias7 = mine_small[1 : 4 * units : 4]
    dalpha2 = mine_small[2 : 4 * units : 4]
    dalpha1 = mine_small[3 : 4 * units : 4]
    dalpha_last = mine_small[4 * units]
    dbias_latent = small[4 * units + 1, :8]

    size = 8 * CODES // 128
    dcoded = payload[:size].reshape(8, CODES).astype(F32)
    picked = payload[size : 2 * size].reshape(8, CODES).astype(F32)
    usage = payload[2 * size : 2 * size + CODES // 128].reshape(CODES)
    mixed_grad = payload[2 * size + CODES // 128 :][: taps * 8 * chans // 128].reshape(taps, 8, chans)
    refreshed = jnp.where(usage[None, :] > 0, codebook, picked)
    dcodebook = (dcoded - coded * jnp.sum(coded * dcoded, axis=0)[None, :]) * coded_scale[None, :]

    meeting = lax.dot_general(
        strided_dirs, mixed_grad, (((0, 2), (0, 2)), ((), ())), preferred_element_type=F32
    )
    dproj_latent = (meeting * scales[:, None]).T + dbias_latent[:, None] * strided_bias[None, :]
    dbias_strided = jnp.sum(latent_proj.astype(F32) * dbias_latent[:, None], axis=0)
    along = jnp.sum(meeting * latent_proj.astype(F32).T, axis=1)
    dstrided_gains = along * lax.rsqrt(squares)
    dweights = lax.dot_general(latent_proj, mixed_grad, (((0,), (1,)), ((), ())), preferred_element_type=F32)
    dstrided_dirs = scales[None, :, None] * dweights.transpose(1, 0, 2) - strided_dirs.astype(F32) * (
        scales * along / squares
    )[None, :, None]

    dirs7, gains7, dirs1, gains1 = [], [], [], []
    for member in range(units):
        total = pieces_sum[member].astype(F32)
        value7 = dilated_dirs[member].astype(F32)
        along7 = jnp.sum(total[:7] * value7, axis=(0, 2))
        dirs7.append(total[:7] - value7 * (along7 / square7[member])[None, :, None])
        gains7.append(along7 / dilated_gains[member])
        value1 = pointwise_dirs[member].astype(F32)
        along1 = jnp.sum(total[7] * value1, axis=1)
        dirs1.append(total[7] - value1 * (along1 / square1[member])[:, None])
        gains1.append(along1 / pointwise_gains[member])
    return (
        output,
        grad_signal,
        jnp.stack(dirs7),
        jnp.stack(gains7),
        dbias7,
        dalpha1,
        dalpha2,
        jnp.stack(dirs1),
        jnp.stack(gains1),
        dbias1,
        dalpha_last,
        dstrided_dirs,
        dstrided_gains,
        dbias_strided,
        dproj_latent,
        dbias_latent,
        dcodebook,
        sums_out[:, :8],
        sums_out[:, 8],
        refreshed,
    )


def solution(mesh):
    in_specs = (
        P("chan", "frames"),
        P(None, None, "chan", None),
        P(None, "chan"),
        P(None, "chan"),
        P(None, "chan"),
        P(None, "chan"),
        P(None, "chan", None),
        P(None, "chan"),
        P(None, "chan"),
        P("chan"),
        P(None, "chan", None),
        P("chan"),
        P("chan"),
        P(None, "chan"),
        P(),
        P(),
        P("chan", None),
        P("chan"),
        P(),
        P("frames"),
        P(),
        P("chan", "frames"),
    )
    out_specs = (
        P("chan", "frames"),
        P("chan", "frames"),
        P(None, None, "chan", None),
        P(None, "chan"),
        P(None, "chan"),
        P(None, "chan"),
        P(None, "chan"),
        P(None, "chan", None),
        P(None, "chan"),
        P(None, "chan"),
        P("chan"),
        P(None, "chan", None),
        P("chan"),
        P("chan"),
        P(None, "chan"),
        P(),
        P(),
        P("chan", None),
        P("chan"),
        P(),
    )
    return jax.shard_map(local, mesh=mesh, in_specs=in_specs, out_specs=out_specs, check_vma=False)
```

```python
import jax
import jax.numpy as jnp
from jax import lax
from jax.experimental import pallas as pl
from jax.experimental.pallas import tpu as pltpu
from jax.sharding import PartitionSpec as P

CODES = 8192
STRIDE = 8
NORM_EPS = 1e-06
COMMIT = 4.0

BF = jnp.bfloat16
F32 = jnp.float32

SEG = 16
HALO = 128
LEAD = 28
CHUNK = 256
VMEM = 60 * 2**20
def cost(micros):
    return pl.CostEstimate(flops=int(micros * 1.15e9), bytes_accessed=0, transcendentals=0)

SIN = (3.1415902692655564, -5.1674066428989045, 2.5440093135845245, -0.5594585999205443)
COS = (0.9999999532244686, -4.934792826917481, 4.0584112640152465, -1.331875904720673, 0.21968809492172123)


def by_powers(square, factors):
    total = factors[-1]
    for factor in factors[-2::-1]:
        total = factor + square * total
    return total


def snake(value, turn, inverse):
    angle = turn * value
    angle = angle - jnp.round(angle)
    square = angle * angle
    part = by_powers(square, SIN)
    return value + (square * part) * (part * inverse)


def snake_parts(value, turn, inverse):
    angle = turn * value
    angle = angle - jnp.round(angle)
    square = angle * angle
    part = by_powers(square, SIN)
    sine2 = (square * part) * (part * inverse)
    double = (angle * part) * (2.0 * by_powers(square, COS))
    return value + sine2, 1.0 + double, (value * double - sine2) * inverse


def terms(value, count):
    parts = []
    for _ in range(count):
        part = value.astype(BF)
        parts.append(part)
        value = value - part.astype(F32)
    return parts


def lanes4(mask):
    return jnp.concatenate([mask] * 4, axis=1)


def own_mask(start, count, span, own):
    row = lax.broadcasted_iota(jnp.int32, (count, 128), 0) + start
    place = (row & (SEG - 1)) * span + (row >> 4)
    return jnp.where((place >= HALO) & (place < HALO + own), 1.0, 0.0).astype(F32)


def fold(values):
    rows, cols = values.shape
    return values.reshape(rows // 8, 8, cols).sum(axis=0)


def load_weights(pieces, member, weights, sems):
    me = lax.axis_index("chan")
    first = (lax.axis_index("frames") & 1) * 4
    own7, own1, near7, near1 = (piece.at[member] for piece in pieces[:4])
    rows = own1.shape[0]

    def place(peer):
        return pl.ds(pl.multiple_of((me ^ peer) * rows, rows), rows)

    moves = [
        (own7, weights.at[pl.ds(0, 7), place(0), :]),
        (own1, weights.at[7, place(0), :]),
        (near7, weights.at[pl.ds(0, 7), place(1), :]),
        (near1, weights.at[7, place(1), :]),
    ]
    if len(pieces) == 6:
        moves += [(pieces[4], weights.at[:, place(2), :]), (pieces[5], weights.at[:, place(3), :])]
    else:
        moves += [
            (pieces[4], weights.at[pl.ds(first, 4), place(2), :]),
            (pieces[5], weights.at[pl.ds(4 - first, 4), place(2), :]),
            (pieces[6], weights.at[pl.ds(first, 4), place(3), :]),
            (pieces[7], weights.at[pl.ds(4 - first, 4), place(3), :]),
        ]
    copies = []
    for piece, target in moves:
        copy = pltpu.make_async_copy(piece, target, sems.at[len(copies)])
        copy.start()
        copies.append(copy)
    return copies


def fill_masks(mask, labels, spacing, rows):
    base = LEAD * SEG
    here = labels[pl.ds(base, rows), :]
    for tap in range(7):
        there = labels[pl.ds(base + (tap - 3) * spacing * SEG, rows), :]
        mask[tap] = jnp.where(there == here, 1.0, 0.0).astype(BF)


def fill_ends(wide, turn, margin, rows):
    edge = margin * SEG
    turn[pl.ds(8, edge + SEG), :] = wide[pl.ds(rows - SEG, edge + SEG), :].astype(F32)
    wide[pl.ds(0, edge), :] = turn[pl.ds(8 + SEG - 1, edge), :].astype(BF)
    turn[pl.ds(8, edge + SEG), :] = wide[pl.ds(edge, edge + SEG), :].astype(F32)
    wide[pl.ds(edge + rows, edge), :] = turn[pl.ds(8 + 1, edge), :].astype(BF)


class Stream:
    def __init__(self, source, target, sems):
        self.source, self.target, self.sems = source, target, sems

    def copy(self, chunk):
        here = pl.ds(chunk * CHUNK, CHUNK)
        return pltpu.make_async_copy(self.source.at[here], self.target.at[here], self.sems.at[chunk])

    def start(self, chunk):
        self.copy(chunk).start()

    def wait(self, chunk):
        self.copy(chunk).wait()


def dot_nt(left, right):
    return lax.dot_general(left, right, (((1,), (1,)), ((), ())), preferred_element_type=F32)


def dot_nn(left, right):
    return lax.dot_general(left, right, (((1,), (0,)), ((), ())), preferred_element_type=F32)


def dot_tn(left, right):
    return lax.dot_general(left, right, (((0,), (0,)), ((), ())), preferred_element_type=F32)


A1, I1, A2, I2, S7, B7, S1, B1 = range(8)


def unit_forward(stream, pieces, member, vecs, labels):
    spacing = 3**member
    rows, chans = stream.shape
    margin = 3 * spacing
    chunks = rows // CHUNK
    wide_rows = rows + 2 * margin * SEG

    def kernel(s_ref, *refs):
        parts, refs = refs[: len(pieces)], refs[len(pieces) :]
        (
            v_ref, l_ref, out_ref, mid_ref, wide_ref, w1_ref,
            weights, wide, turn, mask, stream_in, result, middle, total0, total1, sems, s_sems, o_sems, m_sems, end_sems,
        ) = refs
        incoming = Stream(s_ref, stream_in, s_sems)
        outgoing, outgoing_mid = Stream(result, out_ref, o_sems), Stream(middle, mid_ref, m_sems)
        for chunk in range(chunks):
            incoming.start(chunk)
        copies = load_weights(parts, member, weights, sems)
        fill_masks(mask, l_ref, spacing, rows)
        for chunk in range(chunks):
            incoming.wait(chunk)
            here = pl.ds(chunk * CHUNK, CHUNK)
            act = snake(stream_in[here, :], v_ref[A1 : A1 + 1, :], v_ref[I1 : I1 + 1, :])
            wide[pl.ds(margin * SEG + chunk * CHUNK, CHUNK), :] = act.astype(BF)
        fill_ends(wide, turn, margin, rows)
        keep_wide = pltpu.make_async_copy(wide, wide_ref, end_sems.at[0])
        keep_wide.start()
        for copy in copies:
            copy.wait()
        keep_w1 = pltpu.make_async_copy(weights.at[7], w1_ref, end_sems.at[1])
        keep_w1.start()

        def convolve(chunk, total_ref):
            total = None
            for tap in range(7):
                columns = wide[pl.ds(chunk * CHUNK + tap * spacing * SEG, CHUNK), :]
                if tap != 3:
                    columns = columns * lanes4(mask[tap, pl.ds(chunk * CHUNK, CHUNK), :])
                term = dot_nt(columns, weights[tap])
                total = term if total is None else total + term
            total_ref[...] = total

        def finish(chunk, total_ref):
            here = pl.ds(chunk * CHUNK, CHUNK)
            value = total_ref[...] * v_ref[S7 : S7 + 1, :] + v_ref[B7 : B7 + 1, :]
            middle[here, :] = value
            second = snake(value, v_ref[A2 : A2 + 1, :], v_ref[I2 : I2 + 1, :]).astype(BF)
            term = dot_nt(second, weights[7])
            result[here, :] = stream_in[here, :] + term * v_ref[S1 : S1 + 1, :] + v_ref[B1 : B1 + 1, :]

        totals = (total0, total1)
        convolve(0, totals[0])
        for chunk in range(chunks):
            if chunk + 1 < chunks:
                convolve(chunk + 1, totals[(chunk + 1) % 2])
            finish(chunk, totals[chunk % 2])
            outgoing_mid.start(chunk)
            outgoing.start(chunk)
        keep_wide.wait()
        keep_w1.wait()
        for chunk in range(chunks):
            outgoing_mid.wait(chunk)
            outgoing.wait(chunk)

    whole = pl.BlockSpec(memory_space=pltpu.VMEM)
    held = pl.BlockSpec(memory_space=pl.ANY)
    return pl.pallas_call(
        kernel,
        out_shape=[
            jax.ShapeDtypeStruct((rows, chans), F32),
            jax.ShapeDtypeStruct((rows, chans), F32),
            jax.ShapeDtypeStruct((wide_rows, chans), BF),
            jax.ShapeDtypeStruct((chans, chans), BF),
        ],
        in_specs=[held] * (1 + len(pieces)) + [whole] * 2,
        out_specs=[held] * 4,
        scratch_shapes=[
            pltpu.VMEM((8, chans, chans), BF),
            pltpu.VMEM((wide_rows, chans), BF),
            pltpu.VMEM((margin * SEG + SEG + 16, chans), F32),
            pltpu.VMEM((7, rows, 128), BF),
            pltpu.VMEM((rows, chans), F32),
            pltpu.VMEM((rows, chans), F32),
            pltpu.VMEM((rows, chans), F32),
            pltpu.VMEM((CHUNK, chans), F32),
            pltpu.VMEM((CHUNK, chans), F32),
            pltpu.SemaphoreType.DMA((8,)),
            pltpu.SemaphoreType.DMA((chunks,)),
            pltpu.SemaphoreType.DMA((chunks,)),
            pltpu.SemaphoreType.DMA((chunks,)),
            pltpu.SemaphoreType.DMA((2,)),
        ],
        compiler_params=pltpu.CompilerParams(vmem_limit_bytes=VMEM),
        cost_estimate=cost(12),
        name=f"unit_forward_{spacing}",
    )(stream, *pieces, vecs, labels)


class Names:
    def __init__(self, names, refs):
        self.__dict__.update(zip(names, refs, strict=True))


def units_back(vecs, labels, own, rows, chans, into=None, weights=None, others=()):
    span = rows // SEG
    part = chans // 4
    chunks = rows // CHUNK
    held, whole = pl.BlockSpec(memory_space=pl.ANY), pl.BlockSpec(memory_space=pltpu.VMEM)
    f32_rows, bf_rows = jax.ShapeDtypeStruct((rows, chans), F32), jax.ShapeDtypeStruct((rows, chans), BF)
    ins, outs, scratch = {"labels": (labels, whole)}, {}, {"mask": pltpu.VMEM((7, rows, 128), BF)}
    name, micros = "units_back", 20
    if into is not None:
        member_c, grad, stream, scaled, pieces = into
        spacing_c = 3**member_c
        margin_c = 3 * spacing_c
        name, micros = f"{name}_into_{spacing_c}", micros + 30
        ins |= {"grad": (grad, held), "stream": (stream, held), "scaled": (scaled, held)}
        ins |= {f"piece{n}": (piece, held) for n, piece in enumerate(pieces)}
        ins["vec_c"] = (vecs[member_c], whole)
        ins |= {f"other{n}": (other, whole) for n, other in enumerate(others)}
        outs |= {"out": (f32_rows, held), "sums_c": (jax.ShapeDtypeStruct((8 + 8 * len(others), chans), F32), whole)}
        scratch |= {
            "weights": pltpu.VMEM((8, chans, chans), BF),
            "wide_c": pltpu.VMEM((rows + 2 * margin_c * SEG, chans), BF),
            "turn": pltpu.VMEM((margin_c * SEG + SEG + 16, chans), F32),
            "total_c": pltpu.VMEM((8, chans), F32),
            "stream_in": pltpu.VMEM((rows, chans), F32),
            "result": pltpu.VMEM((rows, chans), F32),
            "back": pltpu.VMEM((rows, chans), F32),
            "w_sems": pltpu.SemaphoreType.DMA((8,)),
            "s_sems": pltpu.SemaphoreType.DMA((chunks,)),
            "o_sems": pltpu.SemaphoreType.DMA((chunks,)),
            "d_sem": pltpu.SemaphoreType.DMA((1,)),
        }
    else:
        ins["grad"] = (weights[1], held)
    scratch |= {"grad_in": pltpu.VMEM((rows, chans), F32), "g_sems": pltpu.SemaphoreType.DMA((chunks,))}
    if weights is not None:
        member_a, _, middle, wide_act, weight1 = weights
        spacing_a = 3**member_a
        name, micros = f"{name}_weights_{spacing_a}", micros + 14
        ins |= {"middle": (middle, held), "wide": (wide_act, held), "w1": (weight1, whole), "vec_a": (vecs[member_a], whole)}
        outs |= {
            "scaled_out": (bf_rows, held),
            "keep": (jax.ShapeDtypeStruct((2, 8, part, chans), BF), held),
            "send": (jax.ShapeDtypeStruct((2, 8, part, chans), BF), held),
            "sums_a": (jax.ShapeDtypeStruct((8, chans), F32), whole),
        }
        scratch |= {
            "middle_in": pltpu.VMEM((rows, chans), F32),
            "wide_a": pltpu.VMEM(wide_act.shape, BF),
            "scaled_a": pltpu.VMEM((rows, chans), BF),
            "low_t": pltpu.VMEM((chans, rows), BF),
            "mid_t": pltpu.VMEM((chans, rows), BF),
            "second": pltpu.VMEM((rows, chans), BF),
            "results": pltpu.VMEM((8, chans, chans), BF),
            "total_a": pltpu.VMEM((3, 8, chans), F32),
            "m_sems": pltpu.SemaphoreType.DMA((chunks,)),
            "x_sem": pltpu.SemaphoreType.DMA((1,)),
            "a_sems": pltpu.SemaphoreType.DMA((chunks,)),
            "r_sems": pltpu.SemaphoreType.DMA((8, 4)),
        }

    def go_into(r):
        get_scaled = pltpu.make_async_copy(r.scaled, r.wide_c.at[pl.ds(margin_c * SEG, rows)], r.d_sem.at[0])
        get_scaled.start()
        parts = [getattr(r, f"piece{n}") for n in range(len(pieces))]
        copies = load_weights(parts, member_c, r.weights, r.w_sems)
        incoming_grad, incoming = Stream(r.grad, r.grad_in, r.g_sems), Stream(r.stream, r.stream_in, r.s_sems)
        outgoing = Stream(r.result, r.out, r.o_sems)
        fill_masks(r.mask, r.labels, spacing_c, rows)
        r.total_c[...] = jnp.zeros_like(r.total_c)
        get_scaled.wait()
        fill_ends(r.wide_c, r.turn, margin_c, rows)
        for copy in copies:
            copy.wait()
        for chunk in range(chunks):
            incoming.start(chunk)
            incoming_grad.start(chunk)
        if weights is not None:
            start_weights(r)
        for chunk in range(chunks):
            total = None
            for tap in range(7):
                columns = r.wide_c[pl.ds(chunk * CHUNK + (6 - tap) * spacing_c * SEG, CHUNK), :]
                if tap != 3:
                    columns = columns * lanes4(r.mask[6 - tap, pl.ds(chunk * CHUNK, CHUNK), :])
                term = dot_nn(columns, r.weights[tap])
                total = term if total is None else total + term
            r.back[pl.ds(chunk * CHUNK, CHUNK), :] = total

        @pl.loop(0, chunks)
        def _(chunk):
            incoming.wait(chunk)
            incoming_grad.wait(chunk)
            here = pl.ds(chunk * CHUNK, CHUNK)
            total = r.back[here, :]
            mine = lanes4(own_mask(chunk * CHUNK, CHUNK, span, own))
            _, slope, by_alpha = snake_parts(r.stream_in[here, :], r.vec_c[A1 : A1 + 1, :], r.vec_c[I1 : I1 + 1, :])
            r.total_c[...] += fold(total * by_alpha * mine)
            r.result[here, :] = r.grad_in[here, :] + total * slope
            outgoing.start(chunk)

        r.sums_c[0:8, :] = jnp.concatenate(
            [r.total_c[...].sum(axis=0, keepdims=True), jnp.zeros((7, chans), F32)], axis=0
        )
        for n in range(len(others)):
            r.sums_c[8 * n + 8 : 8 * n + 16, :] = getattr(r, f"other{n}")[...]
        return outgoing

    def start_weights(r):
        incoming_mid = Stream(r.middle, r.middle_in, r.m_sems)
        for chunk in range(chunks):
            incoming_mid.start(chunk)
        pltpu.make_async_copy(r.wide, r.wide_a, r.x_sem.at[0]).start()

    def go_weights(r):
        me = lax.axis_index("chan")
        incoming, incoming_mid = Stream(r.grad, r.grad_in, r.g_sems), Stream(r.middle, r.middle_in, r.m_sems)
        outgoing = Stream(r.scaled_a, r.scaled_out, r.a_sems)
        grads = r.grad_in if into is None else r.result
        fill_masks(r.mask, r.labels, spacing_a, rows)
        r.total_a[...] = jnp.zeros_like(r.total_a)
        for chunk in range(chunks):
            if into is None:
                incoming.wait(chunk)
            incoming_mid.wait(chunk)
            here = pl.ds(chunk * CHUNK, CHUNK)
            mine = lanes4(own_mask(chunk * CHUNK, CHUNK, span, own))
            grad_here = grads[here, :]
            scaled_here = grad_here * r.vec_a[S1 : S1 + 1, :]
            r.low_t[:, here] = (scaled_here * mine).astype(BF).T
            back = dot_nn(scaled_here.astype(BF), r.w1[...])
            value, slope, by_alpha = snake_parts(
                r.middle_in[here, :], r.vec_a[A2 : A2 + 1, :], r.vec_a[I2 : I2 + 1, :]
            )
            r.second[here, :] = value.astype(BF)
            dmiddle = back * slope
            mine_mid = dmiddle * mine
            r.total_a[0] += fold(grad_here * mine)
            r.total_a[1] += fold(mine_mid)
            r.total_a[2] += fold(back * by_alpha * mine)
            r.scaled_a[here, :] = (dmiddle * r.vec_a[S7 : S7 + 1, :]).astype(BF)
            outgoing.start(chunk)
            r.mid_t[:, here] = (mine_mid * r.vec_a[S7 : S7 + 1, :]).astype(BF).T

        r.sums_a[...] = jnp.concatenate(
            [r.total_a[i].sum(axis=0, keepdims=True) for i in range(3)] + [jnp.zeros((5, chans), F32)], axis=0
        )
        r.results[7] = dot_nn(r.low_t[...], r.second[...]).astype(BF)
        pltpu.make_async_copy(r.wide, r.wide_a, r.x_sem.at[0]).wait()
        targets = (r.keep.at[0], r.send.at[0], r.keep.at[1], r.send.at[1])

        def out(tap, p):
            slot = pl.multiple_of((me ^ p) * part, part)
            return pltpu.make_async_copy(
                r.results.at[tap, pl.ds(slot, part), :], targets[p].at[tap], r.r_sems.at[tap, p]
            )

        for p in range(4):
            out(7, p).start()
        for tap in range(7):
            columns = r.wide_a[pl.ds(tap * (spacing_a * SEG), rows), :]
            if tap != 3:
                columns = columns * lanes4(r.mask[tap])
            r.results[tap] = dot_nn(r.mid_t[...], columns).astype(BF)
            for p in range(4):
                out(tap, p).start()
        for tap in range(8):
            for p in range(4):
                out(tap, p).wait()
        for chunk in range(chunks):
            outgoing.wait(chunk)

    def kernel(*refs):
        r = Names([*ins, *outs, *scratch], refs)
        outgoing = None
        if into is None:
            incoming = Stream(r.grad, r.grad_in, r.g_sems)
            for chunk in range(chunks):
                incoming.start(chunk)
            start_weights(r)
        else:
            outgoing = go_into(r)
        if weights is not None:
            go_weights(r)
        if outgoing is not None:
            for chunk in range(chunks):
                outgoing.wait(chunk)

    results = pl.pallas_call(
        kernel,
        out_shape=[shape for shape, _ in outs.values()],
        in_specs=[spec for _, spec in ins.values()],
        out_specs=[spec for _, spec in outs.values()],
        scratch_shapes=list(scratch.values()),
        compiler_params=pltpu.CompilerParams(vmem_limit_bytes=VMEM),
        cost_estimate=cost(micros),
        name=name,
    )(*[value for value, _ in ins.values()])
    return dict(zip(outs, results, strict=True))


def halve(dilated, pointwise):
    units, _, part, chans = dilated.shape

    def kernel(d_ref, q_ref, f0, f1, f2, held, sems, out_sems):
        first = pl.multiple_of((lax.axis_index("frames") & 1) * 4, 4)
        copies = []
        for u in range(units):
            copies.append(pltpu.make_async_copy(d_ref.at[u], held.at[u, pl.ds(0, 7)], sems.at[u]))
            copies.append(pltpu.make_async_copy(q_ref.at[u], held.at[u, 7], sems.at[units + u]))
        for copy in copies:
            copy.start()
        outs = [
            pltpu.make_async_copy(held.at[0, pl.ds(first, 4)], f0, out_sems.at[0]),
            pltpu.make_async_copy(held.at[1, pl.ds(first, 4)], f1, out_sems.at[1]),
            pltpu.make_async_copy(held.at[2], f2, out_sems.at[2]),
        ]
        for u, out in enumerate(outs):
            copies[2 * u].wait()
            copies[2 * u + 1].wait()
            out.start()
        for out in outs:
            out.wait()

    held = pl.BlockSpec(memory_space=pl.ANY)
    return pl.pallas_call(
        kernel,
        out_shape=[
            jax.ShapeDtypeStruct((4, part, chans), BF),
            jax.ShapeDtypeStruct((4, part, chans), BF),
            jax.ShapeDtypeStruct((8, part, chans), BF),
        ],
        in_specs=[held] * 2,
        out_specs=[held] * 3,
        scratch_shapes=[
            pltpu.VMEM((units, 8, part, chans), BF),
            pltpu.SemaphoreType.DMA((2 * units,)),
            pltpu.SemaphoreType.DMA((units,)),
        ],
        compiler_params=pltpu.CompilerParams(vmem_limit_bytes=VMEM),
        cost_estimate=cost(0.1),
        name="halve",
    )(dilated, pointwise)


def cut(signal):
    part, extent = signal.shape
    own = extent // 4

    def kernel(s_ref, p0, p1, p2, p3, e0, e1, e2, e3, low):
        me = lax.axis_index("chan")
        low[...] = s_ref[...].astype(BF)
        for p, (piece, end) in enumerate(((p0, e0), (p1, e1), (p2, e2), (p3, e3))):
            owner = me ^ p
            start = pl.multiple_of(owner * own, own)
            piece[:, HALO : HALO + own] = low[:, pl.ds(start, own)]
            before = pl.multiple_of(jnp.maximum(start - HALO, 0), HALO)
            piece[:, 0:HALO] = low[:, pl.ds(before, HALO)]
            behind = pl.multiple_of(jnp.minimum(start + own, extent - HALO), HALO)
            piece[:, HALO + own : 2 * HALO + own] = low[:, pl.ds(behind, HALO)]
            outer = pl.multiple_of(jnp.where(owner == 0, extent - HALO, 0), HALO)
            end[...] = low[:, pl.ds(outer, HALO)]

    whole = pl.BlockSpec(memory_space=pltpu.VMEM)
    outs = pl.pallas_call(
        kernel,
        out_shape=[jax.ShapeDtypeStruct((part, own + 2 * HALO), BF)] * 4 + [jax.ShapeDtypeStruct((part, HALO), BF)] * 4,
        in_specs=[whole],
        out_specs=[whole] * 8,
        scratch_shapes=[pltpu.VMEM((part, extent), BF)],
        compiler_params=pltpu.CompilerParams(vmem_limit_bytes=VMEM),
        cost_estimate=cost(0.1),
        name="cut",
    )(signal)
    return outs[0:4], outs[4:8]


def enter(pieces, ends, own):
    part, count = pieces[0].shape
    span = count // SEG

    def kernel(p0, p1, p2, p3, e0, e1, e2, e3, out_ref, turned, placed):
        me = lax.axis_index("chan")
        for p, (piece, end) in enumerate(((p0, e0), (p1, e1), (p2, e2), (p3, e3))):
            turned[...] = piece[...].astype(F32).T

            @pl.when(me == 0)
            def _(end=end):
                turned[0:HALO, :] = end[...].astype(F32).T

            @pl.when(me == 3)
            def _(end=end):
                turned[HALO + own : 2 * HALO + own, :] = end[...].astype(F32).T

            for a in range(SEG):
                placed[pl.ds(a, span, stride=SEG), :] = turned[pl.ds(a * span, span), :]
            out_ref[:, pl.ds(pl.multiple_of((me ^ p) * part, part), part)] = placed[...]

    whole = pl.BlockSpec(memory_space=pltpu.VMEM)
    return pl.pallas_call(
        kernel,
        out_shape=jax.ShapeDtypeStruct((count, 4 * part), F32),
        in_specs=[whole] * 8,
        out_specs=whole,
        scratch_shapes=[pltpu.VMEM((count, part), F32)] * 2,
        compiler_params=pltpu.CompilerParams(vmem_limit_bytes=VMEM),
        cost_estimate=cost(0.1),
        name="enter",
    )(*pieces, *ends)


def lane_sums(squares):
    return jnp.sum(squares.T, axis=0, keepdims=True)


def vectors(dilated, pointwise, gains7, gains1, bias7, bias1, first, second, last, project, cotangent):
    units, taps, part, chans = dilated.shape
    own_frames = cotangent.shape[1] // 4

    def kernel(d_ref, q_ref, g7, g1, b7, b1, a1, a2, a3, p_ref, t_ref, o0, o1, o2, o3, out_ref, pulled):
        out_ref[...] = jnp.zeros_like(out_ref)
        for u in range(units):
            total = jnp.zeros((part, 128), F32)
            for tap in range(taps):
                value = d_ref[u, tap].astype(F32)
                value = value * value
                for g in range(chans // 128):
                    total = total + value[:, g * 128 : (g + 1) * 128]
            value = q_ref[u].astype(F32)
            value = value * value
            total1 = jnp.zeros((part, 128), F32)
            for g in range(chans // 128):
                total1 = total1 + value[:, g * 128 : (g + 1) * 128]
            here = slice(u, u + 1)
            rows = (
                a1[here, :] * (1.0 / jnp.pi),
                1.0 / a1[here, :],
                a2[here, :] * (1.0 / jnp.pi),
                1.0 / a2[here, :],
                g7[here, :] * lax.rsqrt(lane_sums(total) + NORM_EPS),
                b7[here, :],
                g1[here, :] * lax.rsqrt(lane_sums(total1) + NORM_EPS),
                b1[here, :],
            )
            for n, row in enumerate(rows):
                out_ref[8 * u + n : 8 * u + n + 1, :] = row
        out_ref[8 * units : 8 * units + 1, :] = a3[...] * (1.0 / jnp.pi)
        out_ref[8 * units + 1 : 8 * units + 2, :] = 1.0 / a3[...]
        pulled[...] = dot_tn(p_ref[...], t_ref[...])[0:8, :]
        me = lax.axis_index("chan")
        for p, piece in enumerate((o0, o1, o2, o3)):
            piece[0 : 8 * units + 8, :] = out_ref[...]
            frames = pl.ds(pl.multiple_of((me ^ p) * own_frames, own_frames), own_frames)
            piece[8 * units + 8 : 8 * units + 16, :] = pulled[:, frames]

    whole = pl.BlockSpec(memory_space=pltpu.VMEM)
    return pl.pallas_call(
        kernel,
        out_shape=[jax.ShapeDtypeStruct((8 * units + 16, part), F32)] * 4,
        in_specs=[whole] * 11,
        out_specs=[whole] * 4,
        scratch_shapes=[
            pltpu.VMEM((8 * units + 8, part), F32),
            pltpu.VMEM((8, cotangent.shape[1]), F32),
        ],
        compiler_params=pltpu.CompilerParams(vmem_limit_bytes=VMEM),
        cost_estimate=cost(0.1),
        name="vectors",
    )(dilated, pointwise, gains7, gains1, bias7, bias1, first, second, last[None], project, cotangent)


def merge_strided(strided, gains, bias, project):
    taps, rows, chans = strided.shape

    def kernel(w_ref, g_ref, b_ref, p_ref, out_ref, norm_ref):
        total = jnp.zeros((rows, 128), F32)
        for tap in range(taps):
            value = w_ref[tap].astype(F32)
            value = value * value
            for g in range(chans // 128):
                total = total + value[:, g * 128 : (g + 1) * 128]
        inverse = lax.rsqrt(lane_sums(total) + NORM_EPS)
        scale = g_ref[...] * inverse
        norm_ref[...] = jnp.zeros_like(norm_ref)
        norm_ref[0:1, :] = scale
        norm_ref[1:2, :] = scale * inverse * inverse
        norm_ref[2:3, :] = inverse
        plain = p_ref[...].astype(F32)
        scaled = plain * scale
        split = jnp.concatenate(terms(scaled, 3), axis=0)
        for tap in range(taps):
            three = dot_nn(split, w_ref[tap])
            out_ref[8 * tap : 8 * tap + 8, :] = three[0:8] + three[8:16] + three[16:24]
        shift = jnp.sum(plain * b_ref[...], axis=1, keepdims=True)
        out_ref[8 * taps : 8 * taps + 8, :] = jnp.broadcast_to(shift, (8, chans))

    whole = pl.BlockSpec(memory_space=pltpu.VMEM)
    return pl.pallas_call(
        kernel,
        out_shape=[jax.ShapeDtypeStruct((8 * taps + 8, chans), F32), jax.ShapeDtypeStruct((8, rows), F32)],
        in_specs=[whole] * 4,
        out_specs=[whole] * 2,
        compiler_params=pltpu.CompilerParams(vmem_limit_bytes=VMEM),
        cost_estimate=cost(0.1),
        name="merge_strided",
    )(strided, gains[None], bias[None], project)


def look_up(wanted, codebook, project, cotangent, near_count):
    count = wanted.shape[0]
    codes = codebook.shape[1]
    rows, frames = cotangent.shape
    step = 512

    def kernel(i_ref, c_ref, p_ref, t_ref, near_ref, out_ref, sum_ref, found):
        found[...] = jnp.zeros_like(found)
        lane = lax.broadcasted_iota(jnp.int32, (count, 128), 1)

        @pl.loop(0, codes, step=step)
        def _(start):
            start = pl.multiple_of(start, step)
            book = c_ref[:, pl.ds(start, step)]
            book = book * lax.rsqrt(jnp.sum(book * book, axis=0, keepdims=True) + 1.0)
            table = jnp.concatenate(terms(book, 3) + [jnp.zeros((104, step), BF)], axis=0)
            wants = i_ref[...] - start
            hot = jnp.concatenate(
                [jnp.where(wants == lane + g * 128, 1.0, 0.0).astype(BF) for g in range(step // 128)], axis=1
            )
            found[...] += dot_nt(hot, table)

        total = found[...]
        total = total + pltpu.roll(total, 120, 1) + pltpu.roll(total, 112, 1)
        total = jnp.where(lane < 8, total, 0.0)
        near_ref[...] = total[:near_count]
        low = jnp.where((lane >= 8) & (lane < 11), 1.0, total)[near_count:].astype(BF)
        out_ref[...] = dot_nt(p_ref[...], low)
        sum_ref[...] = dot_nn(t_ref[...], low)

    whole = pl.BlockSpec(memory_space=pltpu.VMEM)
    return pl.pallas_call(
        kernel,
        out_shape=[
            jax.ShapeDtypeStruct((near_count, 128), F32),
            jax.ShapeDtypeStruct((rows, frames), F32),
            jax.ShapeDtypeStruct((rows, 128), F32),
        ],
        in_specs=[whole] * 4,
        out_specs=[whole] * 3,
        scratch_shapes=[pltpu.VMEM((count, 128), F32)],
        compiler_params=pltpu.CompilerParams(vmem_limit_bytes=VMEM),
        cost_estimate=cost(0.1),
        name="look_up",
    )(wanted, codebook, project, cotangent)


def code_payload(dchosen, latent, mixed_grad, near, place, refill, after_this):
    count = dchosen.shape[0]
    taps, _, chans = mixed_grad.shape
    blocks, step = refill.shape

    rows = 24 * blocks + 8 * taps
    quarter = rows // 4

    def kernel(d_ref, l_ref, m_ref, n_ref, p_ref, r_ref, _, o0, o1, o2, o3, out_ref):
        lane = lax.broadcasted_iota(jnp.int32, (count, 128), 1)
        owned = p_ref[...] >= 0
        grads = d_ref[...]
        high = grads.astype(BF).astype(F32)
        left = high + pltpu.roll(grads - high, 8, 1) + jnp.where((lane == 16) & owned, 1.0, 0.0)
        left = left.astype(BF)
        right = l_ref[...].astype(BF)

        @pl.loop(0, blocks)
        def _(block):
            wants = n_ref[...] - block * step
            hot = jnp.concatenate(
                [jnp.where(wants == lane + g * 128, 1.0, 0.0).astype(BF) for g in range(step // 128)], axis=1
            )
            into = dot_tn(left, hot)
            wanted = r_ref[pl.ds(block, 1), :]
            hot = jnp.concatenate(
                [
                    jnp.where(p_ref[...] == wanted[:, g * 128 : (g + 1) * 128], 1.0, 0.0).astype(BF)
                    for g in range(step // 128)
                ],
                axis=1,
            )
            picked = dot_tn(right, hot)
            start = pl.multiple_of(block * 24, 8)
            out_ref[pl.ds(start, 24), :] = jnp.concatenate(
                [into[0:8] + into[8:16], picked[0:8], into[16:24]], axis=0
            )

        for tap in range(taps):
            out_ref[24 * blocks + 8 * tap : 24 * blocks + 8 * tap + 8, :] = m_ref[tap]
        me = lax.axis_index("chan")
        for p, piece in enumerate((o0, o1, o2, o3)):
            piece[...] = out_ref[pl.ds(pl.multiple_of((me ^ p) * quarter, 8), quarter), :].astype(BF)

    whole = pl.BlockSpec(memory_space=pltpu.VMEM)
    held = pl.BlockSpec(memory_space=pl.ANY)
    return pl.pallas_call(
        kernel,
        out_shape=[jax.ShapeDtypeStruct((quarter, chans), BF)] * 4,
        in_specs=[whole] * 6 + [held],
        out_specs=[whole] * 4,
        scratch_shapes=[pltpu.VMEM((rows, chans), F32)],
        compiler_params=pltpu.CompilerParams(vmem_limit_bytes=VMEM),
        cost_estimate=cost(0.1),
        name="code_payload",
    )(dchosen, latent, mixed_grad, near, place, refill, after_this)


def strided_back(strided, mixed_grad, project, norms):
    taps, rows, chans = strided.shape
    group = 4

    def kernel(w_ref, m_ref, p_ref, n_ref, out_ref, vec_ref, total, factor, split):
        phase, step = pl.program_id(0), pl.program_id(1)

        @pl.when((phase == 0) & (step == 0))
        def _():
            total[...] = jnp.zeros_like(total)

        @pl.when(phase == 0)
        def _():
            meeting = total[...]
            for tap in range(group):
                meeting = meeting + dot_nt(m_ref[tap], w_ref[tap])
            total[...] = meeting

        @pl.when((phase == 1) & (step == 0))
        def _():
            plain = p_ref[...].astype(F32)
            along = jnp.sum(plain * total[...], axis=0, keepdims=True)
            vec_ref[...] = jnp.zeros_like(vec_ref)
            vec_ref[0:8, :] = total[...] * n_ref[0:1, :]
            vec_ref[8:9, :] = along * n_ref[2:3, :]
            factor[...] = jnp.broadcast_to(along * n_ref[1:2, :], (128, rows)).T
            split[...] = jnp.concatenate(terms(plain * n_ref[0:1, :], 3), axis=0)

        @pl.when(phase == 1)
        def _():
            for tap in range(group):
                three = jnp.concatenate([m_ref[tap]] * 3, axis=0)
                out_ref[tap] = dot_tn(split[...], three) - w_ref[tap].astype(F32) * lanes4(factor[...])

    whole = pl.BlockSpec(memory_space=pltpu.VMEM)
    return pl.pallas_call(
        kernel,
        grid=(2, taps // group),
        out_shape=[jax.ShapeDtypeStruct((taps, rows, chans), F32), jax.ShapeDtypeStruct((16, rows), F32)],
        in_specs=[
            pl.BlockSpec((group, rows, chans), lambda phase, step: (step, 0, 0)),
            pl.BlockSpec((group, 8, chans), lambda phase, step: (step, 0, 0)),
            whole,
            whole,
        ],
        out_specs=[
            pl.BlockSpec((group, rows, chans), lambda phase, step: (phase * step, 0, 0)),
            pl.BlockSpec((16, rows), lambda phase, step: (0, 0)),
        ],
        scratch_shapes=[pltpu.VMEM((8, rows), F32), pltpu.VMEM((rows, 128), F32), pltpu.VMEM((24, rows), BF)],
        compiler_params=pltpu.CompilerParams(vmem_limit_bytes=VMEM),
        cost_estimate=cost(0.1),
        name="strided_back",
    )(strided, mixed_grad, project, norms)


def norm_back(total, dilated, pointwise, gains, member, earlier):
    units, _, part, chans = dilated.shape

    def kernel(*refs):
        held, w_ref, q_ref, g_ref = refs[0], refs[1].at[0], refs[2], refs[3].at[0]
        out7, out1, out_g, res7, res1, row_g, sems = refs[-7:]

        def grad_of(tap):
            return held[tap * part : (tap + 1) * part, :].astype(F32)

        def weight_of(tap):
            return (q_ref[0] if tap == 7 else w_ref[tap]).astype(F32)

        def one(taps):
            square = jnp.zeros((part, 128), F32)
            along = jnp.zeros((part, 128), F32)
            for tap in taps:
                value, grad = weight_of(tap), grad_of(tap)
                both, value2 = value * grad, value * value
                for g in range(chans // 128):
                    cols = slice(g * 128, (g + 1) * 128)
                    square = square + value2[:, cols]
                    along = along + both[:, cols]
            square_sum = jnp.sum(square, axis=1, keepdims=True) + NORM_EPS
            factor = jnp.sum(along, axis=1, keepdims=True) / square_sum
            return lane_sums(along), factor

        along, factor = one(range(7))
        row_g[...] = jnp.zeros_like(row_g)
        row_g[0:1, :] = along / g_ref[0:1, :]
        outs = []
        for tap in range(7):
            res7[tap] = grad_of(tap) - weight_of(tap) * factor
            outs.append(pltpu.make_async_copy(res7.at[tap], out7.at[member, tap], sems.at[tap]))
            outs[-1].start()
        along, factor = one((7,))
        row_g[1:2, :] = along / g_ref[1:2, :]
        res1[...] = grad_of(7) - weight_of(7) * factor
        outs.append(pltpu.make_async_copy(res1, out1.at[member], sems.at[7]))
        outs[-1].start()
        outs.append(pltpu.make_async_copy(row_g, out_g.at[member], sems.at[8]))
        outs[-1].start()
        for copy in outs:
            copy.wait()

    whole = pl.BlockSpec(memory_space=pltpu.VMEM)
    held = pl.BlockSpec(memory_space=pl.ANY)
    return pl.pallas_call(
        kernel,
        grid=(1,),
        out_shape=[
            jax.ShapeDtypeStruct((units, 7, part, chans), F32),
            jax.ShapeDtypeStruct((units, part, chans), F32),
            jax.ShapeDtypeStruct((units, 8, part), F32),
        ],
        in_specs=[
            whole,
            pl.BlockSpec((1, 7, part, chans), lambda step: (member, 0, 0, 0)),
            pl.BlockSpec((1, part, chans), lambda step: (member, 0, 0)),
            pl.BlockSpec((1, 2, part), lambda step: (member, 0, 0)),
        ]
        + [held] * len(earlier),
        out_specs=[held] * 3,
        input_output_aliases={4 + n: n for n in range(len(earlier))},
        scratch_shapes=[
            pltpu.VMEM((7, part, chans), F32),
            pltpu.VMEM((part, chans), F32),
            pltpu.VMEM((8, part), F32),
            pltpu.SemaphoreType.DMA((9,)),
        ],
        compiler_params=pltpu.CompilerParams(vmem_limit_bytes=VMEM),
        cost_estimate=cost(0.1),
        name=f"norm_back_{member}",
    )(total, dilated, pointwise, gains, *earlier)


def leave(grad, own):
    rows, chans = grad.shape
    span = rows // SEG
    part = chans // 4

    def kernel(g_ref, o0, o1, o2, o3, ordered, placed):
        me = lax.axis_index("chan")
        for p, out in enumerate((o0, o1, o2, o3)):
            placed[...] = g_ref[:, pl.ds(pl.multiple_of((me ^ p) * part, part), part)]
            for a in range(SEG):
                ordered[pl.ds(a * span, span), :] = placed[pl.ds(a, span, stride=SEG), :]
            out[...] = ordered[pl.ds(HALO, own), :].T.astype(out.dtype)

    whole = pl.BlockSpec(memory_space=pltpu.VMEM)
    return pl.pallas_call(
        kernel,
        out_shape=[jax.ShapeDtypeStruct((part, own), F32)] + [jax.ShapeDtypeStruct((part, own), BF)] * 3,
        in_specs=[whole],
        out_specs=[whole] * 4,
        scratch_shapes=[pltpu.VMEM((rows, part), F32)] * 2,
        compiler_params=pltpu.CompilerParams(vmem_limit_bytes=VMEM),
        cost_estimate=cost(0.1),
        name="leave",
    )(grad)


def bottleneck(stream, merged, vecs, labels, chosen, picked_grad, own):
    rows, chans = stream.shape
    span = rows // SEG
    groups = span // STRIDE
    count = groups * SEG
    taps = merged.shape[0] // 8 - 1
    edge = 16 * SEG

    def kernel(
        s_ref, w_ref, v_ref, l_ref, c_ref, o_ref, g_ref, lat_ref, dch_ref, m_ref, sum_ref,
        q_ref, wide, full, codes, sums,
    ):
        blank = jnp.zeros((104, chans), BF)
        for tap in range(taps):
            high, rest = terms(w_ref[8 * tap : 8 * tap + 8, :], 2)
            q_ref[tap] = jnp.concatenate([high, high, rest, blank], axis=0)
        shift = jnp.sum(
            jnp.where(
                lax.broadcasted_iota(jnp.int32, (8, 128), 0) == lax.broadcasted_iota(jnp.int32, (8, 128), 1),
                w_ref[8 * taps : 8 * taps + 8, 0:128],
                0.0,
            ),
            axis=0,
            keepdims=True,
        )

        @pl.loop(0, rows, step=CHUNK)
        def _(start):
            start = pl.multiple_of(start, CHUNK)
            act = snake(s_ref[pl.ds(start, CHUNK), :], v_ref[0:1, :], v_ref[1:2, :])
            full[pl.ds(8 + start, CHUNK), :] = act
            wide[pl.ds(edge + start, CHUNK), :] = act.astype(BF)

        wide[pl.ds(0, edge), :] = full[pl.ds(8 + rows - edge - 1, edge), :].astype(BF)
        wide[pl.ds(edge + rows, edge), :] = full[pl.ds(8 + 1, edge), :].astype(BF)

        def tap_mask(tap, first, amount):
            base = (LEAD + first * STRIDE) * SEG
            pieces = []
            for g in range(amount):
                start = base + g * STRIDE * SEG
                there = l_ref[pl.ds(start + (tap - 4) * SEG, SEG), :]
                pieces.append(jnp.where(there == l_ref[pl.ds(start, SEG), :], 1.0, 0.0).astype(F32))
            return jnp.concatenate(pieces, axis=0)

        def tap_columns(tap):
            base = edge + (tap - 4) * SEG
            picked = jnp.concatenate(
                [wide[pl.ds(base + g * STRIDE * SEG, SEG), :] for g in range(groups)], axis=0
            )
            return picked * lanes4(tap_mask(tap, 0, groups).astype(BF))

        total = jnp.zeros((count, 128), F32)
        for tap in range(taps):
            total = total + dot_nt(tap_columns(tap), q_ref[tap])
        lane = lax.broadcasted_iota(jnp.int32, (count, 128), 1)
        latent = jnp.where(lane < 8, total + pltpu.roll(total, 112, 1) + shift + v_ref[2:3, :128], 0.0)
        lat_ref[...] = latent
        inverse = lax.rsqrt(jnp.sum(latent * latent, axis=1, keepdims=True) + 1.0)
        normed = latent * inverse
        spread = (2.0 * COMMIT) * (normed - c_ref[...])
        row = lax.broadcasted_iota(jnp.int32, (count, 128), 0)
        place = (row & (SEG - 1)) * groups + (row >> 4)
        mine = (place >= HALO // STRIDE) & (place < (HALO + own) // STRIDE)
        dch_ref[...] = jnp.where(mine, o_ref[...] - spread, 0.0)
        dlatent = (spread - normed * jnp.sum(normed * spread, axis=1, keepdims=True)) * inverse

        def split(values):
            high = values.astype(BF).astype(F32)
            return high + pltpu.roll(values - high, 8, 1), pltpu.roll(high, 16, 1)

        dmine = jnp.where(mine, dlatent, 0.0)
        sum_ref[1:2, :] = jnp.concatenate([jnp.sum(dmine, axis=0, keepdims=True)] * 4, axis=1)
        pair, _unused = split(dmine)
        pair = pair.astype(BF)
        for tap in range(taps):
            both = dot_tn(pair, tap_columns(tap))
            m_ref[tap] = both[0:8, :] + both[8:16, :]

        pair, again = split(dlatent)
        codes[pl.ds(8 + SEG, count), :] = pair + again
        codes[pl.ds(8, SEG), :] = codes[pl.ds(8 + count - 1, SEG), :]
        codes[pl.ds(8 + SEG + count, SEG), :] = codes[pl.ds(8 + SEG + 1, SEG), :]
        sums[...] = jnp.zeros_like(sums)
        for rest in range(STRIDE):
            total = None
            for tap in (rest - 4, rest + 4, rest + 12):
                if 0 <= tap < taps:
                    hop = (tap - 4 - rest) // STRIDE
                    left = codes[pl.ds(8 + SEG - hop * SEG, count), :] * tap_mask(tap, -hop, groups)
                    term = dot_nn(left.astype(BF), q_ref[tap])
                    total = term if total is None else total + term
            for g in range(groups):
                here = pl.ds((g * STRIDE + rest) * SEG, SEG)
                part = total[g * SEG : (g + 1) * SEG, :]
                value, slope, by_alpha = snake_parts(s_ref[here, :], v_ref[0:1, :], v_ref[1:2, :])
                g_ref[here, :] = part * slope
                mask = lanes4(own_mask((g * STRIDE + rest) * SEG, SEG, span, own))
                sums[...] += fold(part * by_alpha * mask)
        sum_ref[0:1, :] = sums[...].sum(axis=0, keepdims=True)
        sum_ref[2:8, :] = jnp.zeros((6, chans), F32)

    whole = pl.BlockSpec(memory_space=pltpu.VMEM)
    return pl.pallas_call(
        kernel,
        out_shape=[
            jax.ShapeDtypeStruct((rows, chans), F32),
            jax.ShapeDtypeStruct((count, 128), F32),
            jax.ShapeDtypeStruct((count, 128), F32),
            jax.ShapeDtypeStruct((taps, 8, chans), F32),
            jax.ShapeDtypeStruct((8, chans), F32),
        ],
        in_specs=[whole] * 6,
        out_specs=[whole] * 5,
        scratch_shapes=[
            pltpu.VMEM((taps, 128, chans), BF),
            pltpu.VMEM((rows + 2 * edge, chans), BF),
            pltpu.VMEM((rows + 16, chans), F32),
            pltpu.VMEM((count + 2 * SEG + 16, 128), F32),
            pltpu.VMEM((8, chans), F32),
        ],
        compiler_params=pltpu.CompilerParams(vmem_limit_bytes=VMEM),
        cost_estimate=cost(11),
        name="bottleneck",
    )(stream, merged, vecs, labels, chosen, picked_grad)


def swap(value, axis, bit):
    count = lax.axis_size(axis)
    return lax.ppermute(value, axis, [(i, i ^ (1 << bit)) for i in range(count)])


def bits_of(axis):
    count = lax.axis_size(axis)
    return [(axis, bit) for bit in range(count.bit_length() - 1)]


def total_over(value, steps):
    for axis, bit in steps:
        value = value + swap(value, axis, bit)
    return value


def bit_of(axis, bit):
    return (lax.axis_index(axis) >> bit) & 1


def halves_of(value, step):
    axis, bit = step
    half = value.shape[0] // 2
    mine = bit_of(axis, bit)
    kept = lax.dynamic_slice_in_dim(value, mine * half, half)
    return kept, lax.dynamic_slice_in_dim(value, (1 - mine) * half, half).astype(BF)


def add_up(kept, got):
    return (kept.astype(F32) + got.astype(F32)).astype(BF)


def sum_halves(terms_in, rows, step, micros=0.1):
    chans = terms_in[0][0][0].shape[-1]
    flat = [ref for block in terms_in for ref, _ in block]
    half = rows // 2 if step else rows

    def kernel(*refs):
        refs = list(refs)
        ins = [refs.pop(0) for _ in flat]
        outs = refs[: 2 if step else 1]
        total, sems = refs[-2:] if step else (outs[0], None)
        at, start = 0, 0
        for block in terms_in:
            value = None
            for _, index in block:
                ref = ins[at] if index is None else ins[at].at[index]
                term = ref[...].astype(F32)
                value = term if value is None else value + term
                at += 1
            value = value.astype(BF).reshape(-1, chans)
            total[start : start + value.shape[0], :] = value
            start += value.shape[0]
        if start < rows:
            total[start:rows, :] = jnp.zeros((rows - start, chans), BF)
        if step:
            mine = bit_of(*step)
            copies = []
            for n, out in enumerate(outs):
                place = pl.multiple_of((mine if n == 0 else 1 - mine) * half, 16)
                copies.append(pltpu.make_async_copy(total.at[pl.ds(place, half)], out, sems.at[n]))
                copies[-1].start()
            for copy in copies:
                copy.wait()

    def spec(ref, index):
        if index is None:
            return pl.BlockSpec(memory_space=pltpu.VMEM)
        return pl.BlockSpec((1,) + ref.shape[1:], lambda n: (index,) + (0,) * (ref.ndim - 1))

    flat_pairs = [pair for block in terms_in for pair in block]
    terms_in = [[(ref, None if index is None else 0) for ref, index in block] for block in terms_in]
    return pl.pallas_call(
        kernel,
        grid=(1,),
        out_shape=[jax.ShapeDtypeStruct((half, chans), BF)] * (2 if step else 1),
        in_specs=[spec(ref, index) for ref, index in flat_pairs],
        out_specs=[pl.BlockSpec(memory_space=pl.ANY)] * 2 if step else [pl.BlockSpec(memory_space=pltpu.VMEM)],
        scratch_shapes=[pltpu.VMEM((rows, chans), BF), pltpu.SemaphoreType.DMA((2,))] if step else [],
        compiler_params=pltpu.CompilerParams(vmem_limit_bytes=VMEM),
        cost_estimate=cost(micros),
        name="sum_halves",
    )(*flat)


def join(mine, got, step):
    rows, chans = mine.shape

    def kernel(m_ref, g_ref, out_ref):
        upper = bit_of(*step)
        out_ref[pl.ds(pl.multiple_of(upper * rows, 16), rows), :] = m_ref[...]
        out_ref[pl.ds(pl.multiple_of((1 - upper) * rows, 16), rows), :] = g_ref[...]

    whole = pl.BlockSpec(memory_space=pltpu.VMEM)
    return pl.pallas_call(
        kernel,
        out_shape=jax.ShapeDtypeStruct((2 * rows, chans), BF),
        in_specs=[whole] * 2,
        out_specs=whole,
        compiler_params=pltpu.CompilerParams(vmem_limit_bytes=VMEM),
        cost_estimate=cost(0.1),
        name="join",
    )(mine, got)


class Chain:
    def __init__(self, terms_in, rows, steps, micros=0.1):
        self.adds, self.joins = list(steps), list(reversed(steps))
        self.rows = rows
        self.kept, self.sent = sum_halves(terms_in, rows, self.adds[0], micros)
        self.whole = None
        self.left = 2 * len(steps)
        self.start()

    def start(self):
        self.got = swap(self.sent, *(self.adds[0] if self.adds else self.joins[0]))

    def step(self, token):
        got = after(self.got, token)
        self.left -= 1
        if self.adds:
            self.adds.pop(0)
            self.rows //= 2
            terms_in = [[(self.kept, None), (got, None)]]
            if self.adds:
                self.kept, self.sent = sum_halves(terms_in, self.rows, self.adds[0])
            else:
                self.sent = sum_halves(terms_in, self.rows, None)[0]
        else:
            self.sent = self.whole = join(self.sent, got, self.joins.pop(0))
        if self.left:
            self.start()
        return self.sent


def after(value, *others):
    return lax.optimization_barrier((value, *others))[0]


def to_peer(value, peer):
    return lax.ppermute(value, "chan", [(i, i ^ peer) for i in range(4)])


def local(
    signal,
    dilated_dirs,
    dilated_gains,
    dilated_bias,
    snake_first,
    snake_second,
    pointwise_dirs,
    pointwise_gains,
    pointwise_bias,
    snake_last,
    strided_dirs,
    strided_gains,
    strided_bias,
    latent_proj,
    latent_bias,
    codebook,
    output_proj,
    output_bias,
    utterances,
    code_index,
    refill_index,
    cotangent,
):
    part, extent = signal.shape
    chans = 4 * part
    own = extent // 4
    frames = code_index.shape[0]
    own_frames = frames // 4
    whole = lax.axis_size("frames") * extent
    units = dilated_dirs.shape[0]
    span = (own + 2 * HALO) // SEG
    span_frames = span // STRIDE
    extra = HALO // STRIDE
    me = lax.axis_index("chan")
    block = lax.axis_index("frames")
    ring = lax.axis_size("frames")
    origin = block * extent + me * own
    over_chan, over_frames = bits_of("chan"), bits_of("frames")

    halves = halve(dilated_dirs, pointwise_dirs)
    far = [swap(halves[0], "chan", 1)]
    close = [swap(after(dilated_dirs, halves[0]), "chan", 0), swap(after(pointwise_dirs, halves[0]), "chan", 0)]

    project = jnp.concatenate(
        [output_proj] + [term[:, None] for term in terms(output_bias, 3)] + [jnp.zeros((output_bias.shape[0], 117), BF)],
        axis=1,
    )
    packed = vectors(
        after(dilated_dirs, halves[0]), pointwise_dirs, dilated_gains, pointwise_gains, dilated_bias, pointwise_bias,
        snake_first, snake_second, snake_last, project, cotangent,
    )
    packed = [packed[0]] + [to_peer(packed[peer], peer) for peer in (1, 2, 3)]
    code_ends = after(code_index, packed[0])
    around = jnp.concatenate(
        [
            lax.ppermute(code_ends[frames - extra :], "frames", [(i, i + 1) for i in range(ring - 1)]),
            code_index,
            lax.ppermute(code_ends[:extra], "frames", [(i + 1, i) for i in range(ring - 1)]),
        ]
    )

    pieces, ends = cut(after(signal, packed[0]))
    pieces = [pieces[0]] + [to_peer(pieces[peer], peer) for peer in (1, 2, 3)]
    ends = [
        lax.ppermute(
            ends[peer],
            ("frames", "chan"),
            [(4 * (f + 1) + (3 ^ peer), 4 * f + 3) for f in range(ring - 1)]
            + [(4 * f + peer, 4 * (f + 1)) for f in range(ring - 1)],
        )
        for peer in range(4)
    ]
    rest = [swap(far[0], "frames", 0)]
    far_close = [swap(far[0], "chan", 0)]
    rest_close = [swap(rest[0], "chan", 0)]
    for member in (1, 2):
        far.append(swap(after(halves[member], *pieces), "chan", 1))
    lines = packed[0].shape[0] - 8
    vecs = jnp.zeros((lines, chans), F32)
    mine_pulled = None
    for peer in range(4):
        got = packed[peer]
        vecs = lax.dynamic_update_slice(vecs, got[:lines], (0, (me ^ peer) * part))
        mine_pulled = got[lines:] if mine_pulled is None else mine_pulled + got[lines:]
    mine_pulled = jnp.pad(mine_pulled, ((0, 120), (extra, extra)))
    mine_pulled = mine_pulled.reshape(128, SEG, span_frames).transpose(2, 1, 0).reshape(-1, 128)

    bounds = jnp.cumsum(utterances) * STRIDE
    b_place = jnp.arange(-LEAD, span + LEAD, dtype=jnp.int32)
    spots = (origin - HALO + b_place[:, None] + span * jnp.arange(SEG, dtype=jnp.int32)[None, :]).reshape(-1)
    found = jnp.sum((spots[:, None] >= bounds[None, :]).astype(F32), axis=1)
    found = jnp.where((spots >= 0) & (spots < whole), found, -1.0)
    labels = jnp.broadcast_to(found[:, None], (found.shape[0], 128))

    place = (
        jnp.arange(SEG, dtype=jnp.int32)[None, :] * span_frames + jnp.arange(span_frames, dtype=jnp.int32)[:, None]
    ).reshape(-1)
    owned = (place >= extra) & (place < extra + own_frames)
    place = jnp.where(owned, place - extra + block * frames + me * own_frames, -1)
    place = jnp.broadcast_to(place[:, None], (place.shape[0], 128))
    refill = refill_index.reshape(-1, 512)
    near = lax.dynamic_slice_in_dim(around, me * own_frames, own_frames + 2 * extra)
    near = near.reshape(SEG, span_frames).T.reshape(-1)
    wanted = jnp.broadcast_to(jnp.concatenate([near, code_index])[:, None], (near.shape[0] + frames, 128))
    *held, labels, vecs, mine_pulled, place, refill, wanted, _ = lax.optimization_barrier(
        (*pieces, *ends, labels, vecs, mine_pulled, place, refill, wanted, far[0])
    )
    near_rows = wanted[: near.shape[0]]
    stream = enter(held[:4], held[4:], own)

    def unit(member, stream, *far_pieces):
        pieces = (dilated_dirs, pointwise_dirs, *close, *far_pieces)
        vec = vecs[8 * member : 8 * member + 8]
        result, middle, wide, weight1 = unit_forward(stream, pieces, member, vec, labels)
        saved.append((stream, middle, wide, vec, weight1, pieces))
        return result

    saved = []
    stream = unit(0, stream, far[0], rest[0], far_close[0], rest_close[0])
    rest.append(swap(after(far[1], stream), "frames", 0))
    far_close.append(swap(after(far[1], stream), "chan", 0))

    chosen, output, sums_out = look_up(after(wanted, stream), codebook, project, cotangent, near.shape[0])
    rest_close.append(swap(after(rest[1], chosen), "chan", 0))
    stream = unit(1, after(stream, chosen), far[1], rest[1], far_close[1], rest_close[1])
    far_close.append(swap(after(far[2], stream), "chan", 0))
    merged, norms = merge_strided(strided_dirs, strided_gains, strided_bias, after(latent_proj, stream))
    merged = merged + swap(merged, "chan", 0)
    got = swap(merged, "chan", 1)
    stream = unit(2, after(stream, merged), far[2], far_close[2])
    merged = merged + after(got, stream)
    tail_vecs = jnp.concatenate(
        [
            vecs[8 * units : 8 * units + 2],
            jnp.pad(latent_bias, (0, chans - latent_bias.shape[0]))[None],
            jnp.zeros((5, chans), F32),
        ]
    )
    grad, latent, dchosen, mixed_grad, last_sums = bottleneck(
        stream, merged, tail_vecs, labels, chosen, mine_pulled, own
    )

    bit0, bit1 = over_chan

    unit_vecs = [saved[member][3] for member in range(units)]
    rows = grad.shape[0]

    def weights_of(member, grad=None):
        _, middle, wide, _, weight1, _ = saved[member]
        return (member, grad, middle, wide, weight1)

    def into_of(member, grad, scaled):
        return (member, grad, saved[member][0], scaled, saved[member][5])

    back2 = units_back(unit_vecs, labels, own, rows, chans, weights=weights_of(2, grad))
    keep2 = back2["keep"]
    near2 = swap(back2["send"], "chan", 0)
    chain_rows = -(-(8 * part + 128) // (16 * ring)) * 16 * ring
    codes = code_payload(dchosen, latent, mixed_grad, near_rows, place, refill, back2["sums_a"])
    codes = [codes[0]] + [to_peer(codes[peer], peer) for peer in (1, 2, 3)]
    near2 = after(near2, codes[0])
    far2 = add_up(keep2[1], near2[1])
    x2 = swap(far2, "chan", 1)
    back1 = units_back(
        unit_vecs, labels, own, rows, chans, into_of(2, after(grad, far2), back2["scaled_out"]), weights_of(1)
    )
    keep1 = back1["keep"]
    near1 = swap(back1["send"], "chan", 0)
    x2, *codes, _ = lax.optimization_barrier((x2, *codes, back1["sums_a"]))
    chain2 = Chain(
        [[(keep2, 0), (near2, 0), (x2, None)], [(piece, None) for piece in codes]], chain_rows, over_frames, 20
    )
    far1 = add_up(keep1[1], after(near1, chain2.sent)[1])
    x1 = swap(far1, "chan", 1)
    back0 = units_back(
        unit_vecs, labels, own, rows, chans,
        into_of(1, after(back1["out"], far1), back1["scaled_out"]), weights_of(0),
    )
    keep0 = back0["keep"]
    near0 = swap(back0["send"], "chan", 0)
    token = chain2.step(back0["sums_a"])
    more = sums_out[:, :16].astype(BF).reshape(-1, chans)
    more = jnp.pad(more, ((0, 16 - more.shape[0]), (0, 0)))
    chain1 = Chain([[(keep1, 0), (near1, 0), (after(x1, token), None)], [(more, None)]], chain_rows, over_frames)
    last = units_back(
        unit_vecs, labels, own, rows, chans, into_of(0, after(back0["out"], chain1.sent), back0["scaled_out"]),
        others=(back0["sums_a"], back0["sums_c"], back1["sums_a"], back1["sums_c"], back2["sums_a"], last_sums),
    )
    grad, small = last["out"], last["sums_c"]

    token = chain2.step(grad)
    token = chain1.step(token)
    far0 = add_up(keep0[1], after(near0, token)[1])
    x0 = swap(far0, "chan", 1)
    small_steps = [bit0] + over_frames + [bit1]
    small_got = swap(small, *small_steps[0])
    outs = leave(after(grad, far0), own)
    sent_outs = [outs[0]] + [to_peer(outs[peer], peer) for peer in (1, 2, 3)]
    token = outs[0]

    def small_step():
        nonlocal small, small_got, token
        small = small + after(small_got, token)
        small_steps.pop(0)
        if small_steps:
            small_got = swap(small, *small_steps[0])
        token = small

    half = len(over_frames)
    small_step()
    token = chain2.step(token)
    token = chain1.step(token)
    small_step()
    token = chain2.step(token)
    chain0 = Chain([[(keep0, 0), (near0, 0), (after(x0, token), None)]], 8 * part, over_frames)
    token = chain0.sent
    grad_signal = jnp.zeros((part, extent), F32)
    for peer in range(4):
        got = after(sent_outs[peer], token).astype(F32)
        grad_signal = lax.dynamic_update_slice(grad_signal, got, (0, (me ^ peer) * own))
    token = grad_signal
    while len(small_steps) > 2:
        small_step()
    while chain1.left > half:
        token = chain1.step(token)
    token = chain0.step(token)
    small_step()
    while chain2.left > 1:
        token = chain2.step(token)
    token = chain1.step(token)
    token = chain0.step(token)
    small_step()
    while chain1.left > 1:
        token = chain1.step(token)
    while chain0.left > half:
        token = chain0.step(token)
    token = chain2.step(token)
    quarter = codes[0].shape[0]
    total2 = chain2.whole
    codes_mine = total2[8 * part : 8 * part + quarter]
    got_codes = [codes_mine] + [to_peer(codes_mine, peer) for peer in (1, 2, 3)]
    gains = jnp.stack([dilated_gains, pointwise_gains], axis=1)
    results = norm_back(after(total2, token), dilated_dirs, pointwise_dirs, gains, 2, ())
    token = chain0.step(results[0])
    payload = jnp.zeros((4 * quarter, chans), BF)
    for peer in range(4):
        got = after(got_codes[peer], token)
        payload = lax.dynamic_update_slice_in_dim(payload, got, (me ^ peer) * quarter, 0)
    blocks = codebook.shape[1] // 512
    dstrided_dirs, meeting = strided_back(strided_dirs, payload[24 * blocks :].reshape(-1, 8, chans), latent_proj, norms)
    token = dstrided_dirs
    while chain0.left > 1:
        token = chain0.step(token)
    token = chain1.step(token)
    results = norm_back(chain1.whole, dilated_dirs, pointwise_dirs, gains, 1, results)
    payload = after(payload, token)
    codes = codebook.shape[1]
    blocks = codes // 512
    by_code = payload[: 24 * blocks].reshape(blocks, 24, 512).transpose(1, 0, 2).reshape(24, codes).astype(F32)
    dcoded, picked, usage = by_code[0:8], by_code[8:16], by_code[16]
    refreshed = jnp.where(usage[None, :] > 0, codebook, picked)
    coded_scale = lax.rsqrt(jnp.sum(codebook * codebook, axis=0) + 1.0)
    coded = codebook * coded_scale[None, :]
    dcodebook = (dcoded - coded * jnp.sum(coded * dcoded, axis=0)[None, :]) * coded_scale[None, :]

    token = lax.optimization_barrier((results[0], refreshed, dcodebook))[0]
    chain0.step(token)
    total0 = chain0.whole
    results = norm_back(total0, dilated_dirs, pointwise_dirs, gains, 0, results)
    sums_out = chain1.whole[8 * part : 8 * part + output_bias.shape[0] * 16 // chans].astype(F32).reshape(-1, 16)
    mine_small = lax.dynamic_slice_in_dim(small, me * part, part, axis=1)
    dbias_latent = small[6 * 8 + 1, :8]
    dbias1, dbias7, dalpha2 = mine_small[8:48:16], mine_small[9:48:16], mine_small[10:48:16]
    dalpha1 = mine_small[0:48:16]
    dalpha_last = mine_small[6 * 8]
    dproj_latent = meeting[0:8] + dbias_latent[:, None] * strided_bias[None, :]
    dbias_strided = jnp.sum(latent_proj.astype(F32) * dbias_latent[:, None], axis=0)
    return (
        output,
        grad_signal,
        results[0],
        results[2][:, 0],
        dbias7,
        dalpha1,
        dalpha2,
        results[1],
        results[2][:, 1],
        dbias1,
        dalpha_last,
        dstrided_dirs,
        meeting[8],
        dbias_strided,
        dproj_latent,
        dbias_latent,
        dcodebook,
        sums_out[:, :8],
        sums_out[:, 8],
        refreshed,
    )


def solution(mesh):
    in_specs = (
        P("chan", "frames"),
        P(None, None, "chan", None),
        P(None, "chan"),
        P(None, "chan"),
        P(None, "chan"),
        P(None, "chan"),
        P(None, "chan", None),
        P(None, "chan"),
        P(None, "chan"),
        P("chan"),
        P(None, "chan", None),
        P("chan"),
        P("chan"),
        P(None, "chan"),
        P(),
        P(),
        P("chan", None),
        P("chan"),
        P(),
        P("frames"),
        P(),
        P("chan", "frames"),
    )
    out_specs = (
        P("chan", "frames"),
        P("chan", "frames"),
        P(None, None, "chan", None),
        P(None, "chan"),
        P(None, "chan"),
        P(None, "chan"),
        P(None, "chan"),
        P(None, "chan", None),
        P(None, "chan"),
        P(None, "chan"),
        P("chan"),
        P(None, "chan", None),
        P("chan"),
        P("chan"),
        P(None, "chan"),
        P(),
        P(),
        P("chan", None),
        P("chan"),
        P(),
    )
    return jax.shard_map(local, mesh=mesh, in_specs=in_specs, out_specs=out_specs, check_vma=False)
```

```python
import jax
import jax.numpy as jnp
from jax import lax
from jax.experimental import pallas as pl
from jax.experimental.pallas import tpu as pltpu
from jax.sharding import PartitionSpec as P

CODES = 8192
STRIDE = 8
NORM_EPS = 1e-06
COMMIT = 4.0

BF = jnp.bfloat16
F32 = jnp.float32

SEG = 16
HALO = 128
LEAD = 28
CHUNK = 256
VMEM = 60 * 2**20
def cost(micros):
    return pl.CostEstimate(flops=int(micros * 1.15e9), bytes_accessed=0, transcendentals=0)

SIN = (3.1415902692655564, -5.1674066428989045, 2.5440093135845245, -0.5594585999205443)
COS = (0.9999999532244686, -4.934792826917481, 4.0584112640152465, -1.331875904720673, 0.21968809492172123)


def by_powers(square, factors):
    total = factors[-1]
    for factor in factors[-2::-1]:
        total = factor + square * total
    return total


def snake(value, turn, inverse):
    angle = turn * value
    angle = angle - jnp.round(angle)
    square = angle * angle
    part = by_powers(square, SIN)
    return value + (square * part) * (part * inverse)


def snake_parts(value, turn, inverse):
    angle = turn * value
    angle = angle - jnp.round(angle)
    square = angle * angle
    part = by_powers(square, SIN)
    sine2 = (square * part) * (part * inverse)
    double = (angle * part) * (2.0 * by_powers(square, COS))
    return value + sine2, 1.0 + double, (value * double - sine2) * inverse


def terms(value, count):
    parts = []
    for _ in range(count):
        part = value.astype(BF)
        parts.append(part)
        value = value - part.astype(F32)
    return parts


def lanes4(mask):
    return jnp.concatenate([mask] * 4, axis=1)


def own_mask(start, count, span, own):
    row = lax.broadcasted_iota(jnp.int32, (count, 128), 0) + start
    place = (row & (SEG - 1)) * span + (row >> 4)
    return jnp.where((place >= HALO) & (place < HALO + own), 1.0, 0.0).astype(F32)


def fold(values):
    rows, cols = values.shape
    return values.reshape(rows // 8, 8, cols).sum(axis=0)


def load_weights(pieces, member, weights, sems):
    me = lax.axis_index("chan")
    first = (lax.axis_index("frames") & 1) * 4
    own7, own1, near7, near1 = (piece.at[member] for piece in pieces[:4])
    rows = own1.shape[0]

    def place(peer):
        return pl.ds(pl.multiple_of((me ^ peer) * rows, rows), rows)

    moves = [
        (own7, weights.at[pl.ds(0, 7), place(0), :]),
        (own1, weights.at[7, place(0), :]),
        (near7, weights.at[pl.ds(0, 7), place(1), :]),
        (near1, weights.at[7, place(1), :]),
    ]
    if member == 2:
        first = 0
    moves += [
        (pieces[4], weights.at[pl.ds(first, 4), place(2), :]),
        (pieces[5], weights.at[pl.ds(4 - first, 4), place(2), :]),
        (pieces[6], weights.at[pl.ds(first, 4), place(3), :]),
        (pieces[7], weights.at[pl.ds(4 - first, 4), place(3), :]),
    ]
    copies = []
    for piece, target in moves:
        copy = pltpu.make_async_copy(piece, target, sems.at[len(copies)])
        copy.start()
        copies.append(copy)
    return copies


def fill_masks(mask, labels, spacing, rows):
    base = LEAD * SEG
    here = labels[pl.ds(base, rows), :]
    for tap in range(7):
        there = labels[pl.ds(base + (tap - 3) * spacing * SEG, rows), :]
        mask[tap] = jnp.where(there == here, 1.0, 0.0).astype(BF)


def fill_ends(wide, turn, margin, rows):
    edge = margin * SEG
    turn[pl.ds(8, edge + SEG), :] = wide[pl.ds(rows - SEG, edge + SEG), :].astype(F32)
    wide[pl.ds(0, edge), :] = turn[pl.ds(8 + SEG - 1, edge), :].astype(BF)
    turn[pl.ds(8, edge + SEG), :] = wide[pl.ds(edge, edge + SEG), :].astype(F32)
    wide[pl.ds(edge + rows, edge), :] = turn[pl.ds(8 + 1, edge), :].astype(BF)


class Stream:
    def __init__(self, source, target, sems):
        self.source, self.target, self.sems = source, target, sems

    def copy(self, chunk):
        here = pl.ds(chunk * CHUNK, CHUNK)
        return pltpu.make_async_copy(self.source.at[here], self.target.at[here], self.sems.at[chunk])

    def start(self, chunk):
        self.copy(chunk).start()

    def wait(self, chunk):
        self.copy(chunk).wait()


def dot_nt(left, right):
    return lax.dot_general(left, right, (((1,), (1,)), ((), ())), preferred_element_type=F32)


def dot_nn(left, right):
    return lax.dot_general(left, right, (((1,), (0,)), ((), ())), preferred_element_type=F32)


def dot_tn(left, right):
    return lax.dot_general(left, right, (((0,), (0,)), ((), ())), preferred_element_type=F32)


A1, I1, A2, I2, S7, B7, S1, B1 = range(8)


def unit_forward(stream, pieces, member, vecs, labels):
    spacing = 3**member
    rows, chans = stream.shape
    margin = 3 * spacing
    chunks = rows // CHUNK
    wide_rows = rows + 2 * margin * SEG

    def kernel(s_ref, *refs):
        parts, refs = refs[: len(pieces)], refs[len(pieces) :]
        (
            v_ref, l_ref, out_ref, mid_ref, wide_ref, w1_ref,
            weights, wide, turn, mask, stream_in, result, middle, total0, total1, sems, s_sems, o_sems, m_sems, end_sems,
        ) = refs
        v_ref = v_ref.at[pl.ds(8 * member, 8)]
        incoming = Stream(s_ref, stream_in, s_sems)
        outgoing, outgoing_mid = Stream(result, out_ref, o_sems), Stream(middle, mid_ref, m_sems)
        for chunk in range(chunks):
            incoming.start(chunk)
        copies = load_weights(parts, member, weights, sems)
        fill_masks(mask, l_ref, spacing, rows)
        for chunk in range(chunks):
            incoming.wait(chunk)
            here = pl.ds(chunk * CHUNK, CHUNK)
            act = snake(stream_in[here, :], v_ref[A1 : A1 + 1, :], v_ref[I1 : I1 + 1, :])
            wide[pl.ds(margin * SEG + chunk * CHUNK, CHUNK), :] = act.astype(BF)
        fill_ends(wide, turn, margin, rows)
        keep_wide = pltpu.make_async_copy(wide, wide_ref, end_sems.at[0])
        keep_wide.start()
        for copy in copies:
            copy.wait()
        keep_w1 = pltpu.make_async_copy(weights.at[7], w1_ref, end_sems.at[1])
        keep_w1.start()

        def convolve(chunk, total_ref):
            total = None
            for tap in range(7):
                columns = wide[pl.ds(chunk * CHUNK + tap * spacing * SEG, CHUNK), :]
                if tap != 3:
                    columns = columns * lanes4(mask[tap, pl.ds(chunk * CHUNK, CHUNK), :])
                term = dot_nt(columns, weights[tap])
                total = term if total is None else total + term
            total_ref[...] = total

        def finish(chunk, total_ref):
            here = pl.ds(chunk * CHUNK, CHUNK)
            value = total_ref[...] * v_ref[S7 : S7 + 1, :] + v_ref[B7 : B7 + 1, :]
            middle[here, :] = value
            second = snake(value, v_ref[A2 : A2 + 1, :], v_ref[I2 : I2 + 1, :]).astype(BF)
            term = dot_nt(second, weights[7])
            result[here, :] = stream_in[here, :] + term * v_ref[S1 : S1 + 1, :] + v_ref[B1 : B1 + 1, :]

        totals = (total0, total1)
        convolve(0, totals[0])
        for chunk in range(chunks):
            if chunk + 1 < chunks:
                convolve(chunk + 1, totals[(chunk + 1) % 2])
            finish(chunk, totals[chunk % 2])
            outgoing_mid.start(chunk)
            outgoing.start(chunk)
        keep_wide.wait()
        keep_w1.wait()
        for chunk in range(chunks):
            outgoing_mid.wait(chunk)
            outgoing.wait(chunk)

    whole = pl.BlockSpec(memory_space=pltpu.VMEM)
    held = pl.BlockSpec(memory_space=pl.ANY)
    return pl.pallas_call(
        kernel,
        out_shape=[
            jax.ShapeDtypeStruct((rows, chans), F32),
            jax.ShapeDtypeStruct((rows, chans), F32),
            jax.ShapeDtypeStruct((wide_rows, chans), BF),
            jax.ShapeDtypeStruct((chans, chans), BF),
        ],
        in_specs=[held] * (1 + len(pieces)) + [whole] * 2,
        out_specs=[held] * 4,
        scratch_shapes=[
            pltpu.VMEM((8, chans, chans), BF),
            pltpu.VMEM((wide_rows, chans), BF),
            pltpu.VMEM((margin * SEG + SEG + 16, chans), F32),
            pltpu.VMEM((7, rows, 128), BF),
            pltpu.VMEM((rows, chans), F32),
            pltpu.VMEM((rows, chans), F32),
            pltpu.VMEM((rows, chans), F32),
            pltpu.VMEM((CHUNK, chans), F32),
            pltpu.VMEM((CHUNK, chans), F32),
            pltpu.SemaphoreType.DMA((8,)),
            pltpu.SemaphoreType.DMA((chunks,)),
            pltpu.SemaphoreType.DMA((chunks,)),
            pltpu.SemaphoreType.DMA((chunks,)),
            pltpu.SemaphoreType.DMA((2,)),
        ],
        compiler_params=pltpu.CompilerParams(vmem_limit_bytes=VMEM),
        cost_estimate=cost(12),
        name=f"unit_forward_{spacing}",
    )(stream, *pieces, vecs, labels)


class Names:
    def __init__(self, names, refs):
        self.__dict__.update(zip(names, refs, strict=True))


def units_back(vecs, labels, own, rows, chans, into=None, weights=None, others=()):
    span = rows // SEG
    part = chans // 4
    chunks = rows // CHUNK
    held, whole = pl.BlockSpec(memory_space=pl.ANY), pl.BlockSpec(memory_space=pltpu.VMEM)
    f32_rows, bf_rows = jax.ShapeDtypeStruct((rows, chans), F32), jax.ShapeDtypeStruct((rows, chans), BF)
    ins, outs, scratch = {"labels": (labels, whole), "vecs": (vecs, whole)}, {}, {"mask": pltpu.VMEM((7, rows, 128), BF)}
    name, micros = "units_back", 20
    if into is not None:
        member_c, grad, stream, scaled, pieces = into
        spacing_c = 3**member_c
        margin_c = 3 * spacing_c
        name, micros = f"{name}_into_{spacing_c}", micros + 30
        ins |= {"grad": (grad, held), "stream": (stream, held), "scaled": (scaled, held)}
        ins |= {f"piece{n}": (piece, held) for n, piece in enumerate(pieces)}
        ins |= {f"other{n}": (other, whole) for n, other in enumerate(others)}
        outs |= {"out": (f32_rows, held), "sums_c": (jax.ShapeDtypeStruct((8 + 8 * len(others), chans), F32), whole)}
        scratch |= {
            "weights": pltpu.VMEM((8, chans, chans), BF),
            "wide_c": pltpu.VMEM((rows + 2 * margin_c * SEG, chans), BF),
            "turn": pltpu.VMEM((margin_c * SEG + SEG + 16, chans), F32),
            "total_c": pltpu.VMEM((8, chans), F32),
            "stream_in": pltpu.VMEM((rows, chans), F32),
            "result": pltpu.VMEM((rows, chans), F32),
            "back": pltpu.VMEM((rows, chans), F32),
            "w_sems": pltpu.SemaphoreType.DMA((8,)),
            "s_sems": pltpu.SemaphoreType.DMA((chunks,)),
            "o_sems": pltpu.SemaphoreType.DMA((chunks,)),
            "d_sem": pltpu.SemaphoreType.DMA((1,)),
        }
    else:
        ins["grad"] = (weights[1], held)
    scratch |= {"grad_in": pltpu.VMEM((rows, chans), F32), "g_sems": pltpu.SemaphoreType.DMA((chunks,))}
    if weights is not None:
        member_a, _, middle, wide_act, weight1 = weights
        spacing_a = 3**member_a
        name, micros = f"{name}_weights_{spacing_a}", micros + 14
        ins |= {"middle": (middle, held), "wide": (wide_act, held), "w1": (weight1, whole)}
        outs |= {
            "scaled_out": (bf_rows, held),
            "keep": (jax.ShapeDtypeStruct((2, 8, part, chans), BF), held),
            "send": (jax.ShapeDtypeStruct((2, 8, part, chans), BF), held),
            "sums_a": (jax.ShapeDtypeStruct((8, chans), F32), whole),
        }
        scratch |= {
            "middle_in": pltpu.VMEM((rows, chans), F32),
            "wide_a": pltpu.VMEM(wide_act.shape, BF),
            "scaled_a": pltpu.VMEM((rows, chans), BF),
            "low_t": pltpu.VMEM((chans, rows), BF),
            "mid_t": pltpu.VMEM((chans, rows), BF),
            "second": pltpu.VMEM((rows, chans), BF),
            "results": pltpu.VMEM((8, chans, chans), BF),
            "total_a": pltpu.VMEM((3, 8, chans), F32),
            "m_sems": pltpu.SemaphoreType.DMA((chunks,)),
            "x_sem": pltpu.SemaphoreType.DMA((1,)),
            "a_sems": pltpu.SemaphoreType.DMA((chunks,)),
            "r_sems": pltpu.SemaphoreType.DMA((8, 4)),
        }

    def go_into(r):
        get_scaled = pltpu.make_async_copy(r.scaled, r.wide_c.at[pl.ds(margin_c * SEG, rows)], r.d_sem.at[0])
        get_scaled.start()
        parts = [getattr(r, f"piece{n}") for n in range(len(pieces))]
        copies = load_weights(parts, member_c, r.weights, r.w_sems)
        incoming_grad, incoming = Stream(r.grad, r.grad_in, r.g_sems), Stream(r.stream, r.stream_in, r.s_sems)
        outgoing = Stream(r.result, r.out, r.o_sems)
        fill_masks(r.mask, r.labels, spacing_c, rows)
        r.total_c[...] = jnp.zeros_like(r.total_c)
        get_scaled.wait()
        fill_ends(r.wide_c, r.turn, margin_c, rows)
        for copy in copies:
            copy.wait()
        for chunk in range(chunks):
            incoming.start(chunk)
            incoming_grad.start(chunk)
        if weights is not None:
            start_weights(r)
        for chunk in range(chunks):
            total = None
            for tap in range(7):
                columns = r.wide_c[pl.ds(chunk * CHUNK + (6 - tap) * spacing_c * SEG, CHUNK), :]
                if tap != 3:
                    columns = columns * lanes4(r.mask[6 - tap, pl.ds(chunk * CHUNK, CHUNK), :])
                term = dot_nn(columns, r.weights[tap])
                total = term if total is None else total + term
            r.back[pl.ds(chunk * CHUNK, CHUNK), :] = total

        @pl.loop(0, chunks)
        def _(chunk):
            incoming.wait(chunk)
            incoming_grad.wait(chunk)
            here = pl.ds(chunk * CHUNK, CHUNK)
            total = r.back[here, :]
            mine = lanes4(own_mask(chunk * CHUNK, CHUNK, span, own))
            _, slope, by_alpha = snake_parts(r.stream_in[here, :], r.vec_c[A1 : A1 + 1, :], r.vec_c[I1 : I1 + 1, :])
            r.total_c[...] += fold(total * by_alpha * mine)
            r.result[here, :] = r.grad_in[here, :] + total * slope
            outgoing.start(chunk)

        r.sums_c[0:8, :] = jnp.concatenate(
            [r.total_c[...].sum(axis=0, keepdims=True), jnp.zeros((7, chans), F32)], axis=0
        )
        for n in range(len(others)):
            r.sums_c[8 * n + 8 : 8 * n + 16, :] = getattr(r, f"other{n}")[...]
        return outgoing

    def start_weights(r):
        incoming_mid = Stream(r.middle, r.middle_in, r.m_sems)
        for chunk in range(chunks):
            incoming_mid.start(chunk)
        pltpu.make_async_copy(r.wide, r.wide_a, r.x_sem.at[0]).start()

    def go_weights(r):
        me = lax.axis_index("chan")
        incoming, incoming_mid = Stream(r.grad, r.grad_in, r.g_sems), Stream(r.middle, r.middle_in, r.m_sems)
        outgoing = Stream(r.scaled_a, r.scaled_out, r.a_sems)
        grads = r.grad_in if into is None else r.result
        fill_masks(r.mask, r.labels, spacing_a, rows)
        r.total_a[...] = jnp.zeros_like(r.total_a)
        for chunk in range(chunks):
            if into is None:
                incoming.wait(chunk)
            incoming_mid.wait(chunk)
            here = pl.ds(chunk * CHUNK, CHUNK)
            mine = lanes4(own_mask(chunk * CHUNK, CHUNK, span, own))
            grad_here = grads[here, :]
            scaled_here = grad_here * r.vec_a[S1 : S1 + 1, :]
            r.low_t[:, here] = (scaled_here * mine).astype(BF).T
            back = dot_nn(scaled_here.astype(BF), r.w1[...])
            value, slope, by_alpha = snake_parts(
                r.middle_in[here, :], r.vec_a[A2 : A2 + 1, :], r.vec_a[I2 : I2 + 1, :]
            )
            r.second[here, :] = value.astype(BF)
            dmiddle = back * slope
            mine_mid = dmiddle * mine
            r.total_a[0] += fold(grad_here * mine)
            r.total_a[1] += fold(mine_mid)
            r.total_a[2] += fold(back * by_alpha * mine)
            r.scaled_a[here, :] = (dmiddle * r.vec_a[S7 : S7 + 1, :]).astype(BF)
            outgoing.start(chunk)
            r.mid_t[:, here] = (mine_mid * r.vec_a[S7 : S7 + 1, :]).astype(BF).T

        r.sums_a[...] = jnp.concatenate(
            [r.total_a[i].sum(axis=0, keepdims=True) for i in range(3)] + [jnp.zeros((5, chans), F32)], axis=0
        )
        r.results[7] = dot_nn(r.low_t[...], r.second[...]).astype(BF)
        pltpu.make_async_copy(r.wide, r.wide_a, r.x_sem.at[0]).wait()
        targets = (r.keep.at[0], r.send.at[0], r.keep.at[1], r.send.at[1])

        def out(tap, p):
            slot = pl.multiple_of((me ^ p) * part, part)
            return pltpu.make_async_copy(
                r.results.at[tap, pl.ds(slot, part), :], targets[p].at[tap], r.r_sems.at[tap, p]
            )

        for p in range(4):
            out(7, p).start()
        for tap in range(7):
            columns = r.wide_a[pl.ds(tap * (spacing_a * SEG), rows), :]
            if tap != 3:
                columns = columns * lanes4(r.mask[tap])
            r.results[tap] = dot_nn(r.mid_t[...], columns).astype(BF)
            for p in range(4):
                out(tap, p).start()
        for tap in range(8):
            for p in range(4):
                out(tap, p).wait()
        for chunk in range(chunks):
            outgoing.wait(chunk)

    def kernel(*refs):
        r = Names([*ins, *outs, *scratch], refs)
        if into is not None:
            r.vec_c = r.vecs.at[pl.ds(8 * member_c, 8)]
        if weights is not None:
            r.vec_a = r.vecs.at[pl.ds(8 * member_a, 8)]
        outgoing = None
        if into is None:
            incoming = Stream(r.grad, r.grad_in, r.g_sems)
            for chunk in range(chunks):
                incoming.start(chunk)
            start_weights(r)
        else:
            outgoing = go_into(r)
        if weights is not None:
            go_weights(r)
        if outgoing is not None:
            for chunk in range(chunks):
                outgoing.wait(chunk)

    results = pl.pallas_call(
        kernel,
        out_shape=[shape for shape, _ in outs.values()],
        in_specs=[spec for _, spec in ins.values()],
        out_specs=[spec for _, spec in outs.values()],
        scratch_shapes=list(scratch.values()),
        compiler_params=pltpu.CompilerParams(vmem_limit_bytes=VMEM),
        cost_estimate=cost(micros),
        name=name,
    )(*[value for value, _ in ins.values()])
    return dict(zip(outs, results, strict=True))


def halve(dilated, pointwise):
    units, _, part, chans = dilated.shape

    def kernel(d_ref, q_ref, f0, f1, f2, f3, held, sems, out_sems):
        first = pl.multiple_of((lax.axis_index("frames") & 1) * 4, 4)
        copies = []
        for u in range(units):
            copies.append(pltpu.make_async_copy(d_ref.at[u], held.at[u, pl.ds(0, 7)], sems.at[u]))
            copies.append(pltpu.make_async_copy(q_ref.at[u], held.at[u, 7], sems.at[units + u]))
        for copy in copies:
            copy.start()
        outs = [
            pltpu.make_async_copy(held.at[0, pl.ds(first, 4)], f0, out_sems.at[0]),
            pltpu.make_async_copy(held.at[1, pl.ds(first, 4)], f1, out_sems.at[1]),
            pltpu.make_async_copy(held.at[2, pl.ds(0, 4)], f2, out_sems.at[2]),
            pltpu.make_async_copy(held.at[2, pl.ds(4, 4)], f3, out_sems.at[3]),
        ]
        for u, out in zip((0, 1, 2, 2), outs, strict=True):
            if u == 2 and out is outs[3]:
                out.start()
                continue
            copies[2 * u].wait()
            copies[2 * u + 1].wait()
            out.start()
        for out in outs:
            out.wait()

    held = pl.BlockSpec(memory_space=pl.ANY)
    return pl.pallas_call(
        kernel,
        out_shape=[
            jax.ShapeDtypeStruct((4, part, chans), BF),
        ]
        * 4,
        in_specs=[held] * 2,
        out_specs=[held] * 4,
        scratch_shapes=[
            pltpu.VMEM((units, 8, part, chans), BF),
            pltpu.SemaphoreType.DMA((2 * units,)),
            pltpu.SemaphoreType.DMA((units + 1,)),
        ],
        compiler_params=pltpu.CompilerParams(vmem_limit_bytes=VMEM),
        cost_estimate=cost(0.1),
        name="halve",
    )(dilated, pointwise)


def cut(signal, packed, pulled, codes):
    part, extent = signal.shape
    own = extent // 4
    count = own + 2 * HALO
    own_frames = pulled.shape[1] // 4

    def kernel(s_ref, v_ref, u_ref, c_ref, p0, p1, p2, p3, e0, e1, e2, e3, low):
        me = lax.axis_index("chan")
        low[...] = s_ref[...].astype(BF)
        vectors3 = terms(v_ref[...], 3)
        for p, (piece, end) in enumerate(((p0, e0), (p1, e1), (p2, e2), (p3, e3))):
            owner = me ^ p
            start = pl.multiple_of(owner * own, own)
            piece[:, HALO : HALO + own] = low[:, pl.ds(start, own)]
            before = pl.multiple_of(jnp.maximum(start - HALO, 0), HALO)
            piece[:, 0:HALO] = low[:, pl.ds(before, HALO)]
            behind = pl.multiple_of(jnp.minimum(start + own, extent - HALO), HALO)
            piece[:, HALO + own : count] = low[:, pl.ds(behind, HALO)]
            frames = pl.ds(pl.multiple_of(owner * own_frames, own_frames), own_frames)
            pulled2 = jnp.concatenate([u_ref[:, frames], jnp.zeros((8, own_frames), F32)], axis=0)
            high = pulled2.astype(BF).astype(F32)
            both = jnp.concatenate([high[0:8], (pulled2 - high)[0:8]], axis=0).astype(BF)
            piece[:, count : count + 128] = jnp.concatenate(
                [*vectors3, both, jnp.zeros((128 - 3 * packed.shape[0] - 16, 128), BF)], axis=0
            )
            outer = pl.multiple_of(jnp.where(owner == 0, extent - HALO, 0), HALO)
            end[0:part, :] = low[:, pl.ds(outer, HALO)]
        first, last = c_ref[0:1, :], c_ref[codes.shape[0] - 1 : codes.shape[0], :]
        e0[part : part + 16, :] = jnp.concatenate(
            [row.astype(F32) for row in (first >> 7, first & 127, last >> 7, last & 127)] + [jnp.zeros((12, 128), F32)],
            axis=0,
        ).astype(BF)

    whole = pl.BlockSpec(memory_space=pltpu.VMEM)
    outs = pl.pallas_call(
        kernel,
        out_shape=[jax.ShapeDtypeStruct((part, count + 128), BF)] * 4
        + [jax.ShapeDtypeStruct((part + 16, HALO), BF)]
        + [jax.ShapeDtypeStruct((part, HALO), BF)] * 3,
        in_specs=[whole] * 4,
        out_specs=[whole] * 8,
        scratch_shapes=[pltpu.VMEM((part, extent), BF)],
        compiler_params=pltpu.CompilerParams(vmem_limit_bytes=VMEM),
        cost_estimate=cost(0.1),
        name="cut",
    )(signal, packed, pulled, codes)
    return outs[0:4], outs[4:8]


def enter(pieces, ends, lines, own):
    part = pieces[0].shape[0]
    count = own + 2 * HALO
    span = count // SEG

    def kernel(p0, p1, p2, p3, e0, e1, e2, e3, out_ref, vec_ref, pull_ref, code_ref, turned, placed):
        me = lax.axis_index("chan")
        pulled = jnp.zeros((8, part), F32)
        for p, (piece, end) in enumerate(((p0, e0), (p1, e1), (p2, e2), (p3, e3))):
            turned[...] = piece[:, 0:count].astype(F32).T

            @pl.when(me == 0)
            def _(end=end):
                turned[0:HALO, :] = end[0:part, :].astype(F32).T

            @pl.when(me == 3)
            def _(end=end):
                turned[HALO + own : count, :] = end[0:part, :].astype(F32).T

            for a in range(SEG):
                placed[pl.ds(a, span, stride=SEG), :] = turned[pl.ds(a * span, span), :]
            lanes = pl.ds(pl.multiple_of((me ^ p) * part, part), part)
            out_ref[:, lanes] = placed[...]
            tile = piece[:, count : count + 128].astype(F32)
            vec_ref[:, lanes] = tile[0:lines] + tile[lines : 2 * lines] + tile[2 * lines : 3 * lines]
            pulled = pulled + tile[3 * lines : 3 * lines + 8] + tile[3 * lines + 8 : 3 * lines + 16]
        pull_ref[...] = pulled
        tile = e0[part : part + 16, :].astype(F32)
        code_ref[...] = jnp.concatenate(
            [tile[0:1] * 128.0 + tile[1:2], tile[2:3] * 128.0 + tile[3:4], jnp.zeros((6, 128), F32)], axis=0
        )

    whole = pl.BlockSpec(memory_space=pltpu.VMEM)
    return pl.pallas_call(
        kernel,
        out_shape=[
            jax.ShapeDtypeStruct((count, 4 * part), F32),
            jax.ShapeDtypeStruct((lines, 4 * part), F32),
            jax.ShapeDtypeStruct((8, part), F32),
            jax.ShapeDtypeStruct((8, 128), F32),
        ],
        in_specs=[whole] * 8,
        out_specs=[whole] * 4,
        scratch_shapes=[pltpu.VMEM((count, part), F32)] * 2,
        compiler_params=pltpu.CompilerParams(vmem_limit_bytes=VMEM),
        cost_estimate=cost(0.1),
        name="enter",
    )(*pieces, *ends)


def lane_sums(squares):
    return jnp.sum(squares.T, axis=0, keepdims=True)


def vectors(dilated, pointwise, gains7, gains1, bias7, bias1, first, second, last, project, cotangent):
    units, taps, part, chans = dilated.shape

    def kernel(d_ref, q_ref, g7, g1, b7, b1, a1, a2, a3, p_ref, t_ref, out_ref, pulled):
        out_ref[...] = jnp.zeros_like(out_ref)
        for u in range(units):
            total = jnp.zeros((part, 128), F32)
            for tap in range(taps):
                value = d_ref[u, tap].astype(F32)
                value = value * value
                for g in range(chans // 128):
                    total = total + value[:, g * 128 : (g + 1) * 128]
            value = q_ref[u].astype(F32)
            value = value * value
            total1 = jnp.zeros((part, 128), F32)
            for g in range(chans // 128):
                total1 = total1 + value[:, g * 128 : (g + 1) * 128]
            here = slice(u, u + 1)
            rows = (
                a1[here, :] * (1.0 / jnp.pi),
                1.0 / a1[here, :],
                a2[here, :] * (1.0 / jnp.pi),
                1.0 / a2[here, :],
                g7[here, :] * lax.rsqrt(lane_sums(total) + NORM_EPS),
                b7[here, :],
                g1[here, :] * lax.rsqrt(lane_sums(total1) + NORM_EPS),
                b1[here, :],
            )
            for n, row in enumerate(rows):
                out_ref[8 * u + n : 8 * u + n + 1, :] = row
        out_ref[8 * units : 8 * units + 1, :] = a3[...] * (1.0 / jnp.pi)
        out_ref[8 * units + 1 : 8 * units + 2, :] = 1.0 / a3[...]
        pulled[...] = dot_tn(p_ref[...], t_ref[...])[0:8, :]

    whole = pl.BlockSpec(memory_space=pltpu.VMEM)
    return pl.pallas_call(
        kernel,
        out_shape=[
            jax.ShapeDtypeStruct((8 * units + 8, part), F32),
            jax.ShapeDtypeStruct((8, cotangent.shape[1]), F32),
        ],
        in_specs=[whole] * 11,
        out_specs=[whole] * 2,
        compiler_params=pltpu.CompilerParams(vmem_limit_bytes=VMEM),
        cost_estimate=cost(0.1),
        name="vectors",
    )(dilated, pointwise, gains7, gains1, bias7, bias1, first, second, last[None], project, cotangent)


def merge_strided(strided, gains, bias, project):
    taps, rows, chans = strided.shape

    def kernel(w_ref, g_ref, b_ref, p_ref, out_ref, norm_ref):
        total = jnp.zeros((rows, 128), F32)
        for tap in range(taps):
            value = w_ref[tap].astype(F32)
            value = value * value
            for g in range(chans // 128):
                total = total + value[:, g * 128 : (g + 1) * 128]
        inverse = lax.rsqrt(lane_sums(total) + NORM_EPS)
        scale = g_ref[...] * inverse
        norm_ref[...] = jnp.zeros_like(norm_ref)
        norm_ref[0:1, :] = scale
        norm_ref[1:2, :] = scale * inverse * inverse
        norm_ref[2:3, :] = inverse
        plain = p_ref[...].astype(F32)
        scaled = plain * scale
        split = jnp.concatenate(terms(scaled, 3), axis=0)
        for tap in range(taps):
            three = dot_nn(split, w_ref[tap])
            out_ref[8 * tap : 8 * tap + 8, :] = three[0:8] + three[8:16] + three[16:24]
        shift = jnp.sum(plain * b_ref[...], axis=1, keepdims=True)
        out_ref[8 * taps : 8 * taps + 8, :] = jnp.broadcast_to(shift, (8, chans))

    whole = pl.BlockSpec(memory_space=pltpu.VMEM)
    return pl.pallas_call(
        kernel,
        out_shape=[jax.ShapeDtypeStruct((8 * taps + 8, chans), F32), jax.ShapeDtypeStruct((8, rows), F32)],
        in_specs=[whole] * 4,
        out_specs=[whole] * 2,
        compiler_params=pltpu.CompilerParams(vmem_limit_bytes=VMEM),
        cost_estimate=cost(5),
        name="merge_strided",
    )(strided, gains[None], bias[None], project)


def look_up(wanted, codebook, project, cotangent, near_count):
    count = wanted.shape[0]
    codes = codebook.shape[1]
    rows, frames = cotangent.shape
    step = 512

    def kernel(i_ref, c_ref, p_ref, t_ref, near_ref, out_ref, sum_ref, found):
        found[...] = jnp.zeros_like(found)
        lane = lax.broadcasted_iota(jnp.int32, (count, 128), 1)

        @pl.loop(0, codes, step=step)
        def _(start):
            start = pl.multiple_of(start, step)
            book = c_ref[:, pl.ds(start, step)]
            book = book * lax.rsqrt(jnp.sum(book * book, axis=0, keepdims=True) + 1.0)
            table = jnp.concatenate(terms(book, 3) + [jnp.zeros((104, step), BF)], axis=0)
            wants = i_ref[...] - start
            hot = jnp.concatenate(
                [jnp.where(wants == lane + g * 128, 1.0, 0.0).astype(BF) for g in range(step // 128)], axis=1
            )
            found[...] += dot_nt(hot, table)

        total = found[...]
        total = total + pltpu.roll(total, 120, 1) + pltpu.roll(total, 112, 1)
        total = jnp.where(lane < 8, total, 0.0)
        near_ref[...] = total[:near_count]
        low = jnp.where((lane >= 8) & (lane < 11), 1.0, total)[near_count:].astype(BF)
        out_ref[...] = dot_nt(p_ref[...], low)
        sum_ref[...] = dot_nn(t_ref[...], low)

    whole = pl.BlockSpec(memory_space=pltpu.VMEM)
    return pl.pallas_call(
        kernel,
        out_shape=[
            jax.ShapeDtypeStruct((near_count, 128), F32),
            jax.ShapeDtypeStruct((rows, frames), F32),
            jax.ShapeDtypeStruct((rows, 128), F32),
        ],
        in_specs=[whole] * 4,
        out_specs=[whole] * 3,
        scratch_shapes=[pltpu.VMEM((count, 128), F32)],
        compiler_params=pltpu.CompilerParams(vmem_limit_bytes=VMEM),
        cost_estimate=cost(0.1),
        name="look_up",
    )(wanted, codebook, project, cotangent)


def code_payload(dchosen, latent, mixed_grad, near, place, refill, after_this):
    count = dchosen.shape[0]
    taps, _, chans = mixed_grad.shape
    blocks, step = refill.shape

    rows = 24 * blocks + 8 * taps
    quarter = rows // 4

    def kernel(d_ref, l_ref, m_ref, n_ref, p_ref, r_ref, _, o0, o1, o2, o3, out_ref):
        lane = lax.broadcasted_iota(jnp.int32, (count, 128), 1)
        owned = p_ref[...] >= 0
        grads = d_ref[...]
        high = grads.astype(BF).astype(F32)
        left = high + pltpu.roll(grads - high, 8, 1) + jnp.where((lane == 16) & owned, 1.0, 0.0)
        left = left.astype(BF)
        right = l_ref[...].astype(BF)

        @pl.loop(0, blocks)
        def _(block):
            wants = n_ref[...] - block * step
            hot = jnp.concatenate(
                [jnp.where(wants == lane + g * 128, 1.0, 0.0).astype(BF) for g in range(step // 128)], axis=1
            )
            into = dot_tn(left, hot)
            wanted = r_ref[pl.ds(block, 1), :]
            hot = jnp.concatenate(
                [
                    jnp.where(p_ref[...] == wanted[:, g * 128 : (g + 1) * 128], 1.0, 0.0).astype(BF)
                    for g in range(step // 128)
                ],
                axis=1,
            )
            picked = dot_tn(right, hot)
            start = pl.multiple_of(block * 24, 8)
            out_ref[pl.ds(start, 24), :] = jnp.concatenate(
                [into[0:8] + into[8:16], picked[0:8], into[16:24]], axis=0
            )

        for tap in range(taps):
            out_ref[24 * blocks + 8 * tap : 24 * blocks + 8 * tap + 8, :] = m_ref[tap]
        me = lax.axis_index("chan")
        for p, piece in enumerate((o0, o1, o2, o3)):
            piece[...] = out_ref[pl.ds(pl.multiple_of((me ^ p) * quarter, 8), quarter), :].astype(BF)

    whole = pl.BlockSpec(memory_space=pltpu.VMEM)
    held = pl.BlockSpec(memory_space=pl.ANY)
    return pl.pallas_call(
        kernel,
        out_shape=[jax.ShapeDtypeStruct((quarter, chans), BF)] * 4,
        in_specs=[whole] * 6 + [held],
        out_specs=[whole] * 4,
        scratch_shapes=[pltpu.VMEM((rows, chans), F32)],
        compiler_params=pltpu.CompilerParams(vmem_limit_bytes=VMEM),
        cost_estimate=cost(0.1),
        name="code_payload",
    )(dchosen, latent, mixed_grad, near, place, refill, after_this)


def strided_back(strided, mixed_grad, project, norms):
    taps, rows, chans = strided.shape
    group = 4

    def kernel(w_ref, m_ref, p_ref, n_ref, out_ref, vec_ref, kept, total, factor, split):
        phase, step = pl.program_id(0), pl.program_id(1)

        @pl.when((phase == 0) & (step == 0))
        def _():
            total[...] = jnp.zeros_like(total)

        @pl.when(phase == 0)
        def _():
            meeting = total[...]
            for tap in range(group):
                meeting = meeting + dot_nt(m_ref[tap], w_ref[tap])
            total[...] = meeting
            kept[step] = w_ref[...]

        @pl.when((phase == 1) & (step == 0))
        def _():
            plain = p_ref[...].astype(F32)
            along = jnp.sum(plain * total[...], axis=0, keepdims=True)
            vec_ref[...] = jnp.zeros_like(vec_ref)
            vec_ref[0:8, :] = total[...] * n_ref[0:1, :]
            vec_ref[8:9, :] = along * n_ref[2:3, :]
            factor[...] = jnp.broadcast_to(along * n_ref[1:2, :], (128, rows)).T
            split[...] = jnp.concatenate(terms(plain * n_ref[0:1, :], 3), axis=0)

        @pl.when(phase == 1)
        def _():
            for tap in range(group):
                three = jnp.concatenate([m_ref[tap]] * 3, axis=0)
                out_ref[tap] = dot_tn(split[...], three) - kept[step, tap].astype(F32) * lanes4(factor[...])

    whole = pl.BlockSpec(memory_space=pltpu.VMEM)
    return pl.pallas_call(
        kernel,
        grid=(2, taps // group),
        out_shape=[jax.ShapeDtypeStruct((taps, rows, chans), F32), jax.ShapeDtypeStruct((16, rows), F32)],
        in_specs=[
            pl.BlockSpec((group, rows, chans), lambda phase, step: (step * (1 - phase) + (taps // group - 1) * phase, 0, 0)),
            pl.BlockSpec((group, 8, chans), lambda phase, step: (step, 0, 0)),
            whole,
            whole,
        ],
        out_specs=[
            pl.BlockSpec((group, rows, chans), lambda phase, step: (phase * step, 0, 0)),
            pl.BlockSpec((16, rows), lambda phase, step: (0, 0)),
        ],
        scratch_shapes=[
            pltpu.VMEM((taps // group, group, rows, chans), BF),
            pltpu.VMEM((8, rows), F32), pltpu.VMEM((rows, 128), F32),
            pltpu.VMEM((24, rows), BF),
        ],
        compiler_params=pltpu.CompilerParams(vmem_limit_bytes=VMEM),
        cost_estimate=cost(0.1),
        name="strided_back",
    )(strided, mixed_grad, project, norms)


def norm_back(chains, dilated, pointwise, gains, members, earlier):
    units, _, part, chans = dilated.shape
    count = len(members)

    def kernel(*refs):
        halves, refs = refs[: 2 * count], refs[2 * count :]
        w_refs, q_refs, g_refs = (refs[n * count : (n + 1) * count] for n in range(3))
        out7, out1, out_g, helds, res7, res1, row_g, sems = refs[-8:]
        outs = []

        def send(value, target):
            outs.append(pltpu.make_async_copy(value, target, sems.at[len(outs)]))
            outs[-1].start()

        for n, member in enumerate(members):
            rows = halves[2 * n].shape[0]
            upper = bit_of(*chains[n].last)
            helds[n, pl.ds(pl.multiple_of(upper * rows, 16), rows), :] = halves[2 * n][...]
            helds[n, pl.ds(pl.multiple_of((1 - upper) * rows, 16), rows), :] = halves[2 * n + 1][...]

            def grad_of(tap, n=n):
                return helds[n, tap * part : (tap + 1) * part, :].astype(F32)

            def weight_of(tap, n=n):
                return (q_refs[n][0] if tap == 7 else w_refs[n][0, tap]).astype(F32)

            row_g[n] = jnp.zeros_like(row_g[n])
            for which, taps in enumerate((range(7), (7,))):
                square = jnp.zeros((part, 128), F32)
                along = jnp.zeros((part, 128), F32)
                for tap in taps:
                    value, grad = weight_of(tap), grad_of(tap)
                    both, value2 = value * grad, value * value
                    for g in range(chans // 128):
                        cols = slice(g * 128, (g + 1) * 128)
                        square = square + value2[:, cols]
                        along = along + both[:, cols]
                square_sum = jnp.sum(square, axis=1, keepdims=True) + NORM_EPS
                factor = jnp.sum(along, axis=1, keepdims=True) / square_sum
                row_g[n, which : which + 1, :] = lane_sums(along) / g_refs[n][0, which : which + 1, :]
                for tap in taps:
                    target = res1.at[n] if tap == 7 else res7.at[n, tap]
                    target[...] = grad_of(tap) - weight_of(tap) * factor
                    send(target, out1.at[member] if tap == 7 else out7.at[member, tap])
            send(row_g.at[n], out_g.at[member])
        for copy in outs:
            copy.wait()

    whole = pl.BlockSpec(memory_space=pltpu.VMEM)
    held = pl.BlockSpec(memory_space=pl.ANY)

    def block(shape, member):
        return pl.BlockSpec((1,) + shape, lambda step: (member,) + (0,) * len(shape))

    return pl.pallas_call(
        kernel,
        grid=(1,),
        out_shape=[
            jax.ShapeDtypeStruct((units, 7, part, chans), F32),
            jax.ShapeDtypeStruct((units, part, chans), F32),
            jax.ShapeDtypeStruct((units, 8, part), F32),
        ],
        in_specs=[whole] * (2 * count)
        + [block((7, part, chans), member) for member in members]
        + [block((part, chans), member) for member in members]
        + [block((2, part), member) for member in members]
        + [held] * len(earlier),
        out_specs=[held] * 3,
        input_output_aliases={5 * count + n: n for n in range(len(earlier))},
        scratch_shapes=[
            pltpu.VMEM((count, max(2 * chain.whole[0].shape[0] for chain in chains), chans), BF),
            pltpu.VMEM((count, 7, part, chans), F32),
            pltpu.VMEM((count, part, chans), F32),
            pltpu.VMEM((count, 8, part), F32),
            pltpu.SemaphoreType.DMA((9 * count,)),
        ],
        compiler_params=pltpu.CompilerParams(vmem_limit_bytes=VMEM),
        cost_estimate=cost(0.1),
        name="norm_back",
    )(*[half for chain in chains for half in chain.whole], *[dilated] * count, *[pointwise] * count, *[gains] * count, *earlier)


def leave(grad, own):
    rows, chans = grad.shape
    span = rows // SEG
    part = chans // 4

    def kernel(g_ref, o0, o1, o2, o3, ordered, placed):
        me = lax.axis_index("chan")
        for p, out in enumerate((o0, o1, o2, o3)):
            placed[...] = g_ref[:, pl.ds(pl.multiple_of((me ^ p) * part, part), part)]
            for a in range(SEG):
                ordered[pl.ds(a * span, span), :] = placed[pl.ds(a, span, stride=SEG), :]
            out[...] = ordered[pl.ds(HALO, own), :].T.astype(out.dtype)

    whole = pl.BlockSpec(memory_space=pltpu.VMEM)
    return pl.pallas_call(
        kernel,
        out_shape=[jax.ShapeDtypeStruct((part, own), F32)] + [jax.ShapeDtypeStruct((part, own), BF)] * 3,
        in_specs=[whole],
        out_specs=[whole] * 4,
        scratch_shapes=[pltpu.VMEM((rows, part), F32)] * 2,
        compiler_params=pltpu.CompilerParams(vmem_limit_bytes=VMEM),
        cost_estimate=cost(0.1),
        name="leave",
    )(grad)


def settle(pieces):
    part, own = pieces[0].shape

    def kernel(p0, p1, p2, p3, out_ref):
        me = lax.axis_index("chan")
        for p, piece in enumerate((p0, p1, p2, p3)):
            out_ref[:, pl.ds(pl.multiple_of((me ^ p) * own, own), own)] = piece[...].astype(F32)

    whole = pl.BlockSpec(memory_space=pltpu.VMEM)
    return pl.pallas_call(
        kernel,
        out_shape=jax.ShapeDtypeStruct((part, 4 * own), F32),
        in_specs=[whole] * 4,
        out_specs=whole,
        compiler_params=pltpu.CompilerParams(vmem_limit_bytes=VMEM),
        cost_estimate=cost(0.1),
        name="settle",
    )(*pieces)


def bottleneck(stream, merged, bias, vecs, labels, chosen, picked_grad, own):
    rows, chans = stream.shape
    span = rows // SEG
    groups = span // STRIDE
    count = groups * SEG
    taps = merged[0].shape[0] // 8 - 1
    edge = 16 * SEG
    turn_row = vecs.shape[0] - 8

    def kernel(
        s_ref, wa_ref, wb_ref, bias_ref, v_ref, l_ref, c_ref, o_ref, g_ref, lat_ref, dch_ref, m_ref, sum_ref,
        q_ref, wide, full, codes, sums,
    ):
        blank = jnp.zeros((104, chans), BF)
        for tap in range(taps):
            here = slice(8 * tap, 8 * tap + 8)
            high, rest = terms(wa_ref[here, :] + wb_ref[here, :], 2)
            q_ref[tap] = jnp.concatenate([high, high, rest, blank], axis=0)
        shift = jnp.sum(
            jnp.where(
                lax.broadcasted_iota(jnp.int32, (8, 128), 0) == lax.broadcasted_iota(jnp.int32, (8, 128), 1),
                wa_ref[8 * taps : 8 * taps + 8, 0:128] + wb_ref[8 * taps : 8 * taps + 8, 0:128],
                0.0,
            ),
            axis=0,
            keepdims=True,
        )

        @pl.loop(0, rows, step=CHUNK)
        def _(start):
            start = pl.multiple_of(start, CHUNK)
            act = snake(s_ref[pl.ds(start, CHUNK), :], v_ref[turn_row : turn_row + 1, :], v_ref[turn_row + 1 : turn_row + 2, :])
            full[pl.ds(8 + start, CHUNK), :] = act
            wide[pl.ds(edge + start, CHUNK), :] = act.astype(BF)

        wide[pl.ds(0, edge), :] = full[pl.ds(8 + rows - edge - 1, edge), :].astype(BF)
        wide[pl.ds(edge + rows, edge), :] = full[pl.ds(8 + 1, edge), :].astype(BF)

        def tap_mask(tap, first, amount):
            base = (LEAD + first * STRIDE) * SEG
            pieces = []
            for g in range(amount):
                start = base + g * STRIDE * SEG
                there = l_ref[pl.ds(start + (tap - 4) * SEG, SEG), :]
                pieces.append(jnp.where(there == l_ref[pl.ds(start, SEG), :], 1.0, 0.0).astype(F32))
            return jnp.concatenate(pieces, axis=0)

        def tap_columns(tap):
            base = edge + (tap - 4) * SEG
            picked = jnp.concatenate(
                [wide[pl.ds(base + g * STRIDE * SEG, SEG), :] for g in range(groups)], axis=0
            )
            return picked * lanes4(tap_mask(tap, 0, groups).astype(BF))

        total = jnp.zeros((count, 128), F32)
        for tap in range(taps):
            total = total + dot_nt(tap_columns(tap), q_ref[tap])
        lane = lax.broadcasted_iota(jnp.int32, (count, 128), 1)
        latent = jnp.where(lane < 8, total + pltpu.roll(total, 112, 1) + shift + bias_ref[...], 0.0)
        lat_ref[...] = latent
        inverse = lax.rsqrt(jnp.sum(latent * latent, axis=1, keepdims=True) + 1.0)
        normed = latent * inverse
        spread = (2.0 * COMMIT) * (normed - c_ref[...])
        row = lax.broadcasted_iota(jnp.int32, (count, 128), 0)
        place = (row & (SEG - 1)) * groups + (row >> 4)
        mine = (place >= HALO // STRIDE) & (place < (HALO + own) // STRIDE)
        dch_ref[...] = jnp.where(mine, o_ref[...] - spread, 0.0)
        dlatent = (spread - normed * jnp.sum(normed * spread, axis=1, keepdims=True)) * inverse

        def split(values):
            high = values.astype(BF).astype(F32)
            return high + pltpu.roll(values - high, 8, 1), pltpu.roll(high, 16, 1)

        dmine = jnp.where(mine, dlatent, 0.0)
        sum_ref[1:2, :] = jnp.concatenate([jnp.sum(dmine, axis=0, keepdims=True)] * 4, axis=1)
        pair, _unused = split(dmine)
        pair = pair.astype(BF)
        for tap in range(taps):
            both = dot_tn(pair, tap_columns(tap))
            m_ref[tap] = both[0:8, :] + both[8:16, :]

        pair, again = split(dlatent)
        codes[pl.ds(8 + SEG, count), :] = pair + again
        codes[pl.ds(8, SEG), :] = codes[pl.ds(8 + count - 1, SEG), :]
        codes[pl.ds(8 + SEG + count, SEG), :] = codes[pl.ds(8 + SEG + 1, SEG), :]
        sums[...] = jnp.zeros_like(sums)
        for rest in range(STRIDE):
            total = None
            for tap in (rest - 4, rest + 4, rest + 12):
                if 0 <= tap < taps:
                    hop = (tap - 4 - rest) // STRIDE
                    left = codes[pl.ds(8 + SEG - hop * SEG, count), :] * tap_mask(tap, -hop, groups)
                    term = dot_nn(left.astype(BF), q_ref[tap])
                    total = term if total is None else total + term
            for g in range(groups):
                here = pl.ds((g * STRIDE + rest) * SEG, SEG)
                part = total[g * SEG : (g + 1) * SEG, :]
                value, slope, by_alpha = snake_parts(s_ref[here, :], v_ref[turn_row : turn_row + 1, :], v_ref[turn_row + 1 : turn_row + 2, :])
                g_ref[here, :] = part * slope
                mask = lanes4(own_mask((g * STRIDE + rest) * SEG, SEG, span, own))
                sums[...] += fold(part * by_alpha * mask)
        sum_ref[0:1, :] = sums[...].sum(axis=0, keepdims=True)
        sum_ref[2:8, :] = jnp.zeros((6, chans), F32)

    whole = pl.BlockSpec(memory_space=pltpu.VMEM)
    return pl.pallas_call(
        kernel,
        out_shape=[
            jax.ShapeDtypeStruct((rows, chans), F32),
            jax.ShapeDtypeStruct((count, 128), F32),
            jax.ShapeDtypeStruct((count, 128), F32),
            jax.ShapeDtypeStruct((taps, 8, chans), F32),
            jax.ShapeDtypeStruct((8, chans), F32),
        ],
        in_specs=[whole] * 8,
        out_specs=[whole] * 5,
        scratch_shapes=[
            pltpu.VMEM((taps, 128, chans), BF),
            pltpu.VMEM((rows + 2 * edge, chans), BF),
            pltpu.VMEM((rows + 16, chans), F32),
            pltpu.VMEM((count + 2 * SEG + 16, 128), F32),
            pltpu.VMEM((8, chans), F32),
        ],
        compiler_params=pltpu.CompilerParams(vmem_limit_bytes=VMEM),
        cost_estimate=cost(11),
        name="bottleneck",
    )(stream, *merged, bias, vecs, labels, chosen, picked_grad)


def swap(value, axis, bit):
    count = lax.axis_size(axis)
    return lax.ppermute(value, axis, [(i, i ^ (1 << bit)) for i in range(count)])


def bits_of(axis):
    count = lax.axis_size(axis)
    return [(axis, bit) for bit in range(count.bit_length() - 1)]


def total_over(value, steps):
    for axis, bit in steps:
        value = value + swap(value, axis, bit)
    return value


def bit_of(axis, bit):
    return (lax.axis_index(axis) >> bit) & 1


def halves_of(value, step):
    axis, bit = step
    half = value.shape[0] // 2
    mine = bit_of(axis, bit)
    kept = lax.dynamic_slice_in_dim(value, mine * half, half)
    return kept, lax.dynamic_slice_in_dim(value, (1 - mine) * half, half).astype(BF)


def add_up(kept, got):
    return (kept.astype(F32) + got.astype(F32)).astype(BF)


def sum_halves(terms_in, rows, step, micros=0.1):
    chans = terms_in[0][0][0].shape[-1]
    flat = [ref for block in terms_in for ref, _ in block]
    half = rows // 2 if step else rows

    def kernel(*refs):
        refs = list(refs)
        ins = [refs.pop(0) for _ in flat]
        outs = refs[: 2 if step else 1]
        total, sems = refs[-2:] if step else (outs[0], None)
        at, start = 0, 0
        for block in terms_in:
            value = None
            for _, index in block:
                ref = ins[at] if index is None else ins[at].at[index]
                term = ref[...].astype(F32)
                value = term if value is None else value + term
                at += 1
            value = value.astype(BF).reshape(-1, chans)
            total[start : start + value.shape[0], :] = value
            start += value.shape[0]
        if start < rows:
            total[start:rows, :] = jnp.zeros((rows - start, chans), BF)
        if step:
            mine = bit_of(*step)
            copies = []
            for n, out in enumerate(outs):
                place = pl.multiple_of((mine if n == 0 else 1 - mine) * half, 16)
                copies.append(pltpu.make_async_copy(total.at[pl.ds(place, half)], out, sems.at[n]))
                copies[-1].start()
            for copy in copies:
                copy.wait()

    def spec(ref, index):
        if index is None:
            return pl.BlockSpec(memory_space=pltpu.VMEM)
        return pl.BlockSpec((1,) + ref.shape[1:], lambda n: (index,) + (0,) * (ref.ndim - 1))

    flat_pairs = [pair for block in terms_in for pair in block]
    terms_in = [[(ref, None if index is None else 0) for ref, index in block] for block in terms_in]
    return pl.pallas_call(
        kernel,
        grid=(1,),
        out_shape=[jax.ShapeDtypeStruct((half, chans), BF)] * (2 if step else 1),
        in_specs=[spec(ref, index) for ref, index in flat_pairs],
        out_specs=[pl.BlockSpec(memory_space=pl.ANY)] * 2 if step else [pl.BlockSpec(memory_space=pltpu.VMEM)],
        scratch_shapes=[pltpu.VMEM((rows, chans), BF), pltpu.SemaphoreType.DMA((2,))] if step else [],
        compiler_params=pltpu.CompilerParams(vmem_limit_bytes=VMEM),
        cost_estimate=cost(micros),
        name="sum_halves",
    )(*flat)


def join(mine, got, step):
    rows, chans = mine.shape

    def kernel(m_ref, g_ref, out_ref):
        upper = bit_of(*step)
        out_ref[pl.ds(pl.multiple_of(upper * rows, 16), rows), :] = m_ref[...]
        out_ref[pl.ds(pl.multiple_of((1 - upper) * rows, 16), rows), :] = g_ref[...]

    whole = pl.BlockSpec(memory_space=pltpu.VMEM)
    return pl.pallas_call(
        kernel,
        out_shape=jax.ShapeDtypeStruct((2 * rows, chans), BF),
        in_specs=[whole] * 2,
        out_specs=whole,
        compiler_params=pltpu.CompilerParams(vmem_limit_bytes=VMEM),
        cost_estimate=cost(0.1),
        name="join",
    )(mine, got)


class Chain:
    def __init__(self, terms_in, rows, steps, micros=0.1):
        self.adds, self.joins = list(steps), list(reversed(steps))
        self.rows = rows
        self.kept, self.sent = sum_halves(terms_in, rows, self.adds[0], micros)
        self.whole = None
        self.left = 2 * len(steps)
        self.start()

    def start(self):
        self.got = swap(self.sent, *(self.adds[0] if self.adds else self.joins[0]))

    def step(self, token):
        got = after(self.got, token)
        self.left -= 1
        if self.adds:
            self.adds.pop(0)
            self.rows //= 2
            terms_in = [[(self.kept, None), (got, None)]]
            if self.adds:
                self.kept, self.sent = sum_halves(terms_in, self.rows, self.adds[0])
            else:
                self.sent = sum_halves(terms_in, self.rows, None)[0]
        elif self.left:
            self.sent = join(self.sent, got, self.joins.pop(0))
        else:
            self.whole = (self.sent, got)
            self.last = self.joins.pop(0)
        if self.left:
            self.start()
        return self.sent

    def upper(self):
        return jnp.where(bit_of(*self.last) == 1, *self.whole)


def after(value, *others):
    return lax.optimization_barrier((value, *others))[0]


def to_peer(value, peer):
    return lax.ppermute(value, "chan", [(i, i ^ peer) for i in range(4)])


def local(
    signal,
    dilated_dirs,
    dilated_gains,
    dilated_bias,
    snake_first,
    snake_second,
    pointwise_dirs,
    pointwise_gains,
    pointwise_bias,
    snake_last,
    strided_dirs,
    strided_gains,
    strided_bias,
    latent_proj,
    latent_bias,
    codebook,
    output_proj,
    output_bias,
    utterances,
    code_index,
    refill_index,
    cotangent,
):
    part, extent = signal.shape
    chans = 4 * part
    own = extent // 4
    frames = code_index.shape[0]
    own_frames = frames // 4
    whole = lax.axis_size("frames") * extent
    units = dilated_dirs.shape[0]
    span = (own + 2 * HALO) // SEG
    span_frames = span // STRIDE
    extra = HALO // STRIDE
    me = lax.axis_index("chan")
    block = lax.axis_index("frames")
    ring = lax.axis_size("frames")
    origin = block * extent + me * own
    over_chan, over_frames = bits_of("chan"), bits_of("frames")

    halves = halve(dilated_dirs, pointwise_dirs)
    far = [swap(halves[0], "chan", 1)]
    close = [swap(after(dilated_dirs, halves[0]), "chan", 0), swap(after(pointwise_dirs, halves[0]), "chan", 0)]

    project = jnp.concatenate(
        [output_proj] + [term[:, None] for term in terms(output_bias, 3)] + [jnp.zeros((output_bias.shape[0], 117), BF)],
        axis=1,
    )
    packed, pulled = vectors(
        after(dilated_dirs, halves[0]), pointwise_dirs, dilated_gains, pointwise_gains, dilated_bias, pointwise_bias,
        snake_first, snake_second, snake_last, project, cotangent,
    )

    pieces, ends = cut(signal, packed, pulled, code_index.reshape(-1, 128))
    pieces = [pieces[0]] + [to_peer(pieces[peer], peer) for peer in (1, 2, 3)]
    ends = [
        lax.ppermute(
            ends[peer],
            ("frames", "chan"),
            [(4 * (f + 1) + (3 ^ peer), 4 * f + 3) for f in range(ring - 1)]
            + [(4 * f + peer, 4 * (f + 1)) for f in range(ring - 1)],
        )
        for peer in range(4)
    ]
    rest = [swap(far[0], "frames", 0)]
    far_close = [swap(far[0], "chan", 0)]
    rest_close = [swap(rest[0], "chan", 0)]
    far.append(swap(after(halves[1], *pieces), "chan", 1))
    far.append(swap(after(halves[2], *pieces), "chan", 1))

    bounds = jnp.cumsum(utterances) * STRIDE
    b_place = jnp.arange(-LEAD, span + LEAD, dtype=jnp.int32)
    spots = (origin - HALO + b_place[:, None] + span * jnp.arange(SEG, dtype=jnp.int32)[None, :]).reshape(-1)
    found = jnp.sum((spots[:, None] >= bounds[None, :]).astype(F32), axis=1)
    found = jnp.where((spots >= 0) & (spots < whole), found, -1.0)
    labels = jnp.broadcast_to(found[:, None], (found.shape[0], 128))

    place = (
        jnp.arange(SEG, dtype=jnp.int32)[None, :] * span_frames + jnp.arange(span_frames, dtype=jnp.int32)[:, None]
    ).reshape(-1)
    owned = (place >= extra) & (place < extra + own_frames)
    place = jnp.where(owned, place - extra + block * frames + me * own_frames, -1)
    place = jnp.broadcast_to(place[:, None], (place.shape[0], 128))
    refill = refill_index.reshape(-1, 512)
    labels, place, refill, project_in, _ = lax.optimization_barrier((labels, place, refill, latent_proj, halves[0]))
    merged, norms = merge_strided(strided_dirs, strided_gains, strided_bias, project_in)
    *held, _, _ = lax.optimization_barrier((*pieces, *ends, far[0], merged))
    stream, vecs, pulled, edge_codes = enter(held[:4], held[4:], packed.shape[0], own)

    def unit(member, stream, *far_pieces):
        pieces = (dilated_dirs, pointwise_dirs, *close, *far_pieces)
        result, middle, wide, weight1 = unit_forward(stream, pieces, member, vecs, labels)
        saved.append((stream, middle, wide, weight1, pieces))
        return result

    saved = []
    stream = unit(0, stream, far[0], rest[0], far_close[0], rest_close[0])
    rest.append(swap(after(far[1], stream), "frames", 0))
    far_close.append(swap(after(far[1], stream), "chan", 0))
    got = swap(after(merged, stream), "chan", 0)

    edge_codes = edge_codes.astype(jnp.int32)
    around = jnp.concatenate([edge_codes[1, 128 - extra :], code_index, edge_codes[0, :extra]])
    near = lax.dynamic_slice_in_dim(around, me * own_frames, own_frames + 2 * extra)
    near = near.reshape(SEG, span_frames).T.reshape(-1)
    wanted = jnp.broadcast_to(jnp.concatenate([near, code_index])[:, None], (near.shape[0] + frames, 128))
    near_rows = wanted[: near.shape[0]]
    pulled = jnp.pad(pulled, ((0, 120), (extra, extra)))
    pulled = pulled.reshape(128, SEG, span_frames).transpose(2, 1, 0).reshape(-1, 128)
    latent_bias = jnp.pad(latent_bias, (0, 128 - latent_bias.shape[0]))[None]
    wanted, near_rows, pulled, latent_bias, _ = lax.optimization_barrier((wanted, near_rows, pulled, latent_bias, stream))
    chosen, output, sums_out = look_up(wanted, codebook, project, cotangent, near.shape[0])
    merged = merged + after(got, chosen)
    got = swap(merged, "chan", 1)
    rest_close.append(swap(after(rest[1], merged), "chan", 0))
    rest.append(swap(after(halves[3], far[2], merged), "chan", 1))
    far_close.append(swap(after(far[2], merged), "chan", 0))
    stream = unit(1, after(stream, chosen), far[1], rest[1], far_close[1], rest_close[1])
    rest_close.append(swap(after(rest[2], stream), "chan", 0))
    stream = unit(2, stream, far[2], rest[2], far_close[2], rest_close[2])
    merged = (merged, after(got, stream))
    grad, latent, dchosen, mixed_grad, last_sums = bottleneck(
        stream, merged, latent_bias, vecs, labels, chosen, pulled, own
    )

    bit0, bit1 = over_chan

    rows = grad.shape[0]

    def weights_of(member, grad=None):
        _, middle, wide, weight1, _ = saved[member]
        return (member, grad, middle, wide, weight1)

    def into_of(member, grad, scaled):
        return (member, grad, saved[member][0], scaled, saved[member][4])

    back2 = units_back(vecs, labels, own, rows, chans, weights=weights_of(2, grad))
    keep2 = back2["keep"]
    near2 = swap(back2["send"], "chan", 0)
    chain_rows = -(-(8 * part + 128) // (16 * ring)) * 16 * ring
    codes = code_payload(dchosen, latent, mixed_grad, near_rows, place, refill, back2["sums_a"])
    codes = [codes[0]] + [to_peer(codes[peer], peer) for peer in (1, 2, 3)]
    near2 = after(near2, codes[0])
    far2 = add_up(keep2[1], near2[1])
    x2 = swap(far2, "chan", 1)
    back1 = units_back(
        vecs, labels, own, rows, chans, into_of(2, after(grad, far2), back2["scaled_out"]), weights_of(1)
    )
    keep1 = back1["keep"]
    near1 = swap(back1["send"], "chan", 0)
    x2, *codes, _ = lax.optimization_barrier((x2, *codes, back1["sums_a"]))
    chain2 = Chain(
        [[(keep2, 0), (near2, 0), (x2, None)], [(piece, None) for piece in codes]], chain_rows, over_frames, 20
    )
    far1 = add_up(keep1[1], after(near1, chain2.sent)[1])
    x1 = swap(far1, "chan", 1)
    back0 = units_back(
        vecs, labels, own, rows, chans,
        into_of(1, after(back1["out"], far1), back1["scaled_out"]), weights_of(0),
    )
    keep0 = back0["keep"]
    near0 = swap(back0["send"], "chan", 0)
    token = chain2.step(back0["sums_a"])
    more = sums_out[:, :16].astype(BF).reshape(-1, chans)
    more = jnp.pad(more, ((0, 16 - more.shape[0]), (0, 0)))
    chain1 = Chain([[(keep1, 0), (near1, 0), (after(x1, token), None)], [(more, None)]], chain_rows, over_frames)
    last = units_back(
        vecs, labels, own, rows, chans, into_of(0, after(back0["out"], chain1.sent), back0["scaled_out"]),
        others=(back0["sums_a"], back0["sums_c"], back1["sums_a"], back1["sums_c"], back2["sums_a"], last_sums),
    )
    grad, small = last["out"], last["sums_c"]

    token = chain2.step(grad)
    token = chain1.step(token)
    far0 = add_up(keep0[1], after(near0, token)[1])
    x0 = swap(far0, "chan", 1)
    small_steps = [bit0] + over_frames + [bit1]
    small_got = swap(small, *small_steps[0])
    outs = leave(after(grad, far0), own)
    sent_outs = [outs[0]] + [to_peer(outs[peer], peer) for peer in (1, 2, 3)]
    token = outs[0]

    def small_step():
        nonlocal small, small_got, token
        small = small + after(small_got, token)
        small_steps.pop(0)
        if small_steps:
            small_got = swap(small, *small_steps[0])
        token = small

    half = len(over_frames)
    while chain2.adds:
        token = chain2.step(token)
    small_step()
    token = chain1.step(token)
    small_step()
    token = chain2.step(token)
    chain0 = Chain([[(keep0, 0), (near0, 0), (after(x0, token), None)]], 8 * part, over_frames)
    token = chain0.sent
    while chain1.left > half:
        token = chain1.step(token)
    while chain2.left > 1:
        token = chain2.step(token)
    token = chain0.step(token)
    while len(small_steps) > 2:
        small_step()
    while chain0.left > half + 1:
        token = chain0.step(token)
    token = chain2.step(token)
    quarter = codes[0].shape[0]
    first = 8 * part - chain_rows // 2
    codes_mine = chain2.upper()[first : first + quarter]
    got_codes = [codes_mine] + [to_peer(codes_mine, peer) for peer in (1, 2, 3)]
    token = chain1.step(token)
    small_step()
    token = chain0.step(token)
    payload = jnp.zeros((4 * quarter, chans), BF)
    for peer in range(4):
        got = after(got_codes[peer], token)
        payload = lax.dynamic_update_slice_in_dim(payload, got, (me ^ peer) * quarter, 0)
    blocks = codebook.shape[1] // 512
    dstrided_dirs, meeting = strided_back(strided_dirs, payload[24 * blocks :].reshape(-1, 8, chans), latent_proj, norms)
    token = chain0.step(dstrided_dirs)
    while chain1.left > 1:
        token = chain1.step(token)
    gains = jnp.stack([dilated_gains, pointwise_gains], axis=1)
    results = norm_back([chain2], after(dilated_dirs, token), pointwise_dirs, gains, (2,), ())
    token = results[0]
    small_step()
    grad_signal = settle(list(lax.optimization_barrier((*sent_outs, token))[:4]))
    token = grad_signal
    while chain0.left > 1:
        token = chain0.step(token)
    token = chain1.step(token)
    results = norm_back([chain1], after(dilated_dirs, token), pointwise_dirs, gains, (1,), results)
    payload = after(payload, results[0])
    codes = codebook.shape[1]
    blocks = codes // 512
    by_code = payload[: 24 * blocks].reshape(blocks, 24, 512).transpose(1, 0, 2).reshape(24, codes).astype(F32)
    dcoded, picked, usage = by_code[0:8], by_code[8:16], by_code[16]
    refreshed = jnp.where(usage[None, :] > 0, codebook, picked)
    coded_scale = lax.rsqrt(jnp.sum(codebook * codebook, axis=0) + 1.0)
    coded = codebook * coded_scale[None, :]
    dcodebook = (dcoded - coded * jnp.sum(coded * dcoded, axis=0)[None, :]) * coded_scale[None, :]

    token = lax.optimization_barrier((token, refreshed, dcodebook))[0]
    chain0.step(token)
    results = norm_back([chain0], dilated_dirs, pointwise_dirs, gains, (0,), results)
    sums_out = chain1.upper()[first : first + output_bias.shape[0] * 16 // chans].astype(F32).reshape(-1, 16)
    mine_small = lax.dynamic_slice_in_dim(small, me * part, part, axis=1)
    dbias_latent = small[6 * 8 + 1, :8]
    dbias1, dbias7, dalpha2 = mine_small[8:48:16], mine_small[9:48:16], mine_small[10:48:16]
    dalpha1 = mine_small[0:48:16]
    dalpha_last = mine_small[6 * 8]
    dproj_latent = meeting[0:8] + dbias_latent[:, None] * strided_bias[None, :]
    dbias_strided = jnp.sum(latent_proj.astype(F32) * dbias_latent[:, None], axis=0)
    return (
        output,
        grad_signal,
        results[0],
        results[2][:, 0],
        dbias7,
        dalpha1,
        dalpha2,
        results[1],
        results[2][:, 1],
        dbias1,
        dalpha_last,
        dstrided_dirs,
        meeting[8],
        dbias_strided,
        dproj_latent,
        dbias_latent,
        dcodebook,
        sums_out[:, :8],
        sums_out[:, 8],
        refreshed,
    )


def solution(mesh):
    in_specs = (
        P("chan", "frames"),
        P(None, None, "chan", None),
        P(None, "chan"),
        P(None, "chan"),
        P(None, "chan"),
        P(None, "chan"),
        P(None, "chan", None),
        P(None, "chan"),
        P(None, "chan"),
        P("chan"),
        P(None, "chan", None),
        P("chan"),
        P("chan"),
        P(None, "chan"),
        P(),
        P(),
        P("chan", None),
        P("chan"),
        P(),
        P("frames"),
        P(),
        P("chan", "frames"),
    )
    out_specs = (
        P("chan", "frames"),
        P("chan", "frames"),
        P(None, None, "chan", None),
        P(None, "chan"),
        P(None, "chan"),
        P(None, "chan"),
        P(None, "chan"),
        P(None, "chan", None),
        P(None, "chan"),
        P(None, "chan"),
        P("chan"),
        P(None, "chan", None),
        P("chan"),
        P("chan"),
        P(None, "chan"),
        P(),
        P(),
        P("chan", None),
        P("chan"),
        P(),
    )
    return jax.shard_map(local, mesh=mesh, in_specs=in_specs, out_specs=out_specs, check_vma=False)
```

```python
import jax
import jax.numpy as jnp
from jax import lax
from jax.experimental import pallas as pl
from jax.experimental.pallas import tpu as pltpu
from jax.sharding import PartitionSpec as P

CODES = 8192
STRIDE = 8
NORM_EPS = 1e-06
COMMIT = 4.0

BF = jnp.bfloat16
F32 = jnp.float32

SEG = 16
HALO = 128
LEAD = 28
CHUNK = 256
VMEM = 60 * 2**20
def cost(micros):
    return pl.CostEstimate(flops=int(micros * 1.15e9), bytes_accessed=0, transcendentals=0)

SIN = (3.1415902692655564, -5.1674066428989045, 2.5440093135845245, -0.5594585999205443)
COS = (0.9999999532244686, -4.934792826917481, 4.0584112640152465, -1.331875904720673, 0.21968809492172123)


def by_powers(square, factors):
    total = factors[-1]
    for factor in factors[-2::-1]:
        total = factor + square * total
    return total


def snake(value, turn, inverse):
    angle = turn * value
    angle = angle - jnp.round(angle)
    square = angle * angle
    part = by_powers(square, SIN)
    return value + (square * part) * (part * inverse)


def snake_parts(value, turn, inverse):
    angle = turn * value
    angle = angle - jnp.round(angle)
    square = angle * angle
    part = by_powers(square, SIN)
    sine2 = (square * part) * (part * inverse)
    double = (angle * part) * (2.0 * by_powers(square, COS))
    return value + sine2, 1.0 + double, (value * double - sine2) * inverse


def terms(value, count):
    parts = []
    for _ in range(count):
        part = value.astype(BF)
        parts.append(part)
        value = value - part.astype(F32)
    return parts


def lanes4(mask):
    return jnp.concatenate([mask] * 4, axis=1)


def own_mask(start, count, span, own):
    row = lax.broadcasted_iota(jnp.int32, (count, 128), 0) + start
    place = (row & (SEG - 1)) * span + (row >> 4)
    return jnp.where((place >= HALO) & (place < HALO + own), 1.0, 0.0).astype(F32)


def fold(values):
    rows, cols = values.shape
    return values.reshape(rows // 8, 8, cols).sum(axis=0)


def load_weights(pieces, member, weights, sems):
    me = lax.axis_index("chan")
    own7, own1, near7, near1 = (piece.at[member] for piece in pieces[:4])
    rows = own1.shape[0]

    def place(peer):
        return pl.ds(pl.multiple_of((me ^ peer) * rows, rows), rows)

    moves = [
        (own7, weights.at[pl.ds(0, 7), place(0), :]),
        (own1, weights.at[7, place(0), :]),
        (near7, weights.at[pl.ds(0, 7), place(1), :]),
        (near1, weights.at[7, place(1), :]),
    ]
    size = pieces[4].shape[0]
    side = 0 if member == 2 else lax.axis_index("frames") & 1
    first, second = side * (8 - size), (1 - side) * size
    moves += [
        (pieces[4], weights.at[pl.ds(first, size), place(2), :]),
        (pieces[5], weights.at[pl.ds(second, 8 - size), place(2), :]),
        (pieces[6], weights.at[pl.ds(first, size), place(3), :]),
        (pieces[7], weights.at[pl.ds(second, 8 - size), place(3), :]),
    ]
    copies = []
    for piece, target in moves:
        copy = pltpu.make_async_copy(piece, target, sems.at[len(copies)])
        copy.start()
        copies.append(copy)
    return copies


def fill_masks(mask, labels, spacing, rows):
    base = LEAD * SEG
    here = labels[pl.ds(base, rows), :]
    for tap in range(7):
        there = labels[pl.ds(base + (tap - 3) * spacing * SEG, rows), :]
        mask[tap] = jnp.where(there == here, 1.0, 0.0).astype(BF)


def fill_ends(wide, turn, margin, rows):
    edge = margin * SEG
    turn[pl.ds(8, edge + SEG), :] = wide[pl.ds(rows - SEG, edge + SEG), :].astype(F32)
    wide[pl.ds(0, edge), :] = turn[pl.ds(8 + SEG - 1, edge), :].astype(BF)
    turn[pl.ds(8, edge + SEG), :] = wide[pl.ds(edge, edge + SEG), :].astype(F32)
    wide[pl.ds(edge + rows, edge), :] = turn[pl.ds(8 + 1, edge), :].astype(BF)


class Stream:
    def __init__(self, source, target, sems):
        self.source, self.target, self.sems = source, target, sems

    def copy(self, chunk):
        here = pl.ds(chunk * CHUNK, CHUNK)
        return pltpu.make_async_copy(self.source.at[here], self.target.at[here], self.sems.at[chunk])

    def start(self, chunk):
        self.copy(chunk).start()

    def wait(self, chunk):
        self.copy(chunk).wait()


def dot_nt(left, right):
    return lax.dot_general(left, right, (((1,), (1,)), ((), ())), preferred_element_type=F32)


def dot_nn(left, right):
    return lax.dot_general(left, right, (((1,), (0,)), ((), ())), preferred_element_type=F32)


def dot_tn(left, right):
    return lax.dot_general(left, right, (((0,), (0,)), ((), ())), preferred_element_type=F32)


A1, I1, A2, I2, S7, B7, S1, B1 = range(8)


def unit_forward(stream, pieces, member, vecs, labels):
    spacing = 3**member
    rows, chans = stream.shape
    margin = 3 * spacing
    chunks = rows // CHUNK
    wide_rows = rows + 2 * margin * SEG

    def kernel(s_ref, *refs):
        parts, refs = refs[: len(pieces)], refs[len(pieces) :]
        (
            v_ref, l_ref, out_ref, mid_ref, wide_ref, w1_ref,
            weights, wide, turn, mask, stream_in, result, middle, total0, total1, sems, s_sems, o_sems, m_sems, end_sems,
        ) = refs
        v_ref = v_ref.at[pl.ds(8 * member, 8)]
        incoming = Stream(s_ref, stream_in, s_sems)
        outgoing, outgoing_mid = Stream(result, out_ref, o_sems), Stream(middle, mid_ref, m_sems)
        for chunk in range(chunks):
            incoming.start(chunk)
        copies = load_weights(parts, member, weights, sems)
        fill_masks(mask, l_ref, spacing, rows)
        for chunk in range(chunks):
            incoming.wait(chunk)
            here = pl.ds(chunk * CHUNK, CHUNK)
            act = snake(stream_in[here, :], v_ref[A1 : A1 + 1, :], v_ref[I1 : I1 + 1, :])
            wide[pl.ds(margin * SEG + chunk * CHUNK, CHUNK), :] = act.astype(BF)
        fill_ends(wide, turn, margin, rows)
        keep_wide = pltpu.make_async_copy(wide, wide_ref, end_sems.at[0])
        keep_wide.start()
        for copy in copies:
            copy.wait()
        keep_w1 = pltpu.make_async_copy(weights.at[7], w1_ref, end_sems.at[1])
        keep_w1.start()

        def convolve(chunk, total_ref):
            total = None
            for tap in range(7):
                columns = wide[pl.ds(chunk * CHUNK + tap * spacing * SEG, CHUNK), :]
                if tap != 3:
                    columns = columns * lanes4(mask[tap, pl.ds(chunk * CHUNK, CHUNK), :])
                term = dot_nt(columns, weights[tap])
                total = term if total is None else total + term
            total_ref[...] = total

        def finish(chunk, total_ref):
            here = pl.ds(chunk * CHUNK, CHUNK)
            value = total_ref[...] * v_ref[S7 : S7 + 1, :] + v_ref[B7 : B7 + 1, :]
            middle[here, :] = value
            second = snake(value, v_ref[A2 : A2 + 1, :], v_ref[I2 : I2 + 1, :]).astype(BF)
            term = dot_nt(second, weights[7])
            result[here, :] = stream_in[here, :] + term * v_ref[S1 : S1 + 1, :] + v_ref[B1 : B1 + 1, :]

        totals = (total0, total1)
        convolve(0, totals[0])
        for chunk in range(chunks):
            if chunk + 1 < chunks:
                convolve(chunk + 1, totals[(chunk + 1) % 2])
            finish(chunk, totals[chunk % 2])
            outgoing_mid.start(chunk)
            outgoing.start(chunk)
        keep_wide.wait()
        keep_w1.wait()
        for chunk in range(chunks):
            outgoing_mid.wait(chunk)
            outgoing.wait(chunk)

    whole = pl.BlockSpec(memory_space=pltpu.VMEM)
    held = pl.BlockSpec(memory_space=pl.ANY)
    return pl.pallas_call(
        kernel,
        out_shape=[
            jax.ShapeDtypeStruct((rows, chans), F32),
            jax.ShapeDtypeStruct((rows, chans), F32),
            jax.ShapeDtypeStruct((wide_rows, chans), BF),
            jax.ShapeDtypeStruct((chans, chans), BF),
        ],
        in_specs=[held] * (1 + len(pieces)) + [whole] * 2,
        out_specs=[held] * 4,
        scratch_shapes=[
            pltpu.VMEM((8, chans, chans), BF),
            pltpu.VMEM((wide_rows, chans), BF),
            pltpu.VMEM((margin * SEG + SEG + 16, chans), F32),
            pltpu.VMEM((7, rows, 128), BF),
            pltpu.VMEM((rows, chans), F32),
            pltpu.VMEM((rows, chans), F32),
            pltpu.VMEM((rows, chans), F32),
            pltpu.VMEM((CHUNK, chans), F32),
            pltpu.VMEM((CHUNK, chans), F32),
            pltpu.SemaphoreType.DMA((8,)),
            pltpu.SemaphoreType.DMA((chunks,)),
            pltpu.SemaphoreType.DMA((chunks,)),
            pltpu.SemaphoreType.DMA((chunks,)),
            pltpu.SemaphoreType.DMA((2,)),
        ],
        compiler_params=pltpu.CompilerParams(vmem_limit_bytes=VMEM),
        cost_estimate=cost(12),
        name=f"unit_forward_{spacing}",
    )(stream, *pieces, vecs, labels)


class Names:
    def __init__(self, names, refs):
        self.__dict__.update(zip(names, refs, strict=True))


def units_back(vecs, labels, own, rows, chans, into=None, weights=None, others=()):
    span = rows // SEG
    part = chans // 4
    chunks = rows // CHUNK
    held, whole = pl.BlockSpec(memory_space=pl.ANY), pl.BlockSpec(memory_space=pltpu.VMEM)
    f32_rows, bf_rows = jax.ShapeDtypeStruct((rows, chans), F32), jax.ShapeDtypeStruct((rows, chans), BF)
    ins, outs, scratch = {"labels": (labels, whole), "vecs": (vecs, whole)}, {}, {"mask": pltpu.VMEM((7, rows, 128), BF)}
    name, micros = "units_back", 20
    if into is not None:
        member_c, grad, stream, scaled, pieces = into
        spacing_c = 3**member_c
        margin_c = 3 * spacing_c
        name, micros = f"{name}_into_{spacing_c}", micros + 30
        ins |= {"grad": (grad, held), "stream": (stream, held), "scaled": (scaled, held)}
        ins |= {f"piece{n}": (piece, held) for n, piece in enumerate(pieces)}
        ins |= {f"other{n}": (other, whole) for n, (other, _) in enumerate(others)}
        outs |= {"out": (f32_rows, held), "sums_c": (jax.ShapeDtypeStruct((16 if others else 8, chans), F32), whole)}
        scratch |= {
            "weights": pltpu.VMEM((8, chans, chans), BF),
            "wide_c": pltpu.VMEM((rows + 2 * margin_c * SEG, chans), BF),
            "turn": pltpu.VMEM((margin_c * SEG + SEG + 16, chans), F32),
            "total_c": pltpu.VMEM((8, chans), F32),
            "stream_in": pltpu.VMEM((rows, chans), F32),
            "result": pltpu.VMEM((rows, chans), F32),
            "back": pltpu.VMEM((rows, chans), F32),
            "w_sems": pltpu.SemaphoreType.DMA((8,)),
            "s_sems": pltpu.SemaphoreType.DMA((chunks,)),
            "o_sems": pltpu.SemaphoreType.DMA((chunks,)),
            "d_sem": pltpu.SemaphoreType.DMA((1,)),
        }
    else:
        ins["grad"] = (weights[1], held)
    scratch |= {"grad_in": pltpu.VMEM((rows, chans), F32), "g_sems": pltpu.SemaphoreType.DMA((chunks,))}
    if weights is not None:
        member_a, _, middle, wide_act, weight1 = weights
        spacing_a = 3**member_a
        name, micros = f"{name}_weights_{spacing_a}", micros + 14
        ins |= {"middle": (middle, held), "wide": (wide_act, held), "w1": (weight1, whole)}
        outs |= {
            "scaled_out": (bf_rows, held),
            "keep": (jax.ShapeDtypeStruct((2, 8, part, chans), BF), held),
            "send": (jax.ShapeDtypeStruct((2, 8, part, chans), BF), held),
            "sums_a": (jax.ShapeDtypeStruct((8, chans), F32), whole),
        }
        scratch |= {
            "middle_in": pltpu.VMEM((rows, chans), F32),
            "wide_a": pltpu.VMEM(wide_act.shape, BF),
            "scaled_a": pltpu.VMEM((rows, chans), BF),
            "low_t": pltpu.VMEM((chans, rows), BF),
            "mid_t": pltpu.VMEM((chans, rows), BF),
            "second": pltpu.VMEM((rows, chans), BF),
            "results": pltpu.VMEM((8, chans, chans), BF),
            "total_a": pltpu.VMEM((3, 8, chans), F32),
            "m_sems": pltpu.SemaphoreType.DMA((chunks,)),
            "x_sem": pltpu.SemaphoreType.DMA((1,)),
            "a_sems": pltpu.SemaphoreType.DMA((chunks,)),
            "r_sems": pltpu.SemaphoreType.DMA((8, 4)),
        }

    def go_into(r):
        get_scaled = pltpu.make_async_copy(r.scaled, r.wide_c.at[pl.ds(margin_c * SEG, rows)], r.d_sem.at[0])
        get_scaled.start()
        parts = [getattr(r, f"piece{n}") for n in range(len(pieces))]
        copies = load_weights(parts, member_c, r.weights, r.w_sems)
        incoming_grad, incoming = Stream(r.grad, r.grad_in, r.g_sems), Stream(r.stream, r.stream_in, r.s_sems)
        outgoing = Stream(r.result, r.out, r.o_sems)
        fill_masks(r.mask, r.labels, spacing_c, rows)
        r.total_c[...] = jnp.zeros_like(r.total_c)
        get_scaled.wait()
        fill_ends(r.wide_c, r.turn, margin_c, rows)
        for copy in copies:
            copy.wait()
        for chunk in range(chunks):
            incoming.start(chunk)
            incoming_grad.start(chunk)
        if weights is not None:
            start_weights(r)
        for chunk in range(chunks):
            total = None
            for tap in range(7):
                columns = r.wide_c[pl.ds(chunk * CHUNK + (6 - tap) * spacing_c * SEG, CHUNK), :]
                if tap != 3:
                    columns = columns * lanes4(r.mask[6 - tap, pl.ds(chunk * CHUNK, CHUNK), :])
                term = dot_nn(columns, r.weights[tap])
                total = term if total is None else total + term
            r.back[pl.ds(chunk * CHUNK, CHUNK), :] = total

        @pl.loop(0, chunks)
        def _(chunk):
            incoming.wait(chunk)
            incoming_grad.wait(chunk)
            here = pl.ds(chunk * CHUNK, CHUNK)
            total = r.back[here, :]
            mine = lanes4(own_mask(chunk * CHUNK, CHUNK, span, own))
            _, slope, by_alpha = snake_parts(r.stream_in[here, :], r.vec_c[A1 : A1 + 1, :], r.vec_c[I1 : I1 + 1, :])
            r.total_c[...] += fold(total * by_alpha * mine)
            r.result[here, :] = r.grad_in[here, :] + total * slope
            outgoing.start(chunk)

        r.sums_c[0:8, :] = jnp.concatenate(
            [r.total_c[...].sum(axis=0, keepdims=True), jnp.zeros((7, chans), F32)], axis=0
        )
        start = 1
        for n, (_, count) in enumerate(others):
            r.sums_c[start : start + count, :] = getattr(r, f"other{n}")[0:count, :]
            start += count
        if others:
            r.sums_c[start:16, :] = jnp.zeros((16 - start, chans), F32)
        return outgoing

    def start_weights(r):
        incoming_mid = Stream(r.middle, r.middle_in, r.m_sems)
        for chunk in range(chunks):
            incoming_mid.start(chunk)
        pltpu.make_async_copy(r.wide, r.wide_a, r.x_sem.at[0]).start()

    def go_weights(r):
        me = lax.axis_index("chan")
        incoming, incoming_mid = Stream(r.grad, r.grad_in, r.g_sems), Stream(r.middle, r.middle_in, r.m_sems)
        outgoing = Stream(r.scaled_a, r.scaled_out, r.a_sems)
        grads = r.grad_in if into is None else r.result
        fill_masks(r.mask, r.labels, spacing_a, rows)
        r.total_a[...] = jnp.zeros_like(r.total_a)
        for chunk in range(chunks):
            if into is None:
                incoming.wait(chunk)
            incoming_mid.wait(chunk)
            here = pl.ds(chunk * CHUNK, CHUNK)
            mine = lanes4(own_mask(chunk * CHUNK, CHUNK, span, own))
            grad_here = grads[here, :]
            scaled_here = grad_here * r.vec_a[S1 : S1 + 1, :]
            r.low_t[:, here] = (scaled_here * mine).astype(BF).T
            back = dot_nn(scaled_here.astype(BF), r.w1[...])
            value, slope, by_alpha = snake_parts(
                r.middle_in[here, :], r.vec_a[A2 : A2 + 1, :], r.vec_a[I2 : I2 + 1, :]
            )
            r.second[here, :] = value.astype(BF)
            dmiddle = back * slope
            mine_mid = dmiddle * mine
            r.total_a[0] += fold(grad_here * mine)
            r.total_a[1] += fold(mine_mid)
            r.total_a[2] += fold(back * by_alpha * mine)
            r.scaled_a[here, :] = (dmiddle * r.vec_a[S7 : S7 + 1, :]).astype(BF)
            outgoing.start(chunk)
            r.mid_t[:, here] = (mine_mid * r.vec_a[S7 : S7 + 1, :]).astype(BF).T

        r.sums_a[...] = jnp.concatenate(
            [r.total_a[i].sum(axis=0, keepdims=True) for i in range(3)] + [jnp.zeros((5, chans), F32)], axis=0
        )
        r.results[7] = dot_nn(r.low_t[...], r.second[...]).astype(BF)
        pltpu.make_async_copy(r.wide, r.wide_a, r.x_sem.at[0]).wait()
        targets = (r.keep.at[0], r.send.at[0], r.keep.at[1], r.send.at[1])

        def out(tap, p):
            slot = pl.multiple_of((me ^ p) * part, part)
            return pltpu.make_async_copy(
                r.results.at[tap, pl.ds(slot, part), :], targets[p].at[tap], r.r_sems.at[tap, p]
            )

        for p in range(4):
            out(7, p).start()
        for tap in range(7):
            columns = r.wide_a[pl.ds(tap * (spacing_a * SEG), rows), :]
            if tap != 3:
                columns = columns * lanes4(r.mask[tap])
            r.results[tap] = dot_nn(r.mid_t[...], columns).astype(BF)
            for p in range(4):
                out(tap, p).start()
        for tap in range(8):
            for p in range(4):
                out(tap, p).wait()
        for chunk in range(chunks):
            outgoing.wait(chunk)

    def kernel(*refs):
        r = Names([*ins, *outs, *scratch], refs)
        if into is not None:
            r.vec_c = r.vecs.at[pl.ds(8 * member_c, 8)]
        if weights is not None:
            r.vec_a = r.vecs.at[pl.ds(8 * member_a, 8)]
        outgoing = None
        if into is None:
            incoming = Stream(r.grad, r.grad_in, r.g_sems)
            for chunk in range(chunks):
                incoming.start(chunk)
            start_weights(r)
        else:
            outgoing = go_into(r)
        if weights is not None:
            go_weights(r)
        if outgoing is not None:
            for chunk in range(chunks):
                outgoing.wait(chunk)

    results = pl.pallas_call(
        kernel,
        out_shape=[shape for shape, _ in outs.values()],
        in_specs=[spec for _, spec in ins.values()],
        out_specs=[spec for _, spec in outs.values()],
        scratch_shapes=list(scratch.values()),
        compiler_params=pltpu.CompilerParams(vmem_limit_bytes=VMEM),
        cost_estimate=cost(micros),
        name=name,
    )(*[value for value, _ in ins.values()])
    return dict(zip(outs, results, strict=True))


def halve(dilated, pointwise):
    units, _, part, chans = dilated.shape

    def kernel(d_ref, q_ref, f0, f1, f2, f3, held, sems, out_sems):
        side = lax.axis_index("frames") & 1
        copies = []
        for u in range(units):
            copies.append(pltpu.make_async_copy(d_ref.at[u], held.at[u, pl.ds(0, 7)], sems.at[u]))
            copies.append(pltpu.make_async_copy(q_ref.at[u], held.at[u, 7], sems.at[units + u]))
        for copy in copies:
            copy.start()
        outs = [
            pltpu.make_async_copy(held.at[0, pl.ds(side * 4, 4)], f0, out_sems.at[0]),
            pltpu.make_async_copy(held.at[1, pl.ds(side * 4, 4)], f1, out_sems.at[1]),
            pltpu.make_async_copy(held.at[2, pl.ds(0, 4)], f2, out_sems.at[2]),
            pltpu.make_async_copy(held.at[2, pl.ds(4, 4)], f3, out_sems.at[3]),
        ]
        for u, out in zip((0, 1, 2, 2), outs, strict=True):
            if u == 2 and out is outs[3]:
                out.start()
                continue
            copies[2 * u].wait()
            copies[2 * u + 1].wait()
            out.start()
        for out in outs:
            out.wait()

    held = pl.BlockSpec(memory_space=pl.ANY)
    return pl.pallas_call(
        kernel,
        out_shape=[
            jax.ShapeDtypeStruct((taps, part, chans), BF) for taps in (4, 4, 4, 4)
        ],
        in_specs=[held] * 2,
        out_specs=[held] * 4,
        scratch_shapes=[
            pltpu.VMEM((units, 8, part, chans), BF),
            pltpu.SemaphoreType.DMA((2 * units,)),
            pltpu.SemaphoreType.DMA((units + 1,)),
        ],
        compiler_params=pltpu.CompilerParams(vmem_limit_bytes=VMEM),
        cost_estimate=cost(0.1),
        name="halve",
    )(dilated, pointwise)


def cut(signal, packed, pulled, codes):
    part, extent = signal.shape
    own = extent // 4
    count = own + 2 * HALO
    own_frames = pulled.shape[1] // 4

    def kernel(s_ref, v_ref, u_ref, c_ref, p0, p1, p2, p3, e0, e1, e2, e3, low):
        me = lax.axis_index("chan")
        low[...] = s_ref[...].astype(BF)
        vectors3 = terms(v_ref[...], 3)
        for p, (piece, end) in enumerate(((p0, e0), (p1, e1), (p2, e2), (p3, e3))):
            owner = me ^ p
            start = pl.multiple_of(owner * own, own)
            piece[:, HALO : HALO + own] = low[:, pl.ds(start, own)]
            before = pl.multiple_of(jnp.maximum(start - HALO, 0), HALO)
            piece[:, 0:HALO] = low[:, pl.ds(before, HALO)]
            behind = pl.multiple_of(jnp.minimum(start + own, extent - HALO), HALO)
            piece[:, HALO + own : count] = low[:, pl.ds(behind, HALO)]
            frames = pl.ds(pl.multiple_of(owner * own_frames, own_frames), own_frames)
            pulled2 = jnp.concatenate([u_ref[:, frames], jnp.zeros((8, own_frames), F32)], axis=0)
            high = pulled2.astype(BF).astype(F32)
            both = jnp.concatenate([high[0:8], (pulled2 - high)[0:8]], axis=0).astype(BF)
            piece[:, count : count + 128] = jnp.concatenate(
                [*vectors3, both, jnp.zeros((128 - 3 * packed.shape[0] - 16, 128), BF)], axis=0
            )
            outer = pl.multiple_of(jnp.where(owner == 0, extent - HALO, 0), HALO)
            end[0:part, :] = low[:, pl.ds(outer, HALO)]
        first, last = c_ref[0:1, :], c_ref[codes.shape[0] - 1 : codes.shape[0], :]
        e0[part : part + 16, :] = jnp.concatenate(
            [row.astype(F32) for row in (first >> 7, first & 127, last >> 7, last & 127)] + [jnp.zeros((12, 128), F32)],
            axis=0,
        ).astype(BF)

    whole = pl.BlockSpec(memory_space=pltpu.VMEM)
    outs = pl.pallas_call(
        kernel,
        out_shape=[jax.ShapeDtypeStruct((part, count + 128), BF)] * 4
        + [jax.ShapeDtypeStruct((part + 16, HALO), BF)]
        + [jax.ShapeDtypeStruct((part, HALO), BF)] * 3,
        in_specs=[whole] * 4,
        out_specs=[whole] * 8,
        scratch_shapes=[pltpu.VMEM((part, extent), BF)],
        compiler_params=pltpu.CompilerParams(vmem_limit_bytes=VMEM),
        cost_estimate=cost(0.1),
        name="cut",
    )(signal, packed, pulled, codes)
    return outs[0:4], outs[4:8]


def enter(pieces, ends, lines, own):
    part = pieces[0].shape[0]
    count = own + 2 * HALO
    span = count // SEG

    def kernel(p0, p1, p2, p3, e0, e1, e2, e3, out_ref, vec_ref, pull_ref, code_ref, turned, placed):
        me = lax.axis_index("chan")
        pulled = jnp.zeros((8, part), F32)
        for p, (piece, end) in enumerate(((p0, e0), (p1, e1), (p2, e2), (p3, e3))):
            turned[...] = piece[:, 0:count].astype(F32).T

            @pl.when(me == 0)
            def _(end=end):
                turned[0:HALO, :] = end[0:part, :].astype(F32).T

            @pl.when(me == 3)
            def _(end=end):
                turned[HALO + own : count, :] = end[0:part, :].astype(F32).T

            for a in range(SEG):
                placed[pl.ds(a, span, stride=SEG), :] = turned[pl.ds(a * span, span), :]
            lanes = pl.ds(pl.multiple_of((me ^ p) * part, part), part)
            out_ref[:, lanes] = placed[...]
            tile = piece[:, count : count + 128].astype(F32)
            vec_ref[:, lanes] = tile[0:lines] + tile[lines : 2 * lines] + tile[2 * lines : 3 * lines]
            pulled = pulled + tile[3 * lines : 3 * lines + 8] + tile[3 * lines + 8 : 3 * lines + 16]
        pull_ref[...] = pulled
        tile = e0[part : part + 16, :].astype(F32)
        code_ref[...] = jnp.concatenate(
            [tile[0:1] * 128.0 + tile[1:2], tile[2:3] * 128.0 + tile[3:4], jnp.zeros((6, 128), F32)], axis=0
        )

    whole = pl.BlockSpec(memory_space=pltpu.VMEM)
    return pl.pallas_call(
        kernel,
        out_shape=[
            jax.ShapeDtypeStruct((count, 4 * part), F32),
            jax.ShapeDtypeStruct((lines, 4 * part), F32),
            jax.ShapeDtypeStruct((8, part), F32),
            jax.ShapeDtypeStruct((8, 128), F32),
        ],
        in_specs=[whole] * 8,
        out_specs=[whole] * 4,
        scratch_shapes=[pltpu.VMEM((count, part), F32)] * 2,
        compiler_params=pltpu.CompilerParams(vmem_limit_bytes=VMEM),
        cost_estimate=cost(0.1),
        name="enter",
    )(*pieces, *ends)


def lane_sums(squares):
    return jnp.sum(squares.T, axis=0, keepdims=True)


def vectors(dilated, pointwise, gains7, gains1, bias7, bias1, first, second, last, project, cotangent):
    units, taps, part, chans = dilated.shape

    def kernel(d_ref, q_ref, g7, g1, b7, b1, a1, a2, a3, p_ref, t_ref, out_ref, pulled):
        out_ref[...] = jnp.zeros_like(out_ref)
        for u in range(units):
            total = jnp.zeros((part, 128), F32)
            for tap in range(taps):
                value = d_ref[u, tap].astype(F32)
                value = value * value
                for g in range(chans // 128):
                    total = total + value[:, g * 128 : (g + 1) * 128]
            value = q_ref[u].astype(F32)
            value = value * value
            total1 = jnp.zeros((part, 128), F32)
            for g in range(chans // 128):
                total1 = total1 + value[:, g * 128 : (g + 1) * 128]
            here = slice(u, u + 1)
            rows = (
                a1[here, :] * (1.0 / jnp.pi),
                1.0 / a1[here, :],
                a2[here, :] * (1.0 / jnp.pi),
                1.0 / a2[here, :],
                g7[here, :] * lax.rsqrt(lane_sums(total) + NORM_EPS),
                b7[here, :],
                g1[here, :] * lax.rsqrt(lane_sums(total1) + NORM_EPS),
                b1[here, :],
            )
            for n, row in enumerate(rows):
                out_ref[8 * u + n : 8 * u + n + 1, :] = row
        out_ref[8 * units : 8 * units + 1, :] = a3[...] * (1.0 / jnp.pi)
        out_ref[8 * units + 1 : 8 * units + 2, :] = 1.0 / a3[...]
        pulled[...] = dot_tn(p_ref[...], t_ref[...])[0:8, :]

    whole = pl.BlockSpec(memory_space=pltpu.VMEM)
    return pl.pallas_call(
        kernel,
        out_shape=[
            jax.ShapeDtypeStruct((8 * units + 8, part), F32),
            jax.ShapeDtypeStruct((8, cotangent.shape[1]), F32),
        ],
        in_specs=[whole] * 11,
        out_specs=[whole] * 2,
        compiler_params=pltpu.CompilerParams(vmem_limit_bytes=VMEM),
        cost_estimate=cost(0.1),
        name="vectors",
    )(dilated, pointwise, gains7, gains1, bias7, bias1, first, second, last[None], project, cotangent)


def merge_strided(strided, gains, bias, project):
    taps, rows, chans = strided.shape

    def kernel(w_ref, g_ref, b_ref, p_ref, out_ref, norm_ref):
        total = jnp.zeros((rows, 128), F32)
        for tap in range(taps):
            value = w_ref[tap].astype(F32)
            value = value * value
            for g in range(chans // 128):
                total = total + value[:, g * 128 : (g + 1) * 128]
        inverse = lax.rsqrt(lane_sums(total) + NORM_EPS)
        scale = g_ref[...] * inverse
        norm_ref[...] = jnp.zeros_like(norm_ref)
        norm_ref[0:1, :] = scale
        norm_ref[1:2, :] = scale * inverse * inverse
        norm_ref[2:3, :] = inverse
        plain = p_ref[...].astype(F32)
        scaled = plain * scale
        split = jnp.concatenate(terms(scaled, 3), axis=0)
        for tap in range(taps):
            three = dot_nn(split, w_ref[tap])
            out_ref[8 * tap : 8 * tap + 8, :] = three[0:8] + three[8:16] + three[16:24]
        shift = jnp.sum(plain * b_ref[...], axis=1, keepdims=True)
        out_ref[8 * taps : 8 * taps + 8, :] = jnp.broadcast_to(shift, (8, chans))

    whole = pl.BlockSpec(memory_space=pltpu.VMEM)
    return pl.pallas_call(
        kernel,
        out_shape=[jax.ShapeDtypeStruct((8 * taps + 8, chans), F32), jax.ShapeDtypeStruct((8, rows), F32)],
        in_specs=[whole] * 4,
        out_specs=[whole] * 2,
        compiler_params=pltpu.CompilerParams(vmem_limit_bytes=VMEM),
        cost_estimate=cost(5),
        name="merge_strided",
    )(strided, gains[None], bias[None], project)


def look_up(wanted, codebook, project, cotangent, near_count):
    count = wanted.shape[0]
    codes = codebook.shape[1]
    rows, frames = cotangent.shape
    step = 512

    def kernel(i_ref, c_ref, p_ref, t_ref, near_ref, out_ref, sum_ref, found):
        found[...] = jnp.zeros_like(found)
        lane = lax.broadcasted_iota(jnp.int32, (count, 128), 1)

        @pl.loop(0, codes, step=step)
        def _(start):
            start = pl.multiple_of(start, step)
            book = c_ref[:, pl.ds(start, step)]
            book = book * lax.rsqrt(jnp.sum(book * book, axis=0, keepdims=True) + 1.0)
            table = jnp.concatenate(terms(book, 3) + [jnp.zeros((104, step), BF)], axis=0)
            wants = i_ref[...] - start
            hot = jnp.concatenate(
                [jnp.where(wants == lane + g * 128, 1.0, 0.0).astype(BF) for g in range(step // 128)], axis=1
            )
            found[...] += dot_nt(hot, table)

        total = found[...]
        total = total + pltpu.roll(total, 120, 1) + pltpu.roll(total, 112, 1)
        total = jnp.where(lane < 8, total, 0.0)
        near_ref[...] = total[:near_count]
        low = jnp.where((lane >= 8) & (lane < 11), 1.0, total)[near_count:].astype(BF)
        out_ref[...] = dot_nt(p_ref[...], low)
        sum_ref[...] = dot_nn(t_ref[...], low)

    whole = pl.BlockSpec(memory_space=pltpu.VMEM)
    return pl.pallas_call(
        kernel,
        out_shape=[
            jax.ShapeDtypeStruct((near_count, 128), F32),
            jax.ShapeDtypeStruct((rows, frames), F32),
            jax.ShapeDtypeStruct((rows, 128), F32),
        ],
        in_specs=[whole] * 4,
        out_specs=[whole] * 3,
        scratch_shapes=[pltpu.VMEM((count, 128), F32)],
        compiler_params=pltpu.CompilerParams(vmem_limit_bytes=VMEM),
        cost_estimate=cost(0.1),
        name="look_up",
    )(wanted, codebook, project, cotangent)


def code_payload(dchosen, latent, mixed_grad, near, place, refill, after_this):
    count = dchosen.shape[0]
    taps, _, chans = mixed_grad.shape
    blocks, step = refill.shape

    rows = 24 * blocks + 8 * taps
    quarter = rows // 4

    def kernel(d_ref, l_ref, m_ref, n_ref, p_ref, r_ref, _, o0, o1, o2, o3, out_ref):
        lane = lax.broadcasted_iota(jnp.int32, (count, 128), 1)
        owned = p_ref[...] >= 0
        grads = d_ref[...]
        high = grads.astype(BF).astype(F32)
        left = high + pltpu.roll(grads - high, 8, 1) + jnp.where((lane == 16) & owned, 1.0, 0.0)
        left = left.astype(BF)
        right = l_ref[...].astype(BF)

        @pl.loop(0, blocks)
        def _(block):
            wants = n_ref[...] - block * step
            hot = jnp.concatenate(
                [jnp.where(wants == lane + g * 128, 1.0, 0.0).astype(BF) for g in range(step // 128)], axis=1
            )
            into = dot_tn(left, hot)
            wanted = r_ref[pl.ds(block, 1), :]
            hot = jnp.concatenate(
                [
                    jnp.where(p_ref[...] == wanted[:, g * 128 : (g + 1) * 128], 1.0, 0.0).astype(BF)
                    for g in range(step // 128)
                ],
                axis=1,
            )
            picked = dot_tn(right, hot)
            start = pl.multiple_of(block * 24, 8)
            out_ref[pl.ds(start, 24), :] = jnp.concatenate(
                [into[0:8] + into[8:16], picked[0:8], into[16:24]], axis=0
            )

        for tap in range(taps):
            out_ref[24 * blocks + 8 * tap : 24 * blocks + 8 * tap + 8, :] = m_ref[tap]
        me = lax.axis_index("chan")
        for p, piece in enumerate((o0, o1, o2, o3)):
            piece[...] = out_ref[pl.ds(pl.multiple_of((me ^ p) * quarter, 8), quarter), :].astype(BF)

    whole = pl.BlockSpec(memory_space=pltpu.VMEM)
    held = pl.BlockSpec(memory_space=pl.ANY)
    return pl.pallas_call(
        kernel,
        out_shape=[jax.ShapeDtypeStruct((quarter, chans), BF)] * 4,
        in_specs=[whole] * 6 + [held],
        out_specs=[whole] * 4,
        scratch_shapes=[pltpu.VMEM((rows, chans), F32)],
        compiler_params=pltpu.CompilerParams(vmem_limit_bytes=VMEM),
        cost_estimate=cost(0.1),
        name="code_payload",
    )(dchosen, latent, mixed_grad, near, place, refill, after_this)


def strided_meet(strided, mixed_grad, project, norms):
    taps, rows, chans = strided.shape
    group = 4

    def kernel(w_ref, m_ref, p_ref, n_ref, vec_ref, factor_ref, total):
        step = pl.program_id(0)

        @pl.when(step == 0)
        def _():
            total[...] = jnp.zeros_like(total)

        meeting = total[...]
        for tap in range(group):
            meeting = meeting + dot_nt(m_ref[tap], w_ref[tap])
        total[...] = meeting

        @pl.when(step == taps // group - 1)
        def _():
            plain = p_ref[...].astype(F32)
            along = jnp.sum(plain * total[...], axis=0, keepdims=True)
            vec_ref[...] = jnp.zeros_like(vec_ref)
            vec_ref[0:8, :] = total[...] * n_ref[0:1, :]
            vec_ref[8:9, :] = along * n_ref[2:3, :]
            factor_ref[...] = jnp.broadcast_to(along * n_ref[1:2, :], (128, rows)).T

    whole = pl.BlockSpec(memory_space=pltpu.VMEM)
    return pl.pallas_call(
        kernel,
        grid=(taps // group,),
        out_shape=[jax.ShapeDtypeStruct((16, rows), F32), jax.ShapeDtypeStruct((rows, 128), F32)],
        in_specs=[
            pl.BlockSpec((group, rows, chans), lambda step: (step, 0, 0)),
            pl.BlockSpec((group, 8, chans), lambda step: (step, 0, 0)),
            whole,
            whole,
        ],
        out_specs=[
            pl.BlockSpec((16, rows), lambda step: (0, 0)),
            pl.BlockSpec((rows, 128), lambda step: (0, 0)),
        ],
        scratch_shapes=[pltpu.VMEM((8, rows), F32)],
        compiler_params=pltpu.CompilerParams(vmem_limit_bytes=VMEM),
        cost_estimate=cost(0.1),
        name="strided_meet",
    )(strided, mixed_grad, project, norms)


def strided_back(strided, mixed_grad, project, norms, factors):
    taps, rows, chans = strided.shape
    group = 4

    def kernel(w_ref, m_ref, p_ref, n_ref, f_ref, out_ref):
        split = jnp.concatenate(terms(p_ref[...].astype(F32) * n_ref[0:1, :], 3), axis=0)
        for tap in range(group):
            three = jnp.concatenate([m_ref[tap]] * 3, axis=0)
            out_ref[tap] = dot_tn(split, three) - w_ref[tap].astype(F32) * lanes4(f_ref[...])

    whole = pl.BlockSpec(memory_space=pltpu.VMEM)
    return pl.pallas_call(
        kernel,
        grid=(taps // group,),
        out_shape=jax.ShapeDtypeStruct((taps, rows, chans), F32),
        in_specs=[
            pl.BlockSpec((group, rows, chans), lambda step: (step, 0, 0)),
            pl.BlockSpec((group, 8, chans), lambda step: (step, 0, 0)),
            whole,
            whole,
            whole,
        ],
        out_specs=pl.BlockSpec((group, rows, chans), lambda step: (step, 0, 0)),
        compiler_params=pltpu.CompilerParams(vmem_limit_bytes=VMEM),
        cost_estimate=cost(0.1),
        name="strided_back",
    )(strided, mixed_grad, project, norms, factors)


def norm_back(chains, dilated, pointwise, gains, members, earlier):
    units, _, part, chans = dilated.shape
    count = len(members)
    others = earlier[2:]

    def kernel(*refs):
        halves, refs = refs[: 2 * count], refs[2 * count :]
        w_refs, q_refs, g_refs = (refs[n * count : (n + 1) * count] for n in range(3))
        out7, out1, out_g7, out_g1, helds, res7, res1, sems = refs[-8:]
        given = refs[3 * count + 2 : 3 * count + 2 + len(others)] if earlier else ()
        outs = []

        def send(value, target):
            outs.append(pltpu.make_async_copy(value, target, sems.at[len(outs)]))
            outs[-1].start()

        for n, member in enumerate(members):
            rows = halves[2 * n].shape[0]
            upper = bit_of(*chains[n].last)
            helds[n, pl.ds(pl.multiple_of(upper * rows, 16), rows), :] = halves[2 * n][...]
            helds[n, pl.ds(pl.multiple_of((1 - upper) * rows, 16), rows), :] = halves[2 * n + 1][...]

            def grad_of(tap, n=n):
                return helds[n, tap * part : (tap + 1) * part, :].astype(F32)

            def weight_of(tap, n=n):
                return (q_refs[n][0] if tap == 7 else w_refs[n][0, tap]).astype(F32)

            for which, taps in enumerate((range(7), (7,))):
                square = jnp.zeros((part, 128), F32)
                along = jnp.zeros((part, 128), F32)
                for tap in taps:
                    value, grad = weight_of(tap), grad_of(tap)
                    both, value2 = value * grad, value * value
                    for g in range(chans // 128):
                        cols = slice(g * 128, (g + 1) * 128)
                        square = square + value2[:, cols]
                        along = along + both[:, cols]
                square_sum = jnp.sum(square, axis=1, keepdims=True) + NORM_EPS
                factor = jnp.sum(along, axis=1, keepdims=True) / square_sum
                row = lane_sums(along) / g_refs[n][0, which : which + 1, :]
                out_g = (out_g7, out_g1)[which]
                place = member if others else 0
                out_g[place : place + 1, :] = row
                for other in range(len(others) // 2):
                    place = units - 1 - other
                    out_g[place : place + 1, :] = given[2 * other + which][...]
                for tap in taps:
                    target = res1.at[n] if tap == 7 else res7.at[n, tap]
                    target[...] = grad_of(tap) - weight_of(tap) * factor
                    send(target, out1.at[member] if tap == 7 else out7.at[member, tap])
        for copy in outs:
            copy.wait()

    whole = pl.BlockSpec(memory_space=pltpu.VMEM)
    held = pl.BlockSpec(memory_space=pl.ANY)

    def block(shape, member):
        return pl.BlockSpec((1,) + shape, lambda step: (member,) + (0,) * len(shape))

    return pl.pallas_call(
        kernel,
        grid=(1,),
        out_shape=[
            jax.ShapeDtypeStruct((units, 7, part, chans), F32),
            jax.ShapeDtypeStruct((units, part, chans), F32),
        ]
        + [jax.ShapeDtypeStruct((units if others else 1, part), F32)] * 2,
        in_specs=[whole] * (2 * count)
        + [block((7, part, chans), member) for member in members]
        + [block((part, chans), member) for member in members]
        + [block((2, part), member) for member in members]
        + [held] * len(earlier[:2])
        + [whole] * len(others),
        out_specs=[held, held, whole, whole],
        input_output_aliases={5 * count + n: n for n in range(len(earlier[:2]))},
        scratch_shapes=[
            pltpu.VMEM((count, max(2 * chain.whole[0].shape[0] for chain in chains), chans), BF),
            pltpu.VMEM((count, 7, part, chans), F32),
            pltpu.VMEM((count, part, chans), F32),
            pltpu.SemaphoreType.DMA((8 * count,)),
        ],
        compiler_params=pltpu.CompilerParams(vmem_limit_bytes=VMEM),
        cost_estimate=cost(0.1),
        name="norm_back",
    )(*[half for chain in chains for half in chain.whole], *[dilated] * count, *[pointwise] * count, *[gains] * count, *earlier)


def leave(grad, own):
    rows, chans = grad.shape
    span = rows // SEG
    part = chans // 4

    def kernel(g_ref, o0, o1, o2, o3, ordered, placed):
        me = lax.axis_index("chan")
        for p, out in enumerate((o0, o1, o2, o3)):
            placed[...] = g_ref[:, pl.ds(pl.multiple_of((me ^ p) * part, part), part)]
            for a in range(SEG):
                ordered[pl.ds(a * span, span), :] = placed[pl.ds(a, span, stride=SEG), :]
            out[...] = ordered[pl.ds(HALO, own), :].T.astype(out.dtype)

    whole = pl.BlockSpec(memory_space=pltpu.VMEM)
    return pl.pallas_call(
        kernel,
        out_shape=[jax.ShapeDtypeStruct((part, own), F32)] + [jax.ShapeDtypeStruct((part, own), BF)] * 3,
        in_specs=[whole],
        out_specs=[whole] * 4,
        scratch_shapes=[pltpu.VMEM((rows, part), F32)] * 2,
        compiler_params=pltpu.CompilerParams(vmem_limit_bytes=VMEM),
        cost_estimate=cost(0.1),
        name="leave",
    )(grad)


def settle(pieces):
    part, own = pieces[0].shape

    def kernel(p0, p1, p2, p3, out_ref):
        me = lax.axis_index("chan")
        for p, piece in enumerate((p0, p1, p2, p3)):
            out_ref[:, pl.ds(pl.multiple_of((me ^ p) * own, own), own)] = piece[...].astype(F32)

    whole = pl.BlockSpec(memory_space=pltpu.VMEM)
    return pl.pallas_call(
        kernel,
        out_shape=jax.ShapeDtypeStruct((part, 4 * own), F32),
        in_specs=[whole] * 4,
        out_specs=whole,
        compiler_params=pltpu.CompilerParams(vmem_limit_bytes=VMEM),
        cost_estimate=cost(0.1),
        name="settle",
    )(*pieces)


def bottleneck(stream, merged, bias, vecs, labels, chosen, picked_grad, own):
    rows, chans = stream.shape
    span = rows // SEG
    groups = span // STRIDE
    count = groups * SEG
    taps = merged[0].shape[0] // 8 - 1
    edge = 16 * SEG
    turn_row = vecs.shape[0] - 8

    def kernel(
        s_ref, wa_ref, wb_ref, bias_ref, v_ref, l_ref, c_ref, o_ref, g_ref, lat_ref, dch_ref, m_ref, sum_ref,
        q_ref, wide, full, codes, sums,
    ):
        blank = jnp.zeros((104, chans), BF)
        for tap in range(taps):
            here = slice(8 * tap, 8 * tap + 8)
            high, rest = terms(wa_ref[here, :] + wb_ref[here, :], 2)
            q_ref[tap] = jnp.concatenate([high, high, rest, blank], axis=0)
        shift = jnp.sum(
            jnp.where(
                lax.broadcasted_iota(jnp.int32, (8, 128), 0) == lax.broadcasted_iota(jnp.int32, (8, 128), 1),
                wa_ref[8 * taps : 8 * taps + 8, 0:128] + wb_ref[8 * taps : 8 * taps + 8, 0:128],
                0.0,
            ),
            axis=0,
            keepdims=True,
        )

        @pl.loop(0, rows, step=CHUNK)
        def _(start):
            start = pl.multiple_of(start, CHUNK)
            act = snake(s_ref[pl.ds(start, CHUNK), :], v_ref[turn_row : turn_row + 1, :], v_ref[turn_row + 1 : turn_row + 2, :])
            full[pl.ds(8 + start, CHUNK), :] = act
            wide[pl.ds(edge + start, CHUNK), :] = act.astype(BF)

        wide[pl.ds(0, edge), :] = full[pl.ds(8 + rows - edge - 1, edge), :].astype(BF)
        wide[pl.ds(edge + rows, edge), :] = full[pl.ds(8 + 1, edge), :].astype(BF)

        def tap_mask(tap, first, amount):
            base = (LEAD + first * STRIDE) * SEG
            pieces = []
            for g in range(amount):
                start = base + g * STRIDE * SEG
                there = l_ref[pl.ds(start + (tap - 4) * SEG, SEG), :]
                pieces.append(jnp.where(there == l_ref[pl.ds(start, SEG), :], 1.0, 0.0).astype(F32))
            return jnp.concatenate(pieces, axis=0)

        def tap_columns(tap):
            base = edge + (tap - 4) * SEG
            picked = jnp.concatenate(
                [wide[pl.ds(base + g * STRIDE * SEG, SEG), :] for g in range(groups)], axis=0
            )
            return picked * lanes4(tap_mask(tap, 0, groups).astype(BF))

        total = jnp.zeros((count, 128), F32)
        for tap in range(taps):
            total = total + dot_nt(tap_columns(tap), q_ref[tap])
        lane = lax.broadcasted_iota(jnp.int32, (count, 128), 1)
        latent = jnp.where(lane < 8, total + pltpu.roll(total, 112, 1) + shift + bias_ref[...], 0.0)
        lat_ref[...] = latent
        inverse = lax.rsqrt(jnp.sum(latent * latent, axis=1, keepdims=True) + 1.0)
        normed = latent * inverse
        spread = (2.0 * COMMIT) * (normed - c_ref[...])
        row = lax.broadcasted_iota(jnp.int32, (count, 128), 0)
        place = (row & (SEG - 1)) * groups + (row >> 4)
        mine = (place >= HALO // STRIDE) & (place < (HALO + own) // STRIDE)
        dch_ref[...] = jnp.where(mine, o_ref[...] - spread, 0.0)
        dlatent = (spread - normed * jnp.sum(normed * spread, axis=1, keepdims=True)) * inverse

        def split(values):
            high = values.astype(BF).astype(F32)
            return high + pltpu.roll(values - high, 8, 1), pltpu.roll(high, 16, 1)

        dmine = jnp.where(mine, dlatent, 0.0)
        sum_ref[1:2, :] = jnp.concatenate([jnp.sum(dmine, axis=0, keepdims=True)] * 4, axis=1)
        pair, _unused = split(dmine)
        pair = pair.astype(BF)
        for tap in range(taps):
            both = dot_tn(pair, tap_columns(tap))
            m_ref[tap] = both[0:8, :] + both[8:16, :]

        pair, again = split(dlatent)
        codes[pl.ds(8 + SEG, count), :] = pair + again
        codes[pl.ds(8, SEG), :] = codes[pl.ds(8 + count - 1, SEG), :]
        codes[pl.ds(8 + SEG + count, SEG), :] = codes[pl.ds(8 + SEG + 1, SEG), :]
        sums[...] = jnp.zeros_like(sums)
        for rest in range(STRIDE):
            total = None
            for tap in (rest - 4, rest + 4, rest + 12):
                if 0 <= tap < taps:
                    hop = (tap - 4 - rest) // STRIDE
                    left = codes[pl.ds(8 + SEG - hop * SEG, count), :] * tap_mask(tap, -hop, groups)
                    term = dot_nn(left.astype(BF), q_ref[tap])
                    total = term if total is None else total + term
            for g in range(groups):
                here = pl.ds((g * STRIDE + rest) * SEG, SEG)
                part = total[g * SEG : (g + 1) * SEG, :]
                value, slope, by_alpha = snake_parts(s_ref[here, :], v_ref[turn_row : turn_row + 1, :], v_ref[turn_row + 1 : turn_row + 2, :])
                g_ref[here, :] = part * slope
                mask = lanes4(own_mask((g * STRIDE + rest) * SEG, SEG, span, own))
                sums[...] += fold(part * by_alpha * mask)
        sum_ref[0:1, :] = sums[...].sum(axis=0, keepdims=True)
        sum_ref[2:8, :] = jnp.zeros((6, chans), F32)

    whole = pl.BlockSpec(memory_space=pltpu.VMEM)
    return pl.pallas_call(
        kernel,
        out_shape=[
            jax.ShapeDtypeStruct((rows, chans), F32),
            jax.ShapeDtypeStruct((count, 128), F32),
            jax.ShapeDtypeStruct((count, 128), F32),
            jax.ShapeDtypeStruct((taps, 8, chans), F32),
            jax.ShapeDtypeStruct((8, chans), F32),
        ],
        in_specs=[whole] * 8,
        out_specs=[whole] * 5,
        scratch_shapes=[
            pltpu.VMEM((taps, 128, chans), BF),
            pltpu.VMEM((rows + 2 * edge, chans), BF),
            pltpu.VMEM((rows + 16, chans), F32),
            pltpu.VMEM((count + 2 * SEG + 16, 128), F32),
            pltpu.VMEM((8, chans), F32),
        ],
        compiler_params=pltpu.CompilerParams(vmem_limit_bytes=VMEM),
        cost_estimate=cost(11),
        name="bottleneck",
    )(stream, *merged, bias, vecs, labels, chosen, picked_grad)


def swap(value, axis, bit):
    count = lax.axis_size(axis)
    return lax.ppermute(value, axis, [(i, i ^ (1 << bit)) for i in range(count)])


def bits_of(axis):
    count = lax.axis_size(axis)
    return [(axis, bit) for bit in range(count.bit_length() - 1)]


def total_over(value, steps):
    for axis, bit in steps:
        value = value + swap(value, axis, bit)
    return value


def bit_of(axis, bit):
    return (lax.axis_index(axis) >> bit) & 1


def halves_of(value, step):
    axis, bit = step
    half = value.shape[0] // 2
    mine = bit_of(axis, bit)
    kept = lax.dynamic_slice_in_dim(value, mine * half, half)
    return kept, lax.dynamic_slice_in_dim(value, (1 - mine) * half, half).astype(BF)


def add_up(kept, got):
    return (kept.astype(F32) + got.astype(F32)).astype(BF)


def sum_halves(terms_in, rows, step, micros=0.1):
    chans = terms_in[0][0][0].shape[-1]
    flat = [ref for block in terms_in for ref, _ in block]
    half = rows // 2 if step else rows

    def kernel(*refs):
        refs = list(refs)
        ins = [refs.pop(0) for _ in flat]
        outs = refs[: 2 if step else 1]
        total, sems = refs[-2:] if step else (outs[0], None)
        at, start = 0, 0
        for block in terms_in:
            value = None
            for _, index in block:
                ref = ins[at] if index is None else ins[at].at[index]
                term = ref[...].astype(F32)
                value = term if value is None else value + term
                at += 1
            value = value.astype(BF).reshape(-1, chans)
            total[start : start + value.shape[0], :] = value
            start += value.shape[0]
        if start < rows:
            total[start:rows, :] = jnp.zeros((rows - start, chans), BF)
        if step:
            mine = bit_of(*step)
            copies = []
            for n, out in enumerate(outs):
                place = pl.multiple_of((mine if n == 0 else 1 - mine) * half, 16)
                copies.append(pltpu.make_async_copy(total.at[pl.ds(place, half)], out, sems.at[n]))
                copies[-1].start()
            for copy in copies:
                copy.wait()

    def spec(ref, index):
        if index is None:
            return pl.BlockSpec(memory_space=pltpu.VMEM)
        return pl.BlockSpec((1,) + ref.shape[1:], lambda n: (index,) + (0,) * (ref.ndim - 1))

    flat_pairs = [pair for block in terms_in for pair in block]
    terms_in = [[(ref, None if index is None else 0) for ref, index in block] for block in terms_in]
    return pl.pallas_call(
        kernel,
        grid=(1,),
        out_shape=[jax.ShapeDtypeStruct((half, chans), BF)] * (2 if step else 1),
        in_specs=[spec(ref, index) for ref, index in flat_pairs],
        out_specs=[pl.BlockSpec(memory_space=pl.ANY)] * 2 if step else [pl.BlockSpec(memory_space=pltpu.VMEM)],
        scratch_shapes=[pltpu.VMEM((rows, chans), BF), pltpu.SemaphoreType.DMA((2,))] if step else [],
        compiler_params=pltpu.CompilerParams(vmem_limit_bytes=VMEM),
        cost_estimate=cost(micros),
        name="sum_halves",
    )(*flat)


def join(mine, got, step):
    rows, chans = mine.shape

    def kernel(m_ref, g_ref, out_ref):
        upper = bit_of(*step)
        out_ref[pl.ds(pl.multiple_of(upper * rows, 16), rows), :] = m_ref[...]
        out_ref[pl.ds(pl.multiple_of((1 - upper) * rows, 16), rows), :] = g_ref[...]

    whole = pl.BlockSpec(memory_space=pltpu.VMEM)
    return pl.pallas_call(
        kernel,
        out_shape=jax.ShapeDtypeStruct((2 * rows, chans), BF),
        in_specs=[whole] * 2,
        out_specs=whole,
        compiler_params=pltpu.CompilerParams(vmem_limit_bytes=VMEM),
        cost_estimate=cost(0.1),
        name="join",
    )(mine, got)


class Chain:
    def __init__(self, terms_in, rows, steps, micros=0.1):
        self.adds, self.joins = list(steps), list(reversed(steps))
        self.rows = rows
        self.kept, self.sent = sum_halves(terms_in, rows, self.adds[0], micros)
        self.whole = None
        self.left = 2 * len(steps)
        self.start()

    def start(self):
        self.got = swap(self.sent, *(self.adds[0] if self.adds else self.joins[0]))

    def step(self, token):
        got = after(self.got, token)
        self.left -= 1
        if self.adds:
            self.adds.pop(0)
            self.rows //= 2
            terms_in = [[(self.kept, None), (got, None)]]
            if self.adds:
                self.kept, self.sent = sum_halves(terms_in, self.rows, self.adds[0])
            else:
                self.sent = sum_halves(terms_in, self.rows, None)[0]
        elif self.left:
            self.sent = join(self.sent, got, self.joins.pop(0))
        else:
            self.whole = (self.sent, got)
            self.last = self.joins.pop(0)
        if self.left:
            self.start()
        return self.sent

    def upper(self):
        return jnp.where(bit_of(*self.last) == 1, *self.whole)


def after(value, *others):
    return lax.optimization_barrier((value, *others))[0]


def to_peer(value, peer):
    return lax.ppermute(value, "chan", [(i, i ^ peer) for i in range(4)])


def local(
    signal,
    dilated_dirs,
    dilated_gains,
    dilated_bias,
    snake_first,
    snake_second,
    pointwise_dirs,
    pointwise_gains,
    pointwise_bias,
    snake_last,
    strided_dirs,
    strided_gains,
    strided_bias,
    latent_proj,
    latent_bias,
    codebook,
    output_proj,
    output_bias,
    utterances,
    code_index,
    refill_index,
    cotangent,
):
    part, extent = signal.shape
    chans = 4 * part
    own = extent // 4
    frames = code_index.shape[0]
    own_frames = frames // 4
    whole = lax.axis_size("frames") * extent
    units = dilated_dirs.shape[0]
    span = (own + 2 * HALO) // SEG
    span_frames = span // STRIDE
    extra = HALO // STRIDE
    me = lax.axis_index("chan")
    block = lax.axis_index("frames")
    ring = lax.axis_size("frames")
    origin = block * extent + me * own
    over_chan, over_frames = bits_of("chan"), bits_of("frames")

    halves = halve(dilated_dirs, pointwise_dirs)
    far = [swap(halves[0], "chan", 1)]
    close = [swap(after(dilated_dirs, halves[0]), "chan", 0), swap(after(pointwise_dirs, halves[0]), "chan", 0)]

    project = jnp.concatenate(
        [output_proj] + [term[:, None] for term in terms(output_bias, 3)] + [jnp.zeros((output_bias.shape[0], 117), BF)],
        axis=1,
    )
    packed, pulled = vectors(
        after(dilated_dirs, halves[0]), pointwise_dirs, dilated_gains, pointwise_gains, dilated_bias, pointwise_bias,
        snake_first, snake_second, snake_last, project, cotangent,
    )

    pieces, ends = cut(signal, packed, pulled, code_index.reshape(-1, 128))
    pieces = [pieces[0]] + [to_peer(pieces[peer], peer) for peer in (1, 2, 3)]
    ends = [
        lax.ppermute(
            ends[peer],
            ("frames", "chan"),
            [(4 * (f + 1) + (3 ^ peer), 4 * f + 3) for f in range(ring - 1)]
            + [(4 * f + peer, 4 * (f + 1)) for f in range(ring - 1)],
        )
        for peer in range(4)
    ]
    rest = [swap(far[0], "frames", 0)]
    far_close = [swap(far[0], "chan", 0)]
    rest_close = [swap(rest[0], "chan", 0)]
    far.append(swap(after(halves[1], *pieces), "chan", 1))
    far.append(swap(after(halves[2], *pieces), "chan", 1))

    bounds = jnp.cumsum(utterances) * STRIDE
    b_place = jnp.arange(-LEAD, span + LEAD, dtype=jnp.int32)
    spots = (origin - HALO + b_place[:, None] + span * jnp.arange(SEG, dtype=jnp.int32)[None, :]).reshape(-1)
    found = jnp.sum((spots[:, None] >= bounds[None, :]).astype(F32), axis=1)
    found = jnp.where((spots >= 0) & (spots < whole), found, -1.0)
    labels = jnp.broadcast_to(found[:, None], (found.shape[0], 128))

    place = (
        jnp.arange(SEG, dtype=jnp.int32)[None, :] * span_frames + jnp.arange(span_frames, dtype=jnp.int32)[:, None]
    ).reshape(-1)
    owned = (place >= extra) & (place < extra + own_frames)
    place = jnp.where(owned, place - extra + block * frames + me * own_frames, -1)
    place = jnp.broadcast_to(place[:, None], (place.shape[0], 128))
    refill = refill_index.reshape(-1, 512)
    labels, place, refill, project_in, _ = lax.optimization_barrier((labels, place, refill, latent_proj, halves[0]))
    merged, norms = merge_strided(strided_dirs, strided_gains, strided_bias, project_in)
    *held, _, _ = lax.optimization_barrier((*pieces, *ends, far[0], merged))
    stream, vecs, pulled, edge_codes = enter(held[:4], held[4:], packed.shape[0], own)

    def unit(member, stream, *far_pieces):
        pieces = (dilated_dirs, pointwise_dirs, *close, *far_pieces)
        result, middle, wide, weight1 = unit_forward(stream, pieces, member, vecs, labels)
        saved.append((stream, middle, wide, weight1, pieces))
        return result

    saved = []
    stream = unit(0, stream, far[0], rest[0], far_close[0], rest_close[0])
    rest.append(swap(after(far[1], stream), "frames", 0))
    far_close.append(swap(after(far[1], stream), "chan", 0))
    got = swap(after(merged, stream), "chan", 0)

    edge_codes = edge_codes.astype(jnp.int32)
    around = jnp.concatenate([edge_codes[1, 128 - extra :], code_index, edge_codes[0, :extra]])
    near = lax.dynamic_slice_in_dim(around, me * own_frames, own_frames + 2 * extra)
    near = near.reshape(SEG, span_frames).T.reshape(-1)
    wanted = jnp.broadcast_to(jnp.concatenate([near, code_index])[:, None], (near.shape[0] + frames, 128))
    near_rows = wanted[: near.shape[0]]
    pulled = jnp.pad(pulled, ((0, 120), (extra, extra)))
    pulled = pulled.reshape(128, SEG, span_frames).transpose(2, 1, 0).reshape(-1, 128)
    latent_bias = jnp.pad(latent_bias, (0, 128 - latent_bias.shape[0]))[None]
    wanted, near_rows, pulled, latent_bias, _ = lax.optimization_barrier((wanted, near_rows, pulled, latent_bias, stream))
    chosen, output, sums_out = look_up(wanted, codebook, project, cotangent, near.shape[0])
    merged = merged + after(got, chosen)
    got = swap(merged, "chan", 1)
    rest_close.append(swap(after(rest[1], merged), "chan", 0))
    rest.append(swap(after(halves[3], far[2], merged), "chan", 1))
    far_close.append(swap(after(far[2], merged), "chan", 0))
    stream = unit(1, after(stream, chosen), far[1], rest[1], far_close[1], rest_close[1])
    rest_close.append(swap(after(rest[2], stream), "chan", 0))
    stream = unit(2, stream, far[2], rest[2], far_close[2], rest_close[2])
    merged = (merged, after(got, stream))
    grad, latent, dchosen, mixed_grad, last_sums = bottleneck(
        stream, merged, latent_bias, vecs, labels, chosen, pulled, own
    )

    bit0, bit1 = over_chan

    rows = grad.shape[0]

    def weights_of(member, grad=None):
        _, middle, wide, weight1, _ = saved[member]
        return (member, grad, middle, wide, weight1)

    def into_of(member, grad, scaled):
        return (member, grad, saved[member][0], scaled, saved[member][4])

    back2 = units_back(vecs, labels, own, rows, chans, weights=weights_of(2, grad))
    keep2 = back2["keep"]
    near2 = swap(back2["send"], "chan", 0)
    chain_rows = -(-(8 * part + 128) // (16 * ring)) * 16 * ring
    codes = code_payload(dchosen, latent, mixed_grad, near_rows, place, refill, back2["sums_a"])
    codes = [codes[0]] + [to_peer(codes[peer], peer) for peer in (1, 2, 3)]
    near2 = after(near2, codes[0])
    far2 = add_up(keep2[1], near2[1])
    x2 = swap(far2, "chan", 1)
    back1 = units_back(
        vecs, labels, own, rows, chans, into_of(2, after(grad, far2), back2["scaled_out"]), weights_of(1)
    )
    keep1 = back1["keep"]
    near1 = swap(back1["send"], "chan", 0)
    x2, *codes, _ = lax.optimization_barrier((x2, *codes, back1["sums_a"]))
    chain2 = Chain(
        [[(keep2, 0), (near2, 0), (x2, None)], [(piece, None) for piece in codes]], chain_rows, over_frames, 20
    )
    far1 = add_up(keep1[1], after(near1, chain2.sent)[1])
    x1 = swap(far1, "chan", 1)
    back0 = units_back(
        vecs, labels, own, rows, chans,
        into_of(1, after(back1["out"], far1), back1["scaled_out"]), weights_of(0),
    )
    keep0 = back0["keep"]
    near0 = swap(back0["send"], "chan", 0)
    token = chain2.step(back0["sums_a"])
    more = sums_out[:, :16].astype(BF).reshape(-1, chans)
    more = jnp.pad(more, ((0, 16 - more.shape[0]), (0, 0)))
    chain1 = Chain([[(keep1, 0), (near1, 0), (after(x1, token), None)], [(more, None)]], chain_rows, over_frames)
    last = units_back(
        vecs, labels, own, rows, chans, into_of(0, after(back0["out"], chain1.sent), back0["scaled_out"]),
        others=(
            (back0["sums_a"], 3), (back0["sums_c"], 1), (back1["sums_a"], 3), (back1["sums_c"], 1),
            (back2["sums_a"], 3), (last_sums, 2),
        ),
    )
    grad, small = last["out"], last["sums_c"]

    token = chain2.step(grad)
    token = chain1.step(token)
    far0 = add_up(keep0[1], after(near0, token)[1])
    x0 = swap(far0, "chan", 1)
    small_steps = [bit0] + over_frames + [bit1]
    small_got = swap(small, *small_steps[0])
    outs = leave(after(grad, far0), own)
    sent_outs = [outs[0]] + [to_peer(outs[peer], peer) for peer in (1, 2, 3)]
    token = outs[0]

    def small_step():
        nonlocal small, small_got, token
        small = small + after(small_got, token)
        small_steps.pop(0)
        if small_steps:
            small_got = swap(small, *small_steps[0])
        token = small

    half = len(over_frames)
    while chain2.adds:
        token = chain2.step(token)
    small_step()
    token = chain1.step(token)
    small_step()
    token = chain2.step(token)
    chain0 = Chain([[(keep0, 0), (near0, 0), (after(x0, token), None)]], 8 * part, over_frames)
    token = chain0.sent
    while chain1.left > half:
        token = chain1.step(token)
    while chain2.left > 1:
        token = chain2.step(token)
    token = chain0.step(token)
    while len(small_steps) > 2:
        small_step()
    while chain0.left > half + 1:
        token = chain0.step(token)
    token = chain2.step(token)
    quarter = codes[0].shape[0]
    first = 8 * part - chain_rows // 2
    codes_mine = chain2.upper()[first : first + quarter]
    got_codes = [codes_mine] + [to_peer(codes_mine, peer) for peer in (1, 2, 3)]
    token = chain1.step(token)
    small_step()
    token = chain0.step(token)
    payload = jnp.zeros((4 * quarter, chans), BF)
    for peer in range(4):
        got = after(got_codes[peer], token)
        payload = lax.dynamic_update_slice_in_dim(payload, got, (me ^ peer) * quarter, 0)
    blocks = codebook.shape[1] // 512
    mixed_total = payload[24 * blocks :].reshape(-1, 8, chans)
    meeting, factors = strided_meet(strided_dirs, mixed_total, latent_proj, norms)
    token = chain0.step(meeting)
    while chain1.left > 1:
        token = chain1.step(token)
    small_step()
    gains = jnp.stack([dilated_gains, pointwise_gains], axis=1)
    results = norm_back([chain2], after(dilated_dirs, token), pointwise_dirs, gains, (2,), ())
    gains2 = results[2:]
    grad_signal = settle(list(lax.optimization_barrier((*sent_outs, results[0]))[:4]))
    token = grad_signal
    while chain0.left > 1:
        token = chain0.step(token)
    payload = after(payload, token)
    codes = codebook.shape[1]
    blocks = codes // 512
    by_code = payload[: 24 * blocks].reshape(blocks, 24, 512).transpose(1, 0, 2).reshape(24, codes).astype(F32)
    dcoded, picked, usage = by_code[0:8], by_code[8:16], by_code[16]
    refreshed = jnp.where(usage[None, :] > 0, codebook, picked)
    coded_scale = lax.rsqrt(jnp.sum(codebook * codebook, axis=0) + 1.0)
    coded = codebook * coded_scale[None, :]
    dcodebook = (dcoded - coded * jnp.sum(coded * dcoded, axis=0)[None, :]) * coded_scale[None, :]

    factors = lax.optimization_barrier((factors, token, refreshed, dcodebook))[0]
    dstrided_dirs = strided_back(strided_dirs, mixed_total, latent_proj, norms, factors)
    token = chain1.step(dstrided_dirs)
    results = norm_back([chain1], after(dilated_dirs, token), pointwise_dirs, gains, (1,), results[:2])
    token = results[0]
    chain0.step(token)
    results = norm_back([chain0], dilated_dirs, pointwise_dirs, gains, (0,), (*results[:2], *gains2, *results[2:]))
    sums_out = chain1.upper()[first : first + output_bias.shape[0] * 16 // chans].astype(F32).reshape(-1, 16)
    mine_small = lax.dynamic_slice_in_dim(small, me * part, part, axis=1)
    dbias_latent = small[4 * units + 1, :8]
    dalpha1, dbias1, dbias7, dalpha2 = (mine_small[n : 4 * units : 4] for n in range(4))
    dalpha_last = mine_small[4 * units]
    dproj_latent = meeting[0:8] + dbias_latent[:, None] * strided_bias[None, :]
    dbias_strided = jnp.sum(latent_proj.astype(F32) * dbias_latent[:, None], axis=0)
    return (
        output,
        grad_signal,
        results[0],
        results[2],
        dbias7,
        dalpha1,
        dalpha2,
        results[1],
        results[3],
        dbias1,
        dalpha_last,
        dstrided_dirs,
        meeting[8],
        dbias_strided,
        dproj_latent,
        dbias_latent,
        dcodebook,
        sums_out[:, :8],
        sums_out[:, 8],
        refreshed,
    )


def solution(mesh):
    in_specs = (
        P("chan", "frames"),
        P(None, None, "chan", None),
        P(None, "chan"),
        P(None, "chan"),
        P(None, "chan"),
        P(None, "chan"),
        P(None, "chan", None),
        P(None, "chan"),
        P(None, "chan"),
        P("chan"),
        P(None, "chan", None),
        P("chan"),
        P("chan"),
        P(None, "chan"),
        P(),
        P(),
        P("chan", None),
        P("chan"),
        P(),
        P("frames"),
        P(),
        P("chan", "frames"),
    )
    out_specs = (
        P("chan", "frames"),
        P("chan", "frames"),
        P(None, None, "chan", None),
        P(None, "chan"),
        P(None, "chan"),
        P(None, "chan"),
        P(None, "chan"),
        P(None, "chan", None),
        P(None, "chan"),
        P(None, "chan"),
        P("chan"),
        P(None, "chan", None),
        P("chan"),
        P("chan"),
        P(None, "chan"),
        P(),
        P(),
        P("chan", None),
        P("chan"),
        P(),
    )
    return jax.shard_map(local, mesh=mesh, in_specs=in_specs, out_specs=out_specs, check_vma=False)
```

```python
import jax
import jax.numpy as jnp
from jax import lax
from jax.experimental import pallas as pl
from jax.experimental.pallas import tpu as pltpu
from jax.sharding import PartitionSpec as P

CODES = 8192
STRIDE = 8
NORM_EPS = 1e-06
COMMIT = 4.0

BF = jnp.bfloat16
F32 = jnp.float32

SEG = 16
HALO = 128
LEAD = 28
CHUNK = 256
VMEM = 60 * 2**20
def cost(micros):
    return pl.CostEstimate(flops=int(micros * 1.15e9), bytes_accessed=0, transcendentals=0)

SIN = (3.1415902692655564, -5.1674066428989045, 2.5440093135845245, -0.5594585999205443)
COS = (0.9999999532244686, -4.934792826917481, 4.0584112640152465, -1.331875904720673, 0.21968809492172123)


def by_powers(square, factors):
    total = factors[-1]
    for factor in factors[-2::-1]:
        total = factor + square * total
    return total


def snake(value, turn, inverse):
    angle = turn * value
    angle = angle - jnp.round(angle)
    square = angle * angle
    part = by_powers(square, SIN)
    return value + (square * part) * (part * inverse)


def snake_parts(value, turn, inverse):
    angle = turn * value
    angle = angle - jnp.round(angle)
    square = angle * angle
    part = by_powers(square, SIN)
    sine2 = (square * part) * (part * inverse)
    double = (angle * part) * (2.0 * by_powers(square, COS))
    return value + sine2, 1.0 + double, (value * double - sine2) * inverse


def terms(value, count):
    parts = []
    for _ in range(count):
        part = value.astype(BF)
        parts.append(part)
        value = value - part.astype(F32)
    return parts


def lanes4(mask):
    return jnp.concatenate([mask] * 4, axis=1)


def own_mask(start, count, span, own):
    row = lax.broadcasted_iota(jnp.int32, (count, 128), 0) + start
    place = (row & (SEG - 1)) * span + (row >> 4)
    return jnp.where((place >= HALO) & (place < HALO + own), 1.0, 0.0).astype(F32)


def fold(values):
    rows, cols = values.shape
    return values.reshape(rows // 8, 8, cols).sum(axis=0)


def load_weights(pieces, member, weights, sems):
    me = lax.axis_index("chan")
    own7, own1, near7, near1 = (piece.at[member] for piece in pieces[:4])
    rows = own1.shape[0]

    def place(peer):
        return pl.ds(pl.multiple_of((me ^ peer) * rows, rows), rows)

    moves = [
        (own7, weights.at[pl.ds(0, 7), place(0), :]),
        (own1, weights.at[7, place(0), :]),
        (near7, weights.at[pl.ds(0, 7), place(1), :]),
        (near1, weights.at[7, place(1), :]),
    ]
    size = pieces[4].shape[0]
    side = 0 if member == 2 else lax.axis_index("frames") & 1
    first, second = side * (8 - size), (1 - side) * size
    moves += [
        (pieces[4], weights.at[pl.ds(first, size), place(2), :]),
        (pieces[5], weights.at[pl.ds(second, 8 - size), place(2), :]),
        (pieces[6], weights.at[pl.ds(first, size), place(3), :]),
        (pieces[7], weights.at[pl.ds(second, 8 - size), place(3), :]),
    ]
    copies = []
    for piece, target in moves:
        copy = pltpu.make_async_copy(piece, target, sems.at[len(copies)])
        copy.start()
        copies.append(copy)
    return copies


def fill_masks(mask, labels, spacing, rows):
    base = LEAD * SEG
    here = labels[pl.ds(base, rows), :]
    for tap in range(7):
        there = labels[pl.ds(base + (tap - 3) * spacing * SEG, rows), :]
        mask[tap] = jnp.where(there == here, 1.0, 0.0).astype(BF)


def fill_ends(wide, turn, margin, rows):
    edge = margin * SEG
    turn[pl.ds(8, edge + SEG), :] = wide[pl.ds(rows - SEG, edge + SEG), :].astype(F32)
    wide[pl.ds(0, edge), :] = turn[pl.ds(8 + SEG - 1, edge), :].astype(BF)
    turn[pl.ds(8, edge + SEG), :] = wide[pl.ds(edge, edge + SEG), :].astype(F32)
    wide[pl.ds(edge + rows, edge), :] = turn[pl.ds(8 + 1, edge), :].astype(BF)


class Stream:
    def __init__(self, source, target, sems):
        self.source, self.target, self.sems = source, target, sems

    def copy(self, chunk):
        here = pl.ds(chunk * CHUNK, CHUNK)
        return pltpu.make_async_copy(self.source.at[here], self.target.at[here], self.sems.at[chunk])

    def start(self, chunk):
        self.copy(chunk).start()

    def wait(self, chunk):
        self.copy(chunk).wait()


def dot_nt(left, right):
    return lax.dot_general(left, right, (((1,), (1,)), ((), ())), preferred_element_type=F32)


def dot_nn(left, right):
    return lax.dot_general(left, right, (((1,), (0,)), ((), ())), preferred_element_type=F32)


def dot_tn(left, right):
    return lax.dot_general(left, right, (((0,), (0,)), ((), ())), preferred_element_type=F32)


A1, I1, A2, I2, S7, B7, S1, B1 = range(8)


def unit_forward(stream, pieces, member, vecs, labels):
    spacing = 3**member
    rows, chans = stream.shape
    margin = 3 * spacing
    chunks = rows // CHUNK
    wide_rows = rows + 2 * margin * SEG

    def kernel(s_ref, *refs):
        parts, refs = refs[: len(pieces)], refs[len(pieces) :]
        (
            v_ref, l_ref, out_ref, mid_ref, wide_ref, w1_ref,
            weights, wide, turn, mask, stream_in, result, middle, total0, total1, sems, s_sems, o_sems, m_sems, end_sems,
        ) = refs
        v_ref = v_ref.at[pl.ds(8 * member, 8)]
        incoming = Stream(s_ref, stream_in, s_sems)
        outgoing, outgoing_mid = Stream(result, out_ref, o_sems), Stream(middle, mid_ref, m_sems)
        for chunk in range(chunks):
            incoming.start(chunk)
        copies = load_weights(parts, member, weights, sems)
        fill_masks(mask, l_ref, spacing, rows)
        for chunk in range(chunks):
            incoming.wait(chunk)
            here = pl.ds(chunk * CHUNK, CHUNK)
            act = snake(stream_in[here, :], v_ref[A1 : A1 + 1, :], v_ref[I1 : I1 + 1, :])
            wide[pl.ds(margin * SEG + chunk * CHUNK, CHUNK), :] = act.astype(BF)
        fill_ends(wide, turn, margin, rows)
        keep_wide = pltpu.make_async_copy(wide, wide_ref, end_sems.at[0])
        keep_wide.start()
        for copy in copies:
            copy.wait()
        keep_w1 = pltpu.make_async_copy(weights.at[7], w1_ref, end_sems.at[1])
        keep_w1.start()

        def convolve(chunk, total_ref):
            total = None
            for tap in range(7):
                columns = wide[pl.ds(chunk * CHUNK + tap * spacing * SEG, CHUNK), :]
                if tap != 3:
                    columns = columns * lanes4(mask[tap, pl.ds(chunk * CHUNK, CHUNK), :])
                term = dot_nt(columns, weights[tap])
                total = term if total is None else total + term
            total_ref[...] = total

        def finish(chunk, total_ref):
            here = pl.ds(chunk * CHUNK, CHUNK)
            value = total_ref[...] * v_ref[S7 : S7 + 1, :] + v_ref[B7 : B7 + 1, :]
            middle[here, :] = value
            second = snake(value, v_ref[A2 : A2 + 1, :], v_ref[I2 : I2 + 1, :]).astype(BF)
            term = dot_nt(second, weights[7])
            result[here, :] = stream_in[here, :] + term * v_ref[S1 : S1 + 1, :] + v_ref[B1 : B1 + 1, :]

        totals = (total0, total1)
        convolve(0, totals[0])
        for chunk in range(chunks):
            if chunk + 1 < chunks:
                convolve(chunk + 1, totals[(chunk + 1) % 2])
            finish(chunk, totals[chunk % 2])
            outgoing_mid.start(chunk)
            outgoing.start(chunk)
        keep_wide.wait()
        keep_w1.wait()
        for chunk in range(chunks):
            outgoing_mid.wait(chunk)
            outgoing.wait(chunk)

    whole = pl.BlockSpec(memory_space=pltpu.VMEM)
    held = pl.BlockSpec(memory_space=pl.ANY)
    return pl.pallas_call(
        kernel,
        out_shape=[
            jax.ShapeDtypeStruct((rows, chans), F32),
            jax.ShapeDtypeStruct((rows, chans), F32),
            jax.ShapeDtypeStruct((wide_rows, chans), BF),
            jax.ShapeDtypeStruct((chans, chans), BF),
        ],
        in_specs=[held] * (1 + len(pieces)) + [whole] * 2,
        out_specs=[held] * 4,
        scratch_shapes=[
            pltpu.VMEM((8, chans, chans), BF),
            pltpu.VMEM((wide_rows, chans), BF),
            pltpu.VMEM((margin * SEG + SEG + 16, chans), F32),
            pltpu.VMEM((7, rows, 128), BF),
            pltpu.VMEM((rows, chans), F32),
            pltpu.VMEM((rows, chans), F32),
            pltpu.VMEM((rows, chans), F32),
            pltpu.VMEM((CHUNK, chans), F32),
            pltpu.VMEM((CHUNK, chans), F32),
            pltpu.SemaphoreType.DMA((8,)),
            pltpu.SemaphoreType.DMA((chunks,)),
            pltpu.SemaphoreType.DMA((chunks,)),
            pltpu.SemaphoreType.DMA((chunks,)),
            pltpu.SemaphoreType.DMA((2,)),
        ],
        compiler_params=pltpu.CompilerParams(vmem_limit_bytes=VMEM),
        cost_estimate=cost(12),
        name=f"unit_forward_{spacing}",
    )(stream, *pieces, vecs, labels)


class Names:
    def __init__(self, names, refs):
        self.__dict__.update(zip(names, refs, strict=True))


def units_back(vecs, labels, own, rows, chans, into=None, weights=None, others=()):
    span = rows // SEG
    part = chans // 4
    chunks = rows // CHUNK
    held, whole = pl.BlockSpec(memory_space=pl.ANY), pl.BlockSpec(memory_space=pltpu.VMEM)
    f32_rows, bf_rows = jax.ShapeDtypeStruct((rows, chans), F32), jax.ShapeDtypeStruct((rows, chans), BF)
    ins, outs, scratch = {"labels": (labels, whole), "vecs": (vecs, whole)}, {}, {"mask": pltpu.VMEM((7, rows, 128), BF)}
    name, micros = "units_back", 20
    if into is not None:
        member_c, grad, stream, scaled, pieces = into
        spacing_c = 3**member_c
        margin_c = 3 * spacing_c
        name, micros = f"{name}_into_{spacing_c}", micros + 30
        ins |= {"grad": (grad, held), "stream": (stream, held), "scaled": (scaled, held)}
        ins |= {f"piece{n}": (piece, held) for n, piece in enumerate(pieces)}
        ins |= {f"other{n}": (other, whole) for n, (other, _) in enumerate(others)}
        outs |= {"out": (f32_rows, held), "sums_c": (jax.ShapeDtypeStruct((16 if others else 8, chans), F32), whole)}
        scratch |= {
            "weights": pltpu.VMEM((8, chans, chans), BF),
            "wide_c": pltpu.VMEM((rows + 2 * margin_c * SEG, chans), BF),
            "turn": pltpu.VMEM((margin_c * SEG + SEG + 16, chans), F32),
            "total_c": pltpu.VMEM((8, chans), F32),
            "stream_in": pltpu.VMEM((rows, chans), F32),
            "result": pltpu.VMEM((rows, chans), F32),
            "back": pltpu.VMEM((rows, chans), F32),
            "w_sems": pltpu.SemaphoreType.DMA((8,)),
            "s_sems": pltpu.SemaphoreType.DMA((chunks,)),
            "o_sems": pltpu.SemaphoreType.DMA((chunks,)),
            "d_sem": pltpu.SemaphoreType.DMA((1,)),
        }
    else:
        ins["grad"] = (weights[1], held)
    scratch |= {"grad_in": pltpu.VMEM((rows, chans), F32), "g_sems": pltpu.SemaphoreType.DMA((chunks,))}
    if weights is not None:
        member_a, _, middle, wide_act, weight1 = weights
        spacing_a = 3**member_a
        name, micros = f"{name}_weights_{spacing_a}", micros + 14
        ins |= {"middle": (middle, held), "wide": (wide_act, held), "w1": (weight1, whole)}
        outs |= {
            "scaled_out": (bf_rows, held),
            "keep": (jax.ShapeDtypeStruct((2, 8, part, chans), BF), held),
            "send": (jax.ShapeDtypeStruct((2, 8, part, chans), BF), held),
            "sums_a": (jax.ShapeDtypeStruct((8, chans), F32), whole),
        }
        scratch |= {
            "middle_in": pltpu.VMEM((rows, chans), F32),
            "wide_a": pltpu.VMEM(wide_act.shape, BF),
            "scaled_a": pltpu.VMEM((rows, chans), BF),
            "low_t": pltpu.VMEM((chans, rows), BF),
            "mid_t": pltpu.VMEM((chans, rows), BF),
            "second": pltpu.VMEM((rows, chans), BF),
            "results": pltpu.VMEM((8, chans, chans), BF),
            "total_a": pltpu.VMEM((3, 8, chans), F32),
            "m_sems": pltpu.SemaphoreType.DMA((chunks,)),
            "x_sem": pltpu.SemaphoreType.DMA((1,)),
            "a_sems": pltpu.SemaphoreType.DMA((chunks,)),
            "r_sems": pltpu.SemaphoreType.DMA((8, 4)),
        }

    def go_into(r):
        get_scaled = pltpu.make_async_copy(r.scaled, r.wide_c.at[pl.ds(margin_c * SEG, rows)], r.d_sem.at[0])
        get_scaled.start()
        parts = [getattr(r, f"piece{n}") for n in range(len(pieces))]
        copies = load_weights(parts, member_c, r.weights, r.w_sems)
        incoming_grad, incoming = Stream(r.grad, r.grad_in, r.g_sems), Stream(r.stream, r.stream_in, r.s_sems)
        outgoing = Stream(r.result, r.out, r.o_sems)
        fill_masks(r.mask, r.labels, spacing_c, rows)
        r.total_c[...] = jnp.zeros_like(r.total_c)
        get_scaled.wait()
        fill_ends(r.wide_c, r.turn, margin_c, rows)
        for copy in copies:
            copy.wait()
        for chunk in range(chunks):
            incoming.start(chunk)
            incoming_grad.start(chunk)
        if weights is not None:
            start_weights(r)
        for chunk in range(chunks):
            total = None
            for tap in range(7):
                columns = r.wide_c[pl.ds(chunk * CHUNK + (6 - tap) * spacing_c * SEG, CHUNK), :]
                if tap != 3:
                    columns = columns * lanes4(r.mask[6 - tap, pl.ds(chunk * CHUNK, CHUNK), :])
                term = dot_nn(columns, r.weights[tap])
                total = term if total is None else total + term
            r.back[pl.ds(chunk * CHUNK, CHUNK), :] = total

        @pl.loop(0, chunks)
        def _(chunk):
            incoming.wait(chunk)
            incoming_grad.wait(chunk)
            here = pl.ds(chunk * CHUNK, CHUNK)
            total = r.back[here, :]
            mine = lanes4(own_mask(chunk * CHUNK, CHUNK, span, own))
            _, slope, by_alpha = snake_parts(r.stream_in[here, :], r.vec_c[A1 : A1 + 1, :], r.vec_c[I1 : I1 + 1, :])
            r.total_c[...] += fold(total * by_alpha * mine)
            r.result[here, :] = r.grad_in[here, :] + total * slope
            outgoing.start(chunk)

        r.sums_c[0:8, :] = jnp.concatenate(
            [r.total_c[...].sum(axis=0, keepdims=True), jnp.zeros((7, chans), F32)], axis=0
        )
        start = 1
        for n, (_, count) in enumerate(others):
            r.sums_c[start : start + count, :] = getattr(r, f"other{n}")[0:count, :]
            start += count
        if others:
            r.sums_c[start:16, :] = jnp.zeros((16 - start, chans), F32)
        return outgoing

    def start_weights(r):
        incoming_mid = Stream(r.middle, r.middle_in, r.m_sems)
        for chunk in range(chunks):
            incoming_mid.start(chunk)
        pltpu.make_async_copy(r.wide, r.wide_a, r.x_sem.at[0]).start()

    def go_weights(r):
        me = lax.axis_index("chan")
        incoming, incoming_mid = Stream(r.grad, r.grad_in, r.g_sems), Stream(r.middle, r.middle_in, r.m_sems)
        outgoing = Stream(r.scaled_a, r.scaled_out, r.a_sems)
        grads = r.grad_in if into is None else r.result
        fill_masks(r.mask, r.labels, spacing_a, rows)
        r.total_a[...] = jnp.zeros_like(r.total_a)
        for chunk in range(chunks):
            if into is None:
                incoming.wait(chunk)
            incoming_mid.wait(chunk)
            here = pl.ds(chunk * CHUNK, CHUNK)
            mine = lanes4(own_mask(chunk * CHUNK, CHUNK, span, own))
            grad_here = grads[here, :]
            scaled_here = grad_here * r.vec_a[S1 : S1 + 1, :]
            r.low_t[:, here] = (scaled_here * mine).astype(BF).T
            back = dot_nn(scaled_here.astype(BF), r.w1[...])
            value, slope, by_alpha = snake_parts(
                r.middle_in[here, :], r.vec_a[A2 : A2 + 1, :], r.vec_a[I2 : I2 + 1, :]
            )
            r.second[here, :] = value.astype(BF)
            dmiddle = back * slope
            mine_mid = dmiddle * mine
            r.total_a[0] += fold(grad_here * mine)
            r.total_a[1] += fold(mine_mid)
            r.total_a[2] += fold(back * by_alpha * mine)
            r.scaled_a[here, :] = (dmiddle * r.vec_a[S7 : S7 + 1, :]).astype(BF)
            outgoing.start(chunk)
            r.mid_t[:, here] = (mine_mid * r.vec_a[S7 : S7 + 1, :]).astype(BF).T

        r.sums_a[...] = jnp.concatenate(
            [r.total_a[i].sum(axis=0, keepdims=True) for i in range(3)] + [jnp.zeros((5, chans), F32)], axis=0
        )
        r.results[7] = dot_nn(r.low_t[...], r.second[...]).astype(BF)
        pltpu.make_async_copy(r.wide, r.wide_a, r.x_sem.at[0]).wait()
        targets = (r.keep.at[0], r.send.at[0], r.keep.at[1], r.send.at[1])

        def out(tap, p):
            slot = pl.multiple_of((me ^ p) * part, part)
            return pltpu.make_async_copy(
                r.results.at[tap, pl.ds(slot, part), :], targets[p].at[tap], r.r_sems.at[tap, p]
            )

        for p in range(4):
            out(7, p).start()
        for tap in range(7):
            columns = r.wide_a[pl.ds(tap * (spacing_a * SEG), rows), :]
            if tap != 3:
                columns = columns * lanes4(r.mask[tap])
            r.results[tap] = dot_nn(r.mid_t[...], columns).astype(BF)
            for p in range(4):
                out(tap, p).start()
        for tap in range(8):
            for p in range(4):
                out(tap, p).wait()
        for chunk in range(chunks):
            outgoing.wait(chunk)

    def kernel(*refs):
        r = Names([*ins, *outs, *scratch], refs)
        if into is not None:
            r.vec_c = r.vecs.at[pl.ds(8 * member_c, 8)]
        if weights is not None:
            r.vec_a = r.vecs.at[pl.ds(8 * member_a, 8)]
        outgoing = None
        if into is None:
            incoming = Stream(r.grad, r.grad_in, r.g_sems)
            for chunk in range(chunks):
                incoming.start(chunk)
            start_weights(r)
        else:
            outgoing = go_into(r)
        if weights is not None:
            go_weights(r)
        if outgoing is not None:
            for chunk in range(chunks):
                outgoing.wait(chunk)

    results = pl.pallas_call(
        kernel,
        out_shape=[shape for shape, _ in outs.values()],
        in_specs=[spec for _, spec in ins.values()],
        out_specs=[spec for _, spec in outs.values()],
        scratch_shapes=list(scratch.values()),
        compiler_params=pltpu.CompilerParams(vmem_limit_bytes=VMEM),
        cost_estimate=cost(micros),
        name=name,
    )(*[value for value, _ in ins.values()])
    return dict(zip(outs, results, strict=True))


def halve(dilated, pointwise):
    units, _, part, chans = dilated.shape

    def kernel(d_ref, q_ref, f0, f1, f2, f3, held, sems, out_sems):
        side = lax.axis_index("frames") & 1
        copies = []
        for u in range(units):
            copies.append(pltpu.make_async_copy(d_ref.at[u], held.at[u, pl.ds(0, 7)], sems.at[u]))
            copies.append(pltpu.make_async_copy(q_ref.at[u], held.at[u, 7], sems.at[units + u]))
        for copy in copies:
            copy.start()
        outs = [
            pltpu.make_async_copy(held.at[0, pl.ds(side * 4, 4)], f0, out_sems.at[0]),
            pltpu.make_async_copy(held.at[1, pl.ds(side * 4, 4)], f1, out_sems.at[1]),
            pltpu.make_async_copy(held.at[2, pl.ds(0, 4)], f2, out_sems.at[2]),
            pltpu.make_async_copy(held.at[2, pl.ds(4, 4)], f3, out_sems.at[3]),
        ]
        for u, out in zip((0, 1, 2, 2), outs, strict=True):
            if u == 2 and out is outs[3]:
                out.start()
                continue
            copies[2 * u].wait()
            copies[2 * u + 1].wait()
            out.start()
        for out in outs:
            out.wait()

    held = pl.BlockSpec(memory_space=pl.ANY)
    return pl.pallas_call(
        kernel,
        out_shape=[
            jax.ShapeDtypeStruct((taps, part, chans), BF) for taps in (4, 4, 4, 4)
        ],
        in_specs=[held] * 2,
        out_specs=[held] * 4,
        scratch_shapes=[
            pltpu.VMEM((units, 8, part, chans), BF),
            pltpu.SemaphoreType.DMA((2 * units,)),
            pltpu.SemaphoreType.DMA((units + 1,)),
        ],
        compiler_params=pltpu.CompilerParams(vmem_limit_bytes=VMEM),
        cost_estimate=cost(0.1),
        name="halve",
    )(dilated, pointwise)


def cut(signal, packed, pulled, codes):
    part, extent = signal.shape
    own = extent // 4
    count = own + 2 * HALO
    own_frames = pulled.shape[1] // 4

    def kernel(s_ref, v_ref, u_ref, c_ref, p0, p1, p2, p3, e0, e1, e2, e3, low):
        me = lax.axis_index("chan")
        low[...] = s_ref[...].astype(BF)
        vectors3 = terms(v_ref[...], 3)
        for p, (piece, end) in enumerate(((p0, e0), (p1, e1), (p2, e2), (p3, e3))):
            owner = me ^ p
            start = pl.multiple_of(owner * own, own)
            piece[:, HALO : HALO + own] = low[:, pl.ds(start, own)]
            before = pl.multiple_of(jnp.maximum(start - HALO, 0), HALO)
            piece[:, 0:HALO] = low[:, pl.ds(before, HALO)]
            behind = pl.multiple_of(jnp.minimum(start + own, extent - HALO), HALO)
            piece[:, HALO + own : count] = low[:, pl.ds(behind, HALO)]
            frames = pl.ds(pl.multiple_of(owner * own_frames, own_frames), own_frames)
            pulled2 = jnp.concatenate([u_ref[:, frames], jnp.zeros((8, own_frames), F32)], axis=0)
            high = pulled2.astype(BF).astype(F32)
            both = jnp.concatenate([high[0:8], (pulled2 - high)[0:8]], axis=0).astype(BF)
            piece[:, count : count + 128] = jnp.concatenate(
                [*vectors3, both, jnp.zeros((128 - 3 * packed.shape[0] - 16, 128), BF)], axis=0
            )
            outer = pl.multiple_of(jnp.where(owner == 0, extent - HALO, 0), HALO)
            end[0:part, :] = low[:, pl.ds(outer, HALO)]
        first, last = c_ref[0:1, :], c_ref[codes.shape[0] - 1 : codes.shape[0], :]
        e0[part : part + 16, :] = jnp.concatenate(
            [row.astype(F32) for row in (first >> 7, first & 127, last >> 7, last & 127)] + [jnp.zeros((12, 128), F32)],
            axis=0,
        ).astype(BF)

    whole = pl.BlockSpec(memory_space=pltpu.VMEM)
    outs = pl.pallas_call(
        kernel,
        out_shape=[jax.ShapeDtypeStruct((part, count + 128), BF)] * 4
        + [jax.ShapeDtypeStruct((part + 16, HALO), BF)]
        + [jax.ShapeDtypeStruct((part, HALO), BF)] * 3,
        in_specs=[whole] * 4,
        out_specs=[whole] * 8,
        scratch_shapes=[pltpu.VMEM((part, extent), BF)],
        compiler_params=pltpu.CompilerParams(vmem_limit_bytes=VMEM),
        cost_estimate=cost(0.1),
        name="cut",
    )(signal, packed, pulled, codes)
    return outs[0:4], outs[4:8]


def enter(pieces, ends, lines, own):
    part = pieces[0].shape[0]
    count = own + 2 * HALO
    span = count // SEG

    def kernel(p0, p1, p2, p3, e0, e1, e2, e3, out_ref, vec_ref, pull_ref, code_ref, turned, placed):
        me = lax.axis_index("chan")
        pulled = jnp.zeros((8, part), F32)
        for p, (piece, end) in enumerate(((p0, e0), (p1, e1), (p2, e2), (p3, e3))):
            turned[...] = piece[:, 0:count].astype(F32).T

            @pl.when(me == 0)
            def _(end=end):
                turned[0:HALO, :] = end[0:part, :].astype(F32).T

            @pl.when(me == 3)
            def _(end=end):
                turned[HALO + own : count, :] = end[0:part, :].astype(F32).T

            for a in range(SEG):
                placed[pl.ds(a, span, stride=SEG), :] = turned[pl.ds(a * span, span), :]
            lanes = pl.ds(pl.multiple_of((me ^ p) * part, part), part)
            out_ref[:, lanes] = placed[...]
            tile = piece[:, count : count + 128].astype(F32)
            vec_ref[:, lanes] = tile[0:lines] + tile[lines : 2 * lines] + tile[2 * lines : 3 * lines]
            pulled = pulled + tile[3 * lines : 3 * lines + 8] + tile[3 * lines + 8 : 3 * lines + 16]
        pull_ref[...] = pulled
        tile = e0[part : part + 16, :].astype(F32)
        code_ref[...] = jnp.concatenate(
            [tile[0:1] * 128.0 + tile[1:2], tile[2:3] * 128.0 + tile[3:4], jnp.zeros((6, 128), F32)], axis=0
        )

    whole = pl.BlockSpec(memory_space=pltpu.VMEM)
    return pl.pallas_call(
        kernel,
        out_shape=[
            jax.ShapeDtypeStruct((count, 4 * part), F32),
            jax.ShapeDtypeStruct((lines, 4 * part), F32),
            jax.ShapeDtypeStruct((8, part), F32),
            jax.ShapeDtypeStruct((8, 128), F32),
        ],
        in_specs=[whole] * 8,
        out_specs=[whole] * 4,
        scratch_shapes=[pltpu.VMEM((count, part), F32)] * 2,
        compiler_params=pltpu.CompilerParams(vmem_limit_bytes=VMEM),
        cost_estimate=cost(0.1),
        name="enter",
    )(*pieces, *ends)


def lane_sums(squares):
    return jnp.sum(squares.T, axis=0, keepdims=True)


def vectors(dilated, pointwise, gains7, gains1, bias7, bias1, first, second, last, project, cotangent):
    units, taps, part, chans = dilated.shape

    def kernel(d_ref, q_ref, g7, g1, b7, b1, a1, a2, a3, p_ref, t_ref, out_ref, pulled):
        out_ref[...] = jnp.zeros_like(out_ref)
        for u in range(units):
            total = jnp.zeros((part, 128), F32)
            for tap in range(taps):
                value = d_ref[u, tap].astype(F32)
                value = value * value
                for g in range(chans // 128):
                    total = total + value[:, g * 128 : (g + 1) * 128]
            value = q_ref[u].astype(F32)
            value = value * value
            total1 = jnp.zeros((part, 128), F32)
            for g in range(chans // 128):
                total1 = total1 + value[:, g * 128 : (g + 1) * 128]
            here = slice(u, u + 1)
            rows = (
                a1[here, :] * (1.0 / jnp.pi),
                1.0 / a1[here, :],
                a2[here, :] * (1.0 / jnp.pi),
                1.0 / a2[here, :],
                g7[here, :] * lax.rsqrt(lane_sums(total) + NORM_EPS),
                b7[here, :],
                g1[here, :] * lax.rsqrt(lane_sums(total1) + NORM_EPS),
                b1[here, :],
            )
            for n, row in enumerate(rows):
                out_ref[8 * u + n : 8 * u + n + 1, :] = row
        out_ref[8 * units : 8 * units + 1, :] = a3[...] * (1.0 / jnp.pi)
        out_ref[8 * units + 1 : 8 * units + 2, :] = 1.0 / a3[...]
        pulled[...] = dot_tn(p_ref[...], t_ref[...])[0:8, :]

    whole = pl.BlockSpec(memory_space=pltpu.VMEM)
    return pl.pallas_call(
        kernel,
        out_shape=[
            jax.ShapeDtypeStruct((8 * units + 8, part), F32),
            jax.ShapeDtypeStruct((8, cotangent.shape[1]), F32),
        ],
        in_specs=[whole] * 11,
        out_specs=[whole] * 2,
        compiler_params=pltpu.CompilerParams(vmem_limit_bytes=VMEM),
        cost_estimate=cost(0.1),
        name="vectors",
    )(dilated, pointwise, gains7, gains1, bias7, bias1, first, second, last[None], project, cotangent)


def merge_strided(strided, gains, bias, project):
    taps, rows, chans = strided.shape

    def kernel(w_ref, g_ref, b_ref, p_ref, out_ref, norm_ref):
        total = jnp.zeros((rows, 128), F32)
        for tap in range(taps):
            value = w_ref[tap].astype(F32)
            value = value * value
            for g in range(chans // 128):
                total = total + value[:, g * 128 : (g + 1) * 128]
        inverse = lax.rsqrt(lane_sums(total) + NORM_EPS)
        scale = g_ref[...] * inverse
        norm_ref[...] = jnp.zeros_like(norm_ref)
        norm_ref[0:1, :] = scale
        norm_ref[1:2, :] = scale * inverse * inverse
        norm_ref[2:3, :] = inverse
        plain = p_ref[...].astype(F32)
        scaled = plain * scale
        split = jnp.concatenate(terms(scaled, 3), axis=0)
        for tap in range(taps):
            three = dot_nn(split, w_ref[tap])
            out_ref[8 * tap : 8 * tap + 8, :] = three[0:8] + three[8:16] + three[16:24]
        shift = jnp.sum(plain * b_ref[...], axis=1, keepdims=True)
        out_ref[8 * taps : 8 * taps + 8, :] = jnp.broadcast_to(shift, (8, chans))

    whole = pl.BlockSpec(memory_space=pltpu.VMEM)
    return pl.pallas_call(
        kernel,
        out_shape=[jax.ShapeDtypeStruct((8 * taps + 8, chans), F32), jax.ShapeDtypeStruct((8, rows), F32)],
        in_specs=[whole] * 4,
        out_specs=[whole] * 2,
        compiler_params=pltpu.CompilerParams(vmem_limit_bytes=VMEM),
        cost_estimate=cost(5),
        name="merge_strided",
    )(strided, gains[None], bias[None], project)


def look_up(wanted, codebook, project, cotangent, near_count):
    count = wanted.shape[0]
    codes = codebook.shape[1]
    rows, frames = cotangent.shape
    step = 512

    def kernel(i_ref, c_ref, p_ref, t_ref, near_ref, out_ref, sum_ref, found):
        found[...] = jnp.zeros_like(found)
        lane = lax.broadcasted_iota(jnp.int32, (count, 128), 1)

        @pl.loop(0, codes, step=step)
        def _(start):
            start = pl.multiple_of(start, step)
            book = c_ref[:, pl.ds(start, step)]
            book = book * lax.rsqrt(jnp.sum(book * book, axis=0, keepdims=True) + 1.0)
            table = jnp.concatenate(terms(book, 3) + [jnp.zeros((104, step), BF)], axis=0)
            wants = i_ref[...] - start
            hot = jnp.concatenate(
                [jnp.where(wants == lane + g * 128, 1.0, 0.0).astype(BF) for g in range(step // 128)], axis=1
            )
            found[...] += dot_nt(hot, table)

        total = found[...]
        total = total + pltpu.roll(total, 120, 1) + pltpu.roll(total, 112, 1)
        total = jnp.where(lane < 8, total, 0.0)
        near_ref[...] = total[:near_count]
        low = jnp.where((lane >= 8) & (lane < 11), 1.0, total)[near_count:].astype(BF)
        out_ref[...] = dot_nt(p_ref[...], low)
        sum_ref[...] = dot_nn(t_ref[...], low)

    whole = pl.BlockSpec(memory_space=pltpu.VMEM)
    return pl.pallas_call(
        kernel,
        out_shape=[
            jax.ShapeDtypeStruct((near_count, 128), F32),
            jax.ShapeDtypeStruct((rows, frames), F32),
            jax.ShapeDtypeStruct((rows, 128), F32),
        ],
        in_specs=[whole] * 4,
        out_specs=[whole] * 3,
        scratch_shapes=[pltpu.VMEM((count, 128), F32)],
        compiler_params=pltpu.CompilerParams(vmem_limit_bytes=VMEM),
        cost_estimate=cost(0.1),
        name="look_up",
    )(wanted, codebook, project, cotangent)


def code_payload(dchosen, latent, mixed_grad, near, place, refill, after_this):
    count = dchosen.shape[0]
    taps, _, chans = mixed_grad.shape
    blocks, step = refill.shape

    rows = 24 * blocks + 8 * taps
    quarter = rows // 4

    def kernel(d_ref, l_ref, m_ref, n_ref, p_ref, r_ref, _, o0, o1, o2, o3, out_ref):
        lane = lax.broadcasted_iota(jnp.int32, (count, 128), 1)
        owned = p_ref[...] >= 0
        grads = d_ref[...]
        high = grads.astype(BF).astype(F32)
        left = high + pltpu.roll(grads - high, 8, 1) + jnp.where((lane == 16) & owned, 1.0, 0.0)
        left = left.astype(BF)
        right = l_ref[...].astype(BF)

        @pl.loop(0, blocks)
        def _(block):
            wants = n_ref[...] - block * step
            hot = jnp.concatenate(
                [jnp.where(wants == lane + g * 128, 1.0, 0.0).astype(BF) for g in range(step // 128)], axis=1
            )
            into = dot_tn(left, hot)
            wanted = r_ref[pl.ds(block, 1), :]
            hot = jnp.concatenate(
                [
                    jnp.where(p_ref[...] == wanted[:, g * 128 : (g + 1) * 128], 1.0, 0.0).astype(BF)
                    for g in range(step // 128)
                ],
                axis=1,
            )
            picked = dot_tn(right, hot)
            start = pl.multiple_of(block * 24, 8)
            out_ref[pl.ds(start, 24), :] = jnp.concatenate(
                [into[0:8] + into[8:16], picked[0:8], into[16:24]], axis=0
            )

        for tap in range(taps):
            out_ref[24 * blocks + 8 * tap : 24 * blocks + 8 * tap + 8, :] = m_ref[tap]
        me = lax.axis_index("chan")
        for p, piece in enumerate((o0, o1, o2, o3)):
            piece[...] = out_ref[pl.ds(pl.multiple_of((me ^ p) * quarter, 8), quarter), :].astype(BF)

    whole = pl.BlockSpec(memory_space=pltpu.VMEM)
    held = pl.BlockSpec(memory_space=pl.ANY)
    return pl.pallas_call(
        kernel,
        out_shape=[jax.ShapeDtypeStruct((quarter, chans), BF)] * 4,
        in_specs=[whole] * 6 + [held],
        out_specs=[whole] * 4,
        scratch_shapes=[pltpu.VMEM((rows, chans), F32)],
        compiler_params=pltpu.CompilerParams(vmem_limit_bytes=VMEM),
        cost_estimate=cost(0.1),
        name="code_payload",
    )(dchosen, latent, mixed_grad, near, place, refill, after_this)


def strided_meet(strided, mixed_grad, project, norms):
    taps, rows, chans = strided.shape
    group = 4

    def kernel(w_ref, m_ref, p_ref, n_ref, vec_ref, factor_ref, total):
        step = pl.program_id(0)

        @pl.when(step == 0)
        def _():
            total[...] = jnp.zeros_like(total)

        meeting = total[...]
        for tap in range(group):
            meeting = meeting + dot_nt(m_ref[tap], w_ref[tap])
        total[...] = meeting

        @pl.when(step == taps // group - 1)
        def _():
            plain = p_ref[...].astype(F32)
            along = jnp.sum(plain * total[...], axis=0, keepdims=True)
            vec_ref[...] = jnp.zeros_like(vec_ref)
            vec_ref[0:8, :] = total[...] * n_ref[0:1, :]
            vec_ref[8:9, :] = along * n_ref[2:3, :]
            factor_ref[...] = jnp.broadcast_to(along * n_ref[1:2, :], (128, rows)).T

    whole = pl.BlockSpec(memory_space=pltpu.VMEM)
    return pl.pallas_call(
        kernel,
        grid=(taps // group,),
        out_shape=[jax.ShapeDtypeStruct((16, rows), F32), jax.ShapeDtypeStruct((rows, 128), F32)],
        in_specs=[
            pl.BlockSpec((group, rows, chans), lambda step: (step, 0, 0)),
            pl.BlockSpec((group, 8, chans), lambda step: (step, 0, 0)),
            whole,
            whole,
        ],
        out_specs=[
            pl.BlockSpec((16, rows), lambda step: (0, 0)),
            pl.BlockSpec((rows, 128), lambda step: (0, 0)),
        ],
        scratch_shapes=[pltpu.VMEM((8, rows), F32)],
        compiler_params=pltpu.CompilerParams(vmem_limit_bytes=VMEM),
        cost_estimate=cost(0.1),
        name="strided_meet",
    )(strided, mixed_grad, project, norms)


def strided_back(strided, mixed_grad, project, norms, factors):
    taps, rows, chans = strided.shape
    group = 4

    def kernel(w_ref, m_ref, p_ref, n_ref, f_ref, out_ref):
        split = jnp.concatenate(terms(p_ref[...].astype(F32) * n_ref[0:1, :], 3), axis=0)
        for tap in range(group):
            three = jnp.concatenate([m_ref[tap]] * 3, axis=0)
            out_ref[tap] = dot_tn(split, three) - w_ref[tap].astype(F32) * lanes4(f_ref[...])

    whole = pl.BlockSpec(memory_space=pltpu.VMEM)
    return pl.pallas_call(
        kernel,
        grid=(taps // group,),
        out_shape=jax.ShapeDtypeStruct((taps, rows, chans), F32),
        in_specs=[
            pl.BlockSpec((group, rows, chans), lambda step: (step, 0, 0)),
            pl.BlockSpec((group, 8, chans), lambda step: (step, 0, 0)),
            whole,
            whole,
            whole,
        ],
        out_specs=pl.BlockSpec((group, rows, chans), lambda step: (step, 0, 0)),
        compiler_params=pltpu.CompilerParams(vmem_limit_bytes=VMEM),
        cost_estimate=cost(0.1),
        name="strided_back",
    )(strided, mixed_grad, project, norms, factors)


def norm_back(chains, dilated, pointwise, gains, members, earlier):
    units, _, part, chans = dilated.shape
    count = len(members)
    others = earlier[2:]

    def kernel(*refs):
        halves, refs = refs[: 2 * count], refs[2 * count :]
        w_refs, q_refs, g_refs = (refs[n * count : (n + 1) * count] for n in range(3))
        out7, out1, out_g7, out_g1, helds, res7, res1, sems = refs[-8:]
        given = refs[3 * count + 2 : 3 * count + 2 + len(others)] if earlier else ()
        outs = []

        def send(value, target):
            outs.append(pltpu.make_async_copy(value, target, sems.at[len(outs)]))
            outs[-1].start()

        for n, member in enumerate(members):
            rows = halves[2 * n].shape[0]
            upper = bit_of(*chains[n].last)
            helds[n, pl.ds(pl.multiple_of(upper * rows, 16), rows), :] = halves[2 * n][...]
            helds[n, pl.ds(pl.multiple_of((1 - upper) * rows, 16), rows), :] = halves[2 * n + 1][...]

            def grad_of(tap, n=n):
                return helds[n, tap * part : (tap + 1) * part, :].astype(F32)

            def weight_of(tap, n=n):
                return (q_refs[n][0] if tap == 7 else w_refs[n][0, tap]).astype(F32)

            for which, taps in enumerate((range(7), (7,))):
                square = jnp.zeros((part, 128), F32)
                along = jnp.zeros((part, 128), F32)
                for tap in taps:
                    value, grad = weight_of(tap), grad_of(tap)
                    both, value2 = value * grad, value * value
                    for g in range(chans // 128):
                        cols = slice(g * 128, (g + 1) * 128)
                        square = square + value2[:, cols]
                        along = along + both[:, cols]
                square_sum = jnp.sum(square, axis=1, keepdims=True) + NORM_EPS
                factor = jnp.sum(along, axis=1, keepdims=True) / square_sum
                row = lane_sums(along) / g_refs[n][0, which : which + 1, :]
                out_g = (out_g7, out_g1)[which]
                place = member if others else 0
                out_g[place : place + 1, :] = row
                for other in range(len(others) // 2):
                    place = units - 1 - other
                    out_g[place : place + 1, :] = given[2 * other + which][...]
                for tap in taps:
                    target = res1.at[n] if tap == 7 else res7.at[n, tap]
                    target[...] = grad_of(tap) - weight_of(tap) * factor
                    send(target, out1.at[member] if tap == 7 else out7.at[member, tap])
        for copy in outs:
            copy.wait()

    whole = pl.BlockSpec(memory_space=pltpu.VMEM)
    held = pl.BlockSpec(memory_space=pl.ANY)

    def block(shape, member):
        return pl.BlockSpec((1,) + shape, lambda step: (member,) + (0,) * len(shape))

    return pl.pallas_call(
        kernel,
        grid=(1,),
        out_shape=[
            jax.ShapeDtypeStruct((units, 7, part, chans), F32),
            jax.ShapeDtypeStruct((units, part, chans), F32),
        ]
        + [jax.ShapeDtypeStruct((units if others else 1, part), F32)] * 2,
        in_specs=[whole] * (2 * count)
        + [block((7, part, chans), member) for member in members]
        + [block((part, chans), member) for member in members]
        + [block((2, part), member) for member in members]
        + [held] * len(earlier[:2])
        + [whole] * len(others),
        out_specs=[held, held, whole, whole],
        input_output_aliases={5 * count + n: n for n in range(len(earlier[:2]))},
        scratch_shapes=[
            pltpu.VMEM((count, max(2 * chain.whole[0].shape[0] for chain in chains), chans), BF),
            pltpu.VMEM((count, 7, part, chans), F32),
            pltpu.VMEM((count, part, chans), F32),
            pltpu.SemaphoreType.DMA((8 * count,)),
        ],
        compiler_params=pltpu.CompilerParams(vmem_limit_bytes=VMEM),
        cost_estimate=cost(0.1),
        name="norm_back",
    )(*[half for chain in chains for half in chain.whole], *[dilated] * count, *[pointwise] * count, *[gains] * count, *earlier)


def leave(grad, own):
    rows, chans = grad.shape
    span = rows // SEG
    part = chans // 4

    def kernel(g_ref, o0, o1, o2, o3, ordered, placed):
        me = lax.axis_index("chan")
        for p, out in enumerate((o0, o1, o2, o3)):
            placed[...] = g_ref[:, pl.ds(pl.multiple_of((me ^ p) * part, part), part)]
            for a in range(SEG):
                ordered[pl.ds(a * span, span), :] = placed[pl.ds(a, span, stride=SEG), :]
            out[...] = ordered[pl.ds(HALO, own), :].T.astype(out.dtype)

    whole = pl.BlockSpec(memory_space=pltpu.VMEM)
    return pl.pallas_call(
        kernel,
        out_shape=[jax.ShapeDtypeStruct((part, own), F32)] + [jax.ShapeDtypeStruct((part, own), BF)] * 3,
        in_specs=[whole],
        out_specs=[whole] * 4,
        scratch_shapes=[pltpu.VMEM((rows, part), F32)] * 2,
        compiler_params=pltpu.CompilerParams(vmem_limit_bytes=VMEM),
        cost_estimate=cost(0.1),
        name="leave",
    )(grad)


def settle(pieces):
    part, own = pieces[0].shape

    def kernel(p0, p1, p2, p3, out_ref):
        me = lax.axis_index("chan")
        for p, piece in enumerate((p0, p1, p2, p3)):
            out_ref[:, pl.ds(pl.multiple_of((me ^ p) * own, own), own)] = piece[...].astype(F32)

    whole = pl.BlockSpec(memory_space=pltpu.VMEM)
    return pl.pallas_call(
        kernel,
        out_shape=jax.ShapeDtypeStruct((part, 4 * own), F32),
        in_specs=[whole] * 4,
        out_specs=whole,
        compiler_params=pltpu.CompilerParams(vmem_limit_bytes=VMEM),
        cost_estimate=cost(0.1),
        name="settle",
    )(*pieces)


def bottleneck(stream, merged, bias, vecs, labels, chosen, picked_grad, own):
    rows, chans = stream.shape
    span = rows // SEG
    groups = span // STRIDE
    count = groups * SEG
    taps = merged[0].shape[0] // 8 - 1
    edge = 16 * SEG
    turn_row = vecs.shape[0] - 8

    def kernel(
        s_ref, wa_ref, wb_ref, bias_ref, v_ref, l_ref, c_ref, o_ref, g_ref, lat_ref, dch_ref, m_ref, sum_ref,
        q_ref, wide, full, codes, sums,
    ):
        blank = jnp.zeros((104, chans), BF)
        for tap in range(taps):
            here = slice(8 * tap, 8 * tap + 8)
            high, rest = terms(wa_ref[here, :] + wb_ref[here, :], 2)
            q_ref[tap] = jnp.concatenate([high, high, rest, blank], axis=0)
        shift = jnp.sum(
            jnp.where(
                lax.broadcasted_iota(jnp.int32, (8, 128), 0) == lax.broadcasted_iota(jnp.int32, (8, 128), 1),
                wa_ref[8 * taps : 8 * taps + 8, 0:128] + wb_ref[8 * taps : 8 * taps + 8, 0:128],
                0.0,
            ),
            axis=0,
            keepdims=True,
        )

        @pl.loop(0, rows, step=CHUNK)
        def _(start):
            start = pl.multiple_of(start, CHUNK)
            act = snake(s_ref[pl.ds(start, CHUNK), :], v_ref[turn_row : turn_row + 1, :], v_ref[turn_row + 1 : turn_row + 2, :])
            full[pl.ds(8 + start, CHUNK), :] = act
            wide[pl.ds(edge + start, CHUNK), :] = act.astype(BF)

        wide[pl.ds(0, edge), :] = full[pl.ds(8 + rows - edge - 1, edge), :].astype(BF)
        wide[pl.ds(edge + rows, edge), :] = full[pl.ds(8 + 1, edge), :].astype(BF)

        def tap_mask(tap, first, amount):
            base = (LEAD + first * STRIDE) * SEG
            pieces = []
            for g in range(amount):
                start = base + g * STRIDE * SEG
                there = l_ref[pl.ds(start + (tap - 4) * SEG, SEG), :]
                pieces.append(jnp.where(there == l_ref[pl.ds(start, SEG), :], 1.0, 0.0).astype(F32))
            return jnp.concatenate(pieces, axis=0)

        def tap_columns(tap):
            base = edge + (tap - 4) * SEG
            picked = jnp.concatenate(
                [wide[pl.ds(base + g * STRIDE * SEG, SEG), :] for g in range(groups)], axis=0
            )
            return picked * lanes4(tap_mask(tap, 0, groups).astype(BF))

        total = jnp.zeros((count, 128), F32)
        for tap in range(taps):
            total = total + dot_nt(tap_columns(tap), q_ref[tap])
        lane = lax.broadcasted_iota(jnp.int32, (count, 128), 1)
        latent = jnp.where(lane < 8, total + pltpu.roll(total, 112, 1) + shift + bias_ref[...], 0.0)
        lat_ref[...] = latent
        inverse = lax.rsqrt(jnp.sum(latent * latent, axis=1, keepdims=True) + 1.0)
        normed = latent * inverse
        spread = (2.0 * COMMIT) * (normed - c_ref[...])
        row = lax.broadcasted_iota(jnp.int32, (count, 128), 0)
        place = (row & (SEG - 1)) * groups + (row >> 4)
        mine = (place >= HALO // STRIDE) & (place < (HALO + own) // STRIDE)
        dch_ref[...] = jnp.where(mine, o_ref[...] - spread, 0.0)
        dlatent = (spread - normed * jnp.sum(normed * spread, axis=1, keepdims=True)) * inverse

        def split(values):
            high = values.astype(BF).astype(F32)
            return high + pltpu.roll(values - high, 8, 1), pltpu.roll(high, 16, 1)

        dmine = jnp.where(mine, dlatent, 0.0)
        sum_ref[1:2, :] = jnp.concatenate([jnp.sum(dmine, axis=0, keepdims=True)] * 4, axis=1)
        pair, _unused = split(dmine)
        pair = pair.astype(BF)
        for tap in range(taps):
            both = dot_tn(pair, tap_columns(tap))
            m_ref[tap] = both[0:8, :] + both[8:16, :]

        pair, again = split(dlatent)
        codes[pl.ds(8 + SEG, count), :] = pair + again
        codes[pl.ds(8, SEG), :] = codes[pl.ds(8 + count - 1, SEG), :]
        codes[pl.ds(8 + SEG + count, SEG), :] = codes[pl.ds(8 + SEG + 1, SEG), :]
        sums[...] = jnp.zeros_like(sums)
        for rest in range(STRIDE):
            total = None
            for tap in (rest - 4, rest + 4, rest + 12):
                if 0 <= tap < taps:
                    hop = (tap - 4 - rest) // STRIDE
                    left = codes[pl.ds(8 + SEG - hop * SEG, count), :] * tap_mask(tap, -hop, groups)
                    term = dot_nn(left.astype(BF), q_ref[tap])
                    total = term if total is None else total + term
            for g in range(groups):
                here = pl.ds((g * STRIDE + rest) * SEG, SEG)
                part = total[g * SEG : (g + 1) * SEG, :]
                value, slope, by_alpha = snake_parts(s_ref[here, :], v_ref[turn_row : turn_row + 1, :], v_ref[turn_row + 1 : turn_row + 2, :])
                g_ref[here, :] = part * slope
                mask = lanes4(own_mask((g * STRIDE + rest) * SEG, SEG, span, own))
                sums[...] += fold(part * by_alpha * mask)
        sum_ref[0:1, :] = sums[...].sum(axis=0, keepdims=True)
        sum_ref[2:8, :] = jnp.zeros((6, chans), F32)

    whole = pl.BlockSpec(memory_space=pltpu.VMEM)
    return pl.pallas_call(
        kernel,
        out_shape=[
            jax.ShapeDtypeStruct((rows, chans), F32),
            jax.ShapeDtypeStruct((count, 128), F32),
            jax.ShapeDtypeStruct((count, 128), F32),
            jax.ShapeDtypeStruct((taps, 8, chans), F32),
            jax.ShapeDtypeStruct((8, chans), F32),
        ],
        in_specs=[whole] * 8,
        out_specs=[whole] * 5,
        scratch_shapes=[
            pltpu.VMEM((taps, 128, chans), BF),
            pltpu.VMEM((rows + 2 * edge, chans), BF),
            pltpu.VMEM((rows + 16, chans), F32),
            pltpu.VMEM((count + 2 * SEG + 16, 128), F32),
            pltpu.VMEM((8, chans), F32),
        ],
        compiler_params=pltpu.CompilerParams(vmem_limit_bytes=VMEM),
        cost_estimate=cost(11),
        name="bottleneck",
    )(stream, *merged, bias, vecs, labels, chosen, picked_grad)


def swap(value, axis, bit):
    count = lax.axis_size(axis)
    return lax.ppermute(value, axis, [(i, i ^ (1 << bit)) for i in range(count)])


def bits_of(axis):
    count = lax.axis_size(axis)
    return [(axis, bit) for bit in range(count.bit_length() - 1)]


def total_over(value, steps):
    for axis, bit in steps:
        value = value + swap(value, axis, bit)
    return value


def bit_of(axis, bit):
    return (lax.axis_index(axis) >> bit) & 1


def halves_of(value, step):
    axis, bit = step
    half = value.shape[0] // 2
    mine = bit_of(axis, bit)
    kept = lax.dynamic_slice_in_dim(value, mine * half, half)
    return kept, lax.dynamic_slice_in_dim(value, (1 - mine) * half, half).astype(BF)


def add_up(kept, got):
    return (kept.astype(F32) + got.astype(F32)).astype(BF)


def sum_halves(terms_in, rows, step, micros=0.1):
    chans = terms_in[0][0][0].shape[-1]
    flat = [ref for block in terms_in for ref, _ in block]
    half = rows // 2 if step else rows

    def kernel(*refs):
        refs = list(refs)
        ins = [refs.pop(0) for _ in flat]
        outs = refs[: 2 if step else 1]
        total, sems = refs[-2:] if step else (outs[0], None)
        at, start = 0, 0
        for block in terms_in:
            value = None
            for _, index in block:
                ref = ins[at] if index is None else ins[at].at[index]
                term = ref[...].astype(F32)
                value = term if value is None else value + term
                at += 1
            value = value.astype(BF).reshape(-1, chans)
            total[start : start + value.shape[0], :] = value
            start += value.shape[0]
        if start < rows:
            total[start:rows, :] = jnp.zeros((rows - start, chans), BF)
        if step:
            mine = bit_of(*step)
            copies = []
            for n, out in enumerate(outs):
                place = pl.multiple_of((mine if n == 0 else 1 - mine) * half, 16)
                copies.append(pltpu.make_async_copy(total.at[pl.ds(place, half)], out, sems.at[n]))
                copies[-1].start()
            for copy in copies:
                copy.wait()

    def spec(ref, index):
        if index is None:
            return pl.BlockSpec(memory_space=pltpu.VMEM)
        return pl.BlockSpec((1,) + ref.shape[1:], lambda n: (index,) + (0,) * (ref.ndim - 1))

    flat_pairs = [pair for block in terms_in for pair in block]
    terms_in = [[(ref, None if index is None else 0) for ref, index in block] for block in terms_in]
    return pl.pallas_call(
        kernel,
        grid=(1,),
        out_shape=[jax.ShapeDtypeStruct((half, chans), BF)] * (2 if step else 1),
        in_specs=[spec(ref, index) for ref, index in flat_pairs],
        out_specs=[pl.BlockSpec(memory_space=pl.ANY)] * 2 if step else [pl.BlockSpec(memory_space=pltpu.VMEM)],
        scratch_shapes=[pltpu.VMEM((rows, chans), BF), pltpu.SemaphoreType.DMA((2,))] if step else [],
        compiler_params=pltpu.CompilerParams(vmem_limit_bytes=VMEM),
        cost_estimate=cost(micros),
        name="sum_halves",
    )(*flat)


def join(mine, got, step):
    rows, chans = mine.shape

    def kernel(m_ref, g_ref, out_ref):
        upper = bit_of(*step)
        out_ref[pl.ds(pl.multiple_of(upper * rows, 16), rows), :] = m_ref[...]
        out_ref[pl.ds(pl.multiple_of((1 - upper) * rows, 16), rows), :] = g_ref[...]

    whole = pl.BlockSpec(memory_space=pltpu.VMEM)
    return pl.pallas_call(
        kernel,
        out_shape=jax.ShapeDtypeStruct((2 * rows, chans), BF),
        in_specs=[whole] * 2,
        out_specs=whole,
        compiler_params=pltpu.CompilerParams(vmem_limit_bytes=VMEM),
        cost_estimate=cost(0.1),
        name="join",
    )(mine, got)


class Chain:
    def __init__(self, terms_in, rows, steps, micros=0.1):
        self.adds, self.joins = list(steps), list(reversed(steps))
        self.rows = rows
        self.kept, self.sent = sum_halves(terms_in, rows, self.adds[0], micros)
        self.whole = None
        self.left = 2 * len(steps)
        self.start()

    def start(self):
        self.got = swap(self.sent, *(self.adds[0] if self.adds else self.joins[0]))

    def step(self, token):
        got = after(self.got, token)
        self.left -= 1
        if self.adds:
            self.adds.pop(0)
            self.rows //= 2
            terms_in = [[(self.kept, None), (got, None)]]
            if self.adds:
                self.kept, self.sent = sum_halves(terms_in, self.rows, self.adds[0])
            else:
                self.sent = sum_halves(terms_in, self.rows, None)[0]
        elif self.left:
            self.sent = join(self.sent, got, self.joins.pop(0))
        else:
            self.whole = (self.sent, got)
            self.last = self.joins.pop(0)
        if self.left:
            self.start()
        return self.sent

    def upper(self):
        return jnp.where(bit_of(*self.last) == 1, *self.whole)


def after(value, *others):
    return lax.optimization_barrier((value, *others))[0]


def to_peer(value, peer):
    return lax.ppermute(value, "chan", [(i, i ^ peer) for i in range(4)])


def local(
    signal,
    dilated_dirs,
    dilated_gains,
    dilated_bias,
    snake_first,
    snake_second,
    pointwise_dirs,
    pointwise_gains,
    pointwise_bias,
    snake_last,
    strided_dirs,
    strided_gains,
    strided_bias,
    latent_proj,
    latent_bias,
    codebook,
    output_proj,
    output_bias,
    utterances,
    code_index,
    refill_index,
    cotangent,
):
    part, extent = signal.shape
    chans = 4 * part
    own = extent // 4
    frames = code_index.shape[0]
    own_frames = frames // 4
    whole = lax.axis_size("frames") * extent
    units = dilated_dirs.shape[0]
    span = (own + 2 * HALO) // SEG
    span_frames = span // STRIDE
    extra = HALO // STRIDE
    me = lax.axis_index("chan")
    block = lax.axis_index("frames")
    ring = lax.axis_size("frames")
    origin = block * extent + me * own
    over_chan, over_frames = bits_of("chan"), bits_of("frames")

    halves = halve(dilated_dirs, pointwise_dirs)
    far = [swap(halves[0], "chan", 1)]
    close = [swap(after(dilated_dirs, halves[0]), "chan", 0), swap(after(pointwise_dirs, halves[0]), "chan", 0)]

    project = jnp.concatenate(
        [output_proj] + [term[:, None] for term in terms(output_bias, 3)] + [jnp.zeros((output_bias.shape[0], 117), BF)],
        axis=1,
    )
    packed, pulled = vectors(
        after(dilated_dirs, halves[0]), pointwise_dirs, dilated_gains, pointwise_gains, dilated_bias, pointwise_bias,
        snake_first, snake_second, snake_last, project, cotangent,
    )

    pieces, ends = cut(signal, packed, pulled, code_index.reshape(-1, 128))
    pieces = [pieces[0]] + [to_peer(pieces[peer], peer) for peer in (1, 2, 3)]
    ends = [
        lax.ppermute(
            ends[peer],
            ("frames", "chan"),
            [(4 * (f + 1) + (3 ^ peer), 4 * f + 3) for f in range(ring - 1)]
            + [(4 * f + peer, 4 * (f + 1)) for f in range(ring - 1)],
        )
        for peer in range(4)
    ]
    rest = [swap(far[0], "frames", 0)]
    far_close = [swap(far[0], "chan", 0)]
    rest_close = [swap(rest[0], "chan", 0)]
    far.append(swap(after(halves[1], *pieces), "chan", 1))
    far.append(swap(after(halves[2], *pieces), "chan", 1))

    bounds = jnp.cumsum(utterances) * STRIDE
    b_place = jnp.arange(-LEAD, span + LEAD, dtype=jnp.int32)
    spots = (origin - HALO + b_place[:, None] + span * jnp.arange(SEG, dtype=jnp.int32)[None, :]).reshape(-1)
    found = jnp.sum((spots[:, None] >= bounds[None, :]).astype(F32), axis=1)
    found = jnp.where((spots >= 0) & (spots < whole), found, -1.0)
    labels = jnp.broadcast_to(found[:, None], (found.shape[0], 128))

    place = (
        jnp.arange(SEG, dtype=jnp.int32)[None, :] * span_frames + jnp.arange(span_frames, dtype=jnp.int32)[:, None]
    ).reshape(-1)
    owned = (place >= extra) & (place < extra + own_frames)
    place = jnp.where(owned, place - extra + block * frames + me * own_frames, -1)
    place = jnp.broadcast_to(place[:, None], (place.shape[0], 128))
    refill = refill_index.reshape(-1, 512)
    labels, place, refill, project_in, _ = lax.optimization_barrier((labels, place, refill, latent_proj, halves[0]))
    merged, norms = merge_strided(strided_dirs, strided_gains, strided_bias, project_in)
    *held, _, _ = lax.optimization_barrier((*pieces, *ends, far[0], merged))
    stream, vecs, pulled, edge_codes = enter(held[:4], held[4:], packed.shape[0], own)

    def unit(member, stream, *far_pieces):
        pieces = (dilated_dirs, pointwise_dirs, *close, *far_pieces)
        result, middle, wide, weight1 = unit_forward(stream, pieces, member, vecs, labels)
        saved.append((stream, middle, wide, weight1, pieces))
        return result

    saved = []
    stream = unit(0, stream, far[0], rest[0], far_close[0], rest_close[0])
    rest.append(swap(after(far[1], stream), "frames", 0))
    far_close.append(swap(after(far[1], stream), "chan", 0))
    got = swap(after(merged, stream), "chan", 0)

    edge_codes = edge_codes.astype(jnp.int32)
    around = jnp.concatenate([edge_codes[1, 128 - extra :], code_index, edge_codes[0, :extra]])
    near = lax.dynamic_slice_in_dim(around, me * own_frames, own_frames + 2 * extra)
    near = near.reshape(SEG, span_frames).T.reshape(-1)
    wanted = jnp.broadcast_to(jnp.concatenate([near, code_index])[:, None], (near.shape[0] + frames, 128))
    near_rows = wanted[: near.shape[0]]
    pulled = jnp.pad(pulled, ((0, 120), (extra, extra)))
    pulled = pulled.reshape(128, SEG, span_frames).transpose(2, 1, 0).reshape(-1, 128)
    latent_bias = jnp.pad(latent_bias, (0, 128 - latent_bias.shape[0]))[None]
    wanted, near_rows, pulled, latent_bias, _ = lax.optimization_barrier((wanted, near_rows, pulled, latent_bias, stream))
    chosen, output, sums_out = look_up(wanted, codebook, project, cotangent, near.shape[0])
    merged = merged + after(got, chosen)
    got = swap(merged, "chan", 1)
    rest_close.append(swap(after(rest[1], merged), "chan", 0))
    rest.append(swap(after(halves[3], far[2], merged), "chan", 1))
    far_close.append(swap(after(far[2], merged), "chan", 0))
    stream = unit(1, after(stream, chosen), far[1], rest[1], far_close[1], rest_close[1])
    rest_close.append(swap(after(rest[2], stream), "chan", 0))
    stream = unit(2, stream, far[2], rest[2], far_close[2], rest_close[2])
    merged = (merged, after(got, stream))
    grad, latent, dchosen, mixed_grad, last_sums = bottleneck(
        stream, merged, latent_bias, vecs, labels, chosen, pulled, own
    )

    bit0, bit1 = over_chan

    rows = grad.shape[0]

    def weights_of(member, grad=None):
        _, middle, wide, weight1, _ = saved[member]
        return (member, grad, middle, wide, weight1)

    def into_of(member, grad, scaled):
        return (member, grad, saved[member][0], scaled, saved[member][4])

    back2 = units_back(vecs, labels, own, rows, chans, weights=weights_of(2, grad))
    keep2 = back2["keep"]
    near2 = swap(back2["send"], "chan", 0)
    chain_rows = -(-(8 * part + 128) // (16 * ring)) * 16 * ring
    codes = code_payload(dchosen, latent, mixed_grad, near_rows, place, refill, back2["sums_a"])
    codes = [codes[0]] + [to_peer(codes[peer], peer) for peer in (1, 2, 3)]
    near2 = after(near2, codes[0])
    far2 = add_up(keep2[1], near2[1])
    x2 = swap(far2, "chan", 1)
    back1 = units_back(
        vecs, labels, own, rows, chans, into_of(2, after(grad, far2), back2["scaled_out"]), weights_of(1)
    )
    keep1 = back1["keep"]
    near1 = swap(back1["send"], "chan", 0)
    x2, *codes, _ = lax.optimization_barrier((x2, *codes, back1["sums_a"]))
    chain2 = Chain(
        [[(keep2, 0), (near2, 0), (x2, None)], [(piece, None) for piece in codes]], chain_rows, over_frames, 20
    )
    far1 = add_up(keep1[1], after(near1, chain2.sent)[1])
    x1 = swap(far1, "chan", 1)
    back0 = units_back(
        vecs, labels, own, rows, chans,
        into_of(1, after(back1["out"], far1), back1["scaled_out"]), weights_of(0),
    )
    keep0 = back0["keep"]
    near0 = swap(back0["send"], "chan", 0)
    token = chain2.step(back0["sums_a"])
    more = sums_out[:, :16].astype(BF).reshape(-1, chans)
    more = jnp.pad(more, ((0, 16 - more.shape[0]), (0, 0)))
    chain1 = Chain([[(keep1, 0), (near1, 0), (after(x1, token), None)], [(more, None)]], chain_rows, over_frames)
    last = units_back(
        vecs, labels, own, rows, chans, into_of(0, after(back0["out"], chain1.sent), back0["scaled_out"]),
        others=(
            (back0["sums_a"], 3), (back0["sums_c"], 1), (back1["sums_a"], 3), (back1["sums_c"], 1),
            (back2["sums_a"], 3), (last_sums, 2),
        ),
    )
    grad, small = last["out"], last["sums_c"]

    token = chain2.step(grad)
    token = chain1.step(token)
    far0 = add_up(keep0[1], after(near0, token)[1])
    x0 = swap(far0, "chan", 1)
    small_steps = [bit0] + over_frames + [bit1]
    small_got = swap(small, *small_steps[0])
    outs = leave(after(grad, far0), own)
    sent_outs = [outs[0]] + [to_peer(outs[peer], peer) for peer in (1, 2, 3)]
    token = outs[0]

    def small_step():
        nonlocal small, small_got, token
        small = small + after(small_got, token)
        small_steps.pop(0)
        if small_steps:
            small_got = swap(small, *small_steps[0])
        token = small

    half = len(over_frames)
    while chain2.adds:
        token = chain2.step(token)
    small_step()
    token = chain1.step(token)
    small_step()
    token = chain2.step(token)
    chain0 = Chain([[(keep0, 0), (near0, 0), (after(x0, token), None)]], 8 * part, over_frames)
    token = chain0.sent
    while chain1.left > half:
        token = chain1.step(token)
    token = chain0.step(token)
    while chain2.left > 1:
        token = chain2.step(token)
    while len(small_steps) > 2:
        small_step()
    while chain0.left > half + 1:
        token = chain0.step(token)
    token = chain2.step(token)
    quarter = codes[0].shape[0]
    first = 8 * part - chain_rows // 2
    codes_mine = chain2.upper()[first : first + quarter]
    got_codes = [codes_mine] + [to_peer(codes_mine, peer) for peer in (1, 2, 3)]
    token = chain1.step(token)
    small_step()
    token = chain0.step(token)
    payload = jnp.zeros((4 * quarter, chans), BF)
    for peer in range(4):
        got = after(got_codes[peer], token)
        payload = lax.dynamic_update_slice_in_dim(payload, got, (me ^ peer) * quarter, 0)
    blocks = codebook.shape[1] // 512
    mixed_total = payload[24 * blocks :].reshape(-1, 8, chans)
    meeting, factors = strided_meet(strided_dirs, mixed_total, latent_proj, norms)
    token = chain0.step(meeting)
    while chain1.left > 1:
        token = chain1.step(token)
    small_step()
    gains = jnp.stack([dilated_gains, pointwise_gains], axis=1)
    results = norm_back([chain2], after(dilated_dirs, token), pointwise_dirs, gains, (2,), ())
    gains2 = results[2:]
    grad_signal = settle(list(lax.optimization_barrier((*sent_outs, results[0]))[:4]))
    token = grad_signal
    while chain0.left > 1:
        token = chain0.step(token)
    payload = after(payload, token)
    codes = codebook.shape[1]
    blocks = codes // 512
    by_code = payload[: 24 * blocks].reshape(blocks, 24, 512).transpose(1, 0, 2).reshape(24, codes).astype(F32)
    dcoded, picked, usage = by_code[0:8], by_code[8:16], by_code[16]
    refreshed = jnp.where(usage[None, :] > 0, codebook, picked)
    coded_scale = lax.rsqrt(jnp.sum(codebook * codebook, axis=0) + 1.0)
    coded = codebook * coded_scale[None, :]
    dcodebook = (dcoded - coded * jnp.sum(coded * dcoded, axis=0)[None, :]) * coded_scale[None, :]

    factors = lax.optimization_barrier((factors, token, refreshed, dcodebook))[0]
    dstrided_dirs = strided_back(strided_dirs, mixed_total, latent_proj, norms, factors)
    token = chain1.step(dstrided_dirs)
    results = norm_back([chain1], after(dilated_dirs, token), pointwise_dirs, gains, (1,), results[:2])
    token = results[0]
    chain0.step(token)
    results = norm_back([chain0], dilated_dirs, pointwise_dirs, gains, (0,), (*results[:2], *gains2, *results[2:]))
    sums_out = chain1.upper()[first : first + output_bias.shape[0] * 16 // chans].astype(F32).reshape(-1, 16)
    mine_small = lax.dynamic_slice_in_dim(small, me * part, part, axis=1)
    dbias_latent = small[4 * units + 1, :8]
    dalpha1, dbias1, dbias7, dalpha2 = (mine_small[n : 4 * units : 4] for n in range(4))
    dalpha_last = mine_small[4 * units]
    dproj_latent = meeting[0:8] + dbias_latent[:, None] * strided_bias[None, :]
    dbias_strided = jnp.sum(latent_proj.astype(F32) * dbias_latent[:, None], axis=0)
    return (
        output,
        grad_signal,
        results[0],
        results[2],
        dbias7,
        dalpha1,
        dalpha2,
        results[1],
        results[3],
        dbias1,
        dalpha_last,
        dstrided_dirs,
        meeting[8],
        dbias_strided,
        dproj_latent,
        dbias_latent,
        dcodebook,
        sums_out[:, :8],
        sums_out[:, 8],
        refreshed,
    )


def solution(mesh):
    in_specs = (
        P("chan", "frames"),
        P(None, None, "chan", None),
        P(None, "chan"),
        P(None, "chan"),
        P(None, "chan"),
        P(None, "chan"),
        P(None, "chan", None),
        P(None, "chan"),
        P(None, "chan"),
        P("chan"),
        P(None, "chan", None),
        P("chan"),
        P("chan"),
        P(None, "chan"),
        P(),
        P(),
        P("chan", None),
        P("chan"),
        P(),
        P("frames"),
        P(),
        P("chan", "frames"),
    )
    out_specs = (
        P("chan", "frames"),
        P("chan", "frames"),
        P(None, None, "chan", None),
        P(None, "chan"),
        P(None, "chan"),
        P(None, "chan"),
        P(None, "chan"),
        P(None, "chan", None),
        P(None, "chan"),
        P(None, "chan"),
        P("chan"),
        P(None, "chan", None),
        P("chan"),
        P("chan"),
        P(None, "chan"),
        P(),
        P(),
        P("chan", None),
        P("chan"),
        P(),
    )
    return jax.shard_map(local, mesh=mesh, in_specs=in_specs, out_specs=out_specs, check_vma=False)
```
